128 devices in a mesh: dp: 16 (over z, x_hi, core), seq: 8 (over x_lo, y).
Axes of the slice: x: 4 (x_hi: 2, x_lo: 2; x = x_hi * 2 + x_lo), y: 4, z: 4, core: 2. Of those that a mesh axis runs over, the one named last changes fastest.
Arguments:
- tokens: bfloat16 [32768, 1152], P(('dp', 'seq')), may hold values from -6 to 6
- cotangent: bfloat16 [32768, 1152], P(('dp', 'seq')), may hold values from -6 to 6
- lengths: int32 [16], P('dp'), may hold values from 1793 to 2048, as said below
- query_weight: bfloat16 [1152, 1024], P('dp'), may hold values from -0.1875 to 0.1875
- key_weight: bfloat16 [1152, 256], P('dp'), may hold values from -0.1875 to 0.1875
- value_weight: bfloat16 [1152, 256], P('dp'), may hold values from -0.1875 to 0.1875
- out_weight: bfloat16 [1152, 1024], P('dp'), may hold values from -0.1875 to 0.1875
- gate_weight: bfloat16 [1152, 6912], P('dp'), may hold values from -0.1875 to 0.1875
- up_weight: bfloat16 [1152, 6912], P('dp'), may hold values from -0.1875 to 0.1875
- down_weight: bfloat16 [1152, 6912], P('dp'), may hold values from -0.078125 to 0.078125
- input_gain: bfloat16 [1152], P('dp'), may hold values from -0.5 to 0.5
- query_gain: bfloat16 [256], P('dp'), may hold values from -0.5 to 0.5
- key_gain: bfloat16 [256], P('dp'), may hold values from -0.5 to 0.5
- attention_gain: bfloat16 [1152], P('dp'), may hold values from -0.5 to 0.5
- feedforward_gain: bfloat16 [1152], P('dp'), may hold values from -0.5 to 0.5
- output_gain: bfloat16 [1152], P('dp'), may hold values from -0.5 to 0.5
Outputs:
- layer_output: bfloat16 [32768, 1152], P(('dp', 'seq'))
- tokens_grad: bfloat16 [32768, 1152], P(('dp', 'seq'))
- query_weight_grad: float32 [1152, 1024], P('dp')
- key_weight_grad: float32 [1152, 256], P('dp')
- value_weight_grad: float32 [1152, 256], P('dp')
- out_weight_grad: float32 [1152, 1024], P('dp')
- gate_weight_grad: float32 [1152, 6912], P('dp')
- up_weight_grad: float32 [1152, 6912], P('dp')
- down_weight_grad: float32 [1152, 6912], P('dp')
- input_gain_grad: float32 [1152], P('dp')
- query_gain_grad: float32 [256], P('dp')
- key_gain_grad: float32 [256], P('dp')
- attention_gain_grad: float32 [1152], P('dp')
- feedforward_gain_grad: float32 [1152], P('dp')
- output_gain_grad: float32 [1152], P('dp')
The draws below stay inside these ranges and needn't reach their ends.
Inputs may be any that keep to these rules, and one draw needn't show every extreme that they name: lengths[g] counts the true tokens of sequence g, which fill the first rows of its 2048; the rest are padding. In every draw some sequence is full.
All inputs are finite; a program needn't handle non-finite values.
Results may differ from the reference program's by a relative error of at most 0.033.
Values may be sent and summed in bfloat16 or wider, within the bound.
No kernel may reach another device: no remote copies, remote signals or barrier semaphores. Data moves between devices by JAX's collectives and lax.ppermute only.
A program may use at most 256 MiB of HBM per device.

```python
import math
import jax
import jax.numpy as jnp
from jax import lax

D = 1152
FF = 6912
HEADS = 4
HEAD_DIM = 256
WINDOW = 512
TOK_DEV = 256
GROUP = 2048
TOKENS = 32768
N_DP = 16


def draw_lengths(key, part):
    key = jax.random.fold_in(key, 11)
    first_key, second_key = jax.random.split(key)
    drawn = jax.random.randint(first_key, (N_DP,), GROUP - TOK_DEV + 1, GROUP + 1, dtype=jnp.int32)
    full_group = jax.random.randint(second_key, (), 0, N_DP, dtype=jnp.int32)
    return jnp.where(jnp.arange(N_DP, dtype=jnp.int32) == full_group, GROUP, drawn).astype(jnp.int32)


def shard_levels(rng, shape, cuts, smallest, top_value):
    loudness, own = 1.0, jax.random.fold_in(rng, 6)
    for position, blocks in cuts:
        steps = jnp.exp(jax.random.uniform(jax.random.fold_in(own, position), (blocks,), jnp.float32, smallest / len(cuts), top_value / len(cuts)))
        loudness = loudness * jnp.repeat(steps, shape[position] // blocks).reshape([-1 if axis == position else 1 for axis in range(len(shape))])
    return loudness


def normal_values(key, dims, deviation, reach, cuts=(), kind=jnp.bfloat16):
    entries = jax.random.normal(key, dims, jnp.float32) * deviation
    if len(cuts) > 0:
        entries = shard_levels(key, dims, cuts, -0.22, 0.18) * entries
    return jnp.clip(entries, min=-reach, max=reach).astype(kind)


def setup_inputs(seed: int = 0) -> dict:
    streams_of = jax.random.split(jax.random.key(seed), 17)
    return {
        "tokens": normal_values(streams_of[0], (TOKENS, D), 1.0, 6.0, ((0, 128),)),
        "cotangent": normal_values(streams_of[1], (TOKENS, D), 1.0, 6.0, ((0, 128),)),
        "lengths": draw_lengths(jax.random.fold_in(streams_of[16], 71), 0),
        "query_weight": normal_values(streams_of[3], (D, HEADS * HEAD_DIM), D ** -0.5, 0.1875, ((0, 16),)),
        "key_weight": normal_values(streams_of[4], (D, HEAD_DIM), D ** -0.5, 0.1875, ((0, 16),)),
        "value_weight": normal_values(streams_of[5], (D, HEAD_DIM), D ** -0.5, 0.1875, ((0, 16),)),
        "out_weight": normal_values(streams_of[6], (D, HEADS * HEAD_DIM), (HEADS * HEAD_DIM) ** -0.5, 0.1875, ((0, 16),)),
        "gate_weight": normal_values(streams_of[7], (D, FF), D ** -0.5, 0.1875, ((0, 16),)),
        "up_weight": normal_values(streams_of[8], (D, FF), D ** -0.5, 0.1875, ((0, 16),)),
        "down_weight": normal_values(streams_of[9], (D, FF), FF ** -0.5, 0.078125, ((0, 16),)),
        "input_gain": jnp.clip(jax.random.uniform(streams_of[10], (D,), jnp.float32, -0.5, 0.5) * shard_levels(streams_of[10], (D,), ((0, 16),), -0.4, 0.0), -0.5, 0.5).astype(jnp.bfloat16),
        "query_gain": jnp.clip(jax.random.uniform(streams_of[11], (HEAD_DIM,), jnp.float32, -0.5, 0.5) * shard_levels(streams_of[11], (HEAD_DIM,), ((0, 16),), -0.4, 0.0), -0.5, 0.5).astype(jnp.bfloat16),
        "key_gain": jnp.clip(jax.random.uniform(streams_of[12], (HEAD_DIM,), jnp.float32, -0.5, 0.5) * shard_levels(streams_of[12], (HEAD_DIM,), ((0, 16),), -0.4, 0.0), -0.5, 0.5).astype(jnp.bfloat16),
        "attention_gain": jnp.clip(jax.random.uniform(streams_of[13], (D,), jnp.float32, -0.5, 0.5) * shard_levels(streams_of[13], (D,), ((0, 16),), -0.4, 0.0), -0.5, 0.5).astype(jnp.bfloat16),
        "feedforward_gain": jnp.clip(jax.random.uniform(streams_of[14], (D,), jnp.float32, -0.5, 0.5) * shard_levels(streams_of[14], (D,), ((0, 16),), -0.4, 0.0), -0.5, 0.5).astype(jnp.bfloat16),
        "output_gain": jnp.clip(jax.random.uniform(streams_of[15], (D,), jnp.float32, -0.5, 0.5) * shard_levels(streams_of[15], (D,), ((0, 16),), -0.4, 0.0), -0.5, 0.5).astype(jnp.bfloat16),
    }


EPSILON = 1e-06
GELU_COEFF = 0.044715

@jax.custom_vjp
def low(v):
    return lax.optimization_barrier(v.astype(jnp.bfloat16)).astype(jnp.float32)

@jax.custom_vjp
def low_back(v):
    return v

def low_keep(v):
    return (low(v), None)

def low_pass(kept, grad):
    return (grad,)

def back_keep(v):
    return (v, None)

def back_low(kept, grad):
    return (low(grad),)
low.defvjp(low_keep, low_pass)
low_back.defvjp(back_keep, back_low)

def normalize(values):
    return values * lax.rsqrt(lax.optimization_barrier(jnp.mean(values * values, axis=-1, keepdims=True)) + EPSILON)

def rotary_tables(positions, head_size):
    half_size = head_size // 2
    exponents = lax.iota(jnp.float32, half_size) * (2.0 / head_size)
    frequency = jnp.power(10000.0, -exponents)
    angles = positions.astype(jnp.float32)[:, None] * frequency[None, :]
    return (jnp.cos(angles), jnp.sin(angles))

def rotate(values, cosine_table, sine_table):
    half_size = values.shape[-1] // 2
    first_half = values[..., :half_size]
    second_half = values[..., half_size:]
    return jnp.concatenate([first_half * cosine_table - second_half * sine_table, second_half * cosine_table + first_half * sine_table], axis=-1)

def gelu_tanh(values):
    root_coeff = math.sqrt(2.0 / math.pi)
    return 0.5 * values * (1.0 + jnp.tanh(root_coeff * (values + GELU_COEFF * values * values * values)))

def matmul(left, right):
    return jnp.dot(left, right, preferred_element_type=jnp.float32, precision=lax.Precision.HIGHEST)

def forward_group(values, params, length_value):
    query_weight, key_weight, value_weight, out_weight, gate_weight, up_weight, down_weight, input_gain, query_gain, key_gain, attention_gain, feedforward_gain, output_gain = params
    group_rows = values.shape[0]
    head_size = key_weight.shape[1]
    head_count = query_weight.shape[1] // head_size
    positions = lax.iota(jnp.int32, group_rows)
    cosine_table, sine_table = rotary_tables(positions, head_size)
    attention_input = low(normalize(values) * (1.0 + input_gain))
    query_raw = low_back(matmul(attention_input, query_weight))
    key_raw = low_back(matmul(attention_input, key_weight))
    value_raw = low_back(matmul(attention_input, value_weight))
    query_heads = normalize(query_raw.reshape(group_rows, head_count, head_size)) * (1.0 + query_gain)
    query_low = low(rotate(query_heads, cosine_table[:, None, :], sine_table[:, None, :]))
    key_low = low(rotate(normalize(key_raw) * (1.0 + key_gain), cosine_table, sine_table))
    value_low = low(value_raw)
    block_rows = math.gcd(group_rows, 512)
    key_padded = jnp.pad(key_low, ((WINDOW, 0), (0, 0)))
    value_padded = jnp.pad(value_low, ((WINDOW, 0), (0, 0)))
    scaling_factor = head_size ** (-0.5)

    def attend(first_row):
        query_block = lax.dynamic_slice_in_dim(query_low, first_row, block_rows, 0)
        key_block = lax.dynamic_slice_in_dim(key_padded, first_row, block_rows + WINDOW, 0)
        value_block = lax.dynamic_slice_in_dim(value_padded, first_row, block_rows + WINDOW, 0)
        query_pos = first_row + lax.iota(jnp.int32, block_rows)
        key_pos = first_row - WINDOW + lax.iota(jnp.int32, block_rows + WINDOW)
        offsets = query_pos[:, None] - key_pos[None, :]
        allowed = (offsets >= 0) & (offsets < WINDOW) & (key_pos[None, :] >= 0)
        scores = low_back(jnp.einsum('thd,kd->htk', query_block, key_block, precision=lax.Precision.HIGHEST) * scaling_factor)
        masked = jnp.where(allowed[None], scores, -1e+30)
        row_top = lax.optimization_barrier(jnp.max(masked, axis=-1, keepdims=True))
        exponent_terms = jnp.exp(masked - row_top)
        probs = exponent_terms / lax.optimization_barrier(jnp.sum(exponent_terms, axis=-1, keepdims=True))
        probs_low = low(probs)
        return low(low_back(jnp.einsum('htk,kd->thd', probs_low, value_block, precision=lax.Precision.HIGHEST)))
    starts = lax.iota(jnp.int32, group_rows // block_rows) * block_rows
    context = lax.map(jax.checkpoint(attend), starts).reshape(group_rows, head_count * head_size)
    attention_raw = low_back(matmul(context, out_weight.T))
    hidden_state = values + normalize(attention_raw) * (1.0 + attention_gain)
    feed_input = low(normalize(hidden_state) * (1.0 + feedforward_gain))
    gate_raw = low_back(matmul(feed_input, gate_weight))
    up_raw = low_back(matmul(feed_input, up_weight))
    hidden = low(gelu_tanh(gate_raw) * up_raw)
    down_raw = low_back(matmul(hidden, down_weight.T))
    layer_value = hidden_state + normalize(down_raw) * (1.0 + output_gain)
    valid_rows = (positions < length_value).astype(values.dtype)[:, None]
    return layer_value * valid_rows

def reference(tokens, cotangent, lengths, query_weight, key_weight, value_weight, out_weight, gate_weight, up_weight, down_weight, input_gain, query_gain, key_gain, attention_gain, feedforward_gain, output_gain):
    params = tuple((array_item.astype(jnp.float32) for array_item in (query_weight, key_weight, value_weight, out_weight, gate_weight, up_weight, down_weight, input_gain, query_gain, key_gain, attention_gain, feedforward_gain, output_gain)))
    inputs = tokens.astype(jnp.float32).reshape(N_DP, GROUP, D)
    upstream = cotangent.astype(jnp.float32).reshape(N_DP, GROUP, D)

    def one_group(totals, group_item):
        values, seed_grad, length_value = group_item
        outputs, pullback = jax.vjp(lambda first_arg, second_arg: forward_group(first_arg, second_arg, length_value), values, params)
        values_grad, params_grad = pullback(seed_grad)
        return (tuple((left_item + right_item for left_item, right_item in zip(totals, params_grad))), (outputs, values_grad))
    zero_grads = tuple((jnp.zeros_like(array_item) for array_item in params))
    totals, (outputs, values_grads) = lax.scan(one_group, zero_grads, (inputs, upstream, lengths))
    layer_output = outputs.reshape(TOKENS, D).astype(jnp.bfloat16)
    tokens_grad = values_grads.reshape(TOKENS, D).astype(jnp.bfloat16)
    return (layer_output, tokens_grad, totals[0], totals[1], totals[2], totals[3], totals[4], totals[5], totals[6], totals[7], totals[8], totals[9], totals[10], totals[11], totals[12])
```

```python
import math

import jax
import jax.numpy as jnp
from jax import lax
from jax.sharding import Mesh
from jax.sharding import PartitionSpec as P

WINDOW = 512


EPSILON = 1e-06
GELU_COEFF = 0.044715


AXES = ("z", "xh", "core", "xl", "y")
SIZES = (4, 2, 2, 2, 4)
DP = ("z", "xh", "core")
SEQ = ("xl", "y")
FEED_SLICE = 1792


def from_behind(array, by):
    pairs = [(i, i + by) for i in range(8) if 0 <= i + by < 8]
    return lax.ppermute(array, SEQ, pairs)


def take(array, axis, by):
    count = lax.axis_size(axis)
    return lax.ppermute(array, axis, [((i + by) % count, i) for i in range(count)])


def give(array, axis, by):
    count = lax.axis_size(axis)
    return lax.ppermute(array, axis, [(i, (i + by) % count) for i in range(count)])


def swap_x(array):
    return lax.ppermute(array, ("xh", "xl"), [(0, 3), (3, 0), (1, 2), (2, 1)])


def gather_rows(block):
    rows, width = block.shape
    z = lax.axis_index("z")
    xh = lax.axis_index("xh")
    core = lax.axis_index("core")
    beside = swap_x(block)
    pair = jnp.where(xh == 0, jnp.stack([block, beside]), jnp.stack([beside, block]))
    own = jnp.zeros((4, 2, rows, width), block.dtype)
    own = lax.dynamic_update_slice_in_dim(own, pair[None], z, 0)
    for by in (1, 3, 2):
        own = lax.dynamic_update_slice_in_dim(own, take(pair, "z", by)[None], (z + by) % 4, 0)
    other = give(own, "core", 1)
    both = jnp.where(
        core == 0, jnp.stack([own, other], axis=2), jnp.stack([other, own], axis=2)
    )
    return both.reshape(16 * rows, width)


def gather_ring(block):
    return [block, take(block, "y", 1), take(block, "y", 2), take(block, "y", 3)]


def sum_ring(blocks):
    total = blocks[0].astype(jnp.float32)
    for by in (1, 3, 2):
        total = total + give(blocks[by].astype(jnp.bfloat16), "y", by).astype(jnp.float32)
    return total


def pick(array, index, axis):
    return lax.dynamic_index_in_dim(array, index, axis, keepdims=False)


def reduce_rows(part):
    z = lax.axis_index("z")
    xh = lax.axis_index("xh")
    core = lax.axis_index("core")
    width = part.shape[1]
    rows = part.shape[0] // 16
    by_core = part.reshape(8, 2, rows, width)
    got = give(pick(by_core, 1 - core, 1), "core", 1)
    chip = (pick(by_core, core, 1).astype(jnp.float32) + got.astype(jnp.float32)).astype(
        jnp.bfloat16
    )
    by_z = chip.reshape(4, 2, rows, width)
    total = pick(by_z, z, 0).astype(jnp.float32)
    for by in (1, 3, 2):
        total = total + give(pick(by_z, (z + by) % 4, 0), "z", by).astype(jnp.float32)
    column = total.astype(jnp.bfloat16)
    got = swap_x(pick(column, 1 - xh, 0))
    half = (pick(column, xh, 0).astype(jnp.float32) + got.astype(jnp.float32)).astype(jnp.bfloat16)
    got = give(half, "xl", 1)
    return (half.astype(jnp.float32) + got.astype(jnp.float32)).astype(jnp.bfloat16)


def in_order(blocks):
    y = lax.axis_index("y")
    ordered = []
    for place in range(4):
        value = blocks[(place - 3) % 4]
        for at in range(3):
            value = jnp.where(y == at, blocks[(place - at) % 4], value)
        ordered.append(value.astype(jnp.float32))
    return ordered


def inverse_rms(values):
    return lax.rsqrt(jnp.mean(values * values, axis=-1, keepdims=True) + EPSILON)


def rms_backward(values, scaling, upstream):
    inner = jnp.mean(upstream * values, axis=-1, keepdims=True)
    return scaling * (upstream - values * (scaling * scaling) * inner)


def rotary_tables(positions, head_size):
    half_size = head_size // 2
    exponents = lax.iota(jnp.float32, half_size) * (2.0 / head_size)
    frequency = jnp.power(10000.0, -exponents)
    angles = positions.astype(jnp.float32)[:, None] * frequency[None, :]
    return (jnp.cos(angles), jnp.sin(angles))


def rotate(values, cosine_table, sine_table):
    half_size = values.shape[-1] // 2
    first_half = values[..., :half_size]
    second_half = values[..., half_size:]
    return jnp.concatenate(
        [
            first_half * cosine_table - second_half * sine_table,
            second_half * cosine_table + first_half * sine_table,
        ],
        axis=-1,
    )


def rotate_back(upstream, cosine_table, sine_table):
    half_size = upstream.shape[-1] // 2
    first_half = upstream[..., :half_size]
    second_half = upstream[..., half_size:]
    return jnp.concatenate(
        [
            first_half * cosine_table + second_half * sine_table,
            second_half * cosine_table - first_half * sine_table,
        ],
        axis=-1,
    )


def gelu_parts(values):
    root_coeff = math.sqrt(2.0 / math.pi)
    bend = jnp.tanh(root_coeff * (values + GELU_COEFF * values * values * values))
    gelu_value = 0.5 * values * (1.0 + bend)
    gelu_slope = 0.5 * (1.0 + bend) + 0.5 * values * (1.0 - bend * bend) * root_coeff * (
        1.0 + 3.0 * GELU_COEFF * values * values
    )
    return (gelu_value, gelu_slope)


def feed_slice(weight):
    y = lax.axis_index("y")
    padded = jnp.pad(weight, ((0, 0), (0, 4 * FEED_SLICE - weight.shape[1])))
    return lax.dynamic_slice_in_dim(padded, y * FEED_SLICE, FEED_SLICE, 1)


def local(
    tokens,
    cotangent,
    lengths,
    query_weight,
    key_weight,
    value_weight,
    out_weight,
    gate_weight,
    up_weight,
    down_weight,
    input_gain,
    query_gain,
    key_gain,
    attention_gain,
    feedforward_gain,
    output_gain,
):
    low = jnp.bfloat16
    row_count, model_width = tokens.shape
    head_size = key_weight.shape[1]
    head_count = query_weight.shape[1] // head_size
    query_width = head_count * head_size
    feed_width = gate_weight.shape[1]
    gain_shard = input_gain.shape[0]
    head_shard = query_gain.shape[0]
    scaling_factor = head_size ** (-0.5)
    y = lax.axis_index("y")
    seq_index = lax.axis_index("xl") * 4 + y
    positions = seq_index * row_count + lax.iota(jnp.int32, row_count)
    valid_rows = (positions < lengths[0]).astype(jnp.float32)[:, None]
    cosine_table, sine_table = rotary_tables(positions, head_size)
    hop_total = 2

    def spread(vector):
        return jnp.pad(vector, (0, gain_shard - head_shard))

    gain_columns = jnp.stack(
        [
            input_gain,
            attention_gain,
            feedforward_gain,
            output_gain,
            spread(query_gain),
            spread(key_gain),
        ],
        axis=1,
    )
    gain_columns = jnp.pad(gain_columns, ((0, 0), (0, 122)))
    first = gather_rows(
        jnp.concatenate([query_weight, key_weight, value_weight, gain_columns], axis=1)
    )
    full_qkv = first[:, : query_width + 2 * head_size]
    gains = 1.0 + first[:, query_width + 2 * head_size :].astype(jnp.float32)
    full_out = gather_rows(out_weight)
    gate_up = lax.all_gather(
        jnp.concatenate([feed_slice(gate_weight), feed_slice(up_weight)], axis=1),
        DP,
        axis=0,
        tiled=True,
    )
    down = lax.all_gather(feed_slice(down_weight), DP, axis=0, tiled=True)
    gain_rows = gains.T
    one_input = gain_rows[0]
    one_attention = gain_rows[1]
    one_feed = gain_rows[2]
    one_output = gain_rows[3]
    one_query = gain_rows[4].reshape(16, gain_shard)[:, :head_shard].reshape(head_size)
    one_key = gain_rows[5].reshape(16, gain_shard)[:, :head_shard].reshape(head_size)

    residual = tokens.astype(jnp.float32)
    input_scale = inverse_rms(residual)
    normed_input = residual * input_scale
    attention_input = (normed_input * one_input).astype(low)
    input_ring = jnp.concatenate(gather_ring(attention_input), axis=0)
    qkv_raw = jnp.dot(attention_input, full_qkv, preferred_element_type=jnp.float32)
    query_raw = qkv_raw[:, :query_width]
    key_raw = qkv_raw[:, query_width : query_width + head_size]
    value_raw = qkv_raw[:, query_width + head_size :]
    query_heads = query_raw.reshape(row_count, head_count, head_size)
    query_scale = inverse_rms(query_heads)
    query_hat = query_heads * query_scale
    query_low = rotate(
        query_hat * one_query, cosine_table[:, None, :], sine_table[:, None, :]
    ).astype(low)
    key_scale = inverse_rms(key_raw)
    key_hat = key_raw * key_scale
    key_low = rotate(key_hat * one_key, cosine_table, sine_table).astype(low)
    value_low = value_raw.astype(low)
    local_pair = jnp.concatenate([key_low, value_low], axis=1)
    rim_blocks = [from_behind(local_pair, distance) for distance in (1, 2)]
    key_rows = jnp.concatenate(rim_blocks[::-1] + [local_pair], axis=0)
    key_count = key_rows.shape[0]
    key_positions = (seq_index - hop_total) * row_count + lax.iota(jnp.int32, key_count)
    offsets = positions[:, None] - key_positions[None, :]
    allowed = (offsets >= 0) & (offsets < WINDOW) & (key_positions[None, :] >= 0)
    keys_only = key_rows[:, :head_size]
    values_only = key_rows[:, head_size:]

    def masked_scores():
        raw_scores = (
            jnp.einsum("thd,kd->htk", query_low, keys_only, preferred_element_type=jnp.float32)
            * scaling_factor
        )
        return jnp.where(allowed[None], raw_scores, -1e30)

    masked = masked_scores()
    row_top = jnp.max(masked, axis=-1, keepdims=True)
    exponent_terms = jnp.exp(masked - row_top)
    row_total = jnp.sum(exponent_terms, axis=-1, keepdims=True)
    log_total = row_top + jnp.log(row_total)
    probs_low = (exponent_terms / row_total).astype(low)
    context = jnp.einsum("htk,kd->thd", probs_low, values_only, preferred_element_type=jnp.float32)
    context_low = context.reshape(row_count, query_width).astype(low)
    attention_raw = jnp.einsum(
        "tq,dq->td", context_low, full_out, preferred_element_type=jnp.float32
    )
    attention_scale = inverse_rms(attention_raw)
    attention_hat = attention_raw * attention_scale
    hidden_state = residual + attention_hat * one_attention
    state_scale = inverse_rms(hidden_state)
    state_hat = hidden_state * state_scale
    feed_input = (state_hat * one_feed).astype(low)

    feed_ring = jnp.concatenate(gather_ring(feed_input), axis=0)
    gate_up_raw = jnp.dot(feed_ring, gate_up, preferred_element_type=jnp.float32)
    gate_raw = gate_up_raw[:, :FEED_SLICE]
    up_raw = gate_up_raw[:, FEED_SLICE:]
    gelu_value, gelu_slope = gelu_parts(gate_raw)
    hidden_low = (gelu_value * up_raw).astype(low)
    down_part = jnp.einsum("tf,df->td", hidden_low, down, preferred_element_type=jnp.float32)
    down_raw = sum_ring(jnp.split(down_part, 4, axis=0))
    down_scale = inverse_rms(down_raw)
    down_hat = down_raw * down_scale
    layer_value = hidden_state + down_hat * one_output
    layer_output = (valid_rows * layer_value).astype(low)
    upstream = cotangent.astype(jnp.float32) * valid_rows
    output_gain_vec = jnp.sum(upstream * down_hat, axis=0)
    down_grad_low = rms_backward(down_raw, down_scale, upstream * one_output).astype(low)

    down_ring = jnp.concatenate(gather_ring(down_grad_low), axis=0)
    hidden_grad = jnp.dot(down_ring, down, preferred_element_type=jnp.float32)
    down_weight_part = jnp.einsum(
        "tc,tf->cf", down_ring, hidden_low, preferred_element_type=jnp.float32
    ).astype(low)
    gate_grad_low = (hidden_grad * up_raw * gelu_slope).astype(low)
    up_grad_low = (hidden_grad * gelu_value).astype(low)
    gate_up_grad = jnp.concatenate([gate_grad_low, up_grad_low], axis=1)
    feed_part = jnp.einsum("tf,df->td", gate_up_grad, gate_up, preferred_element_type=jnp.float32)
    gate_up_part = jnp.einsum(
        "tc,tf->cf", feed_ring, gate_up_grad, preferred_element_type=jnp.float32
    ).astype(low)
    block_part = sum_ring(jnp.split(feed_part, 4, axis=0))
    down_weight_sum = reduce_rows(down_weight_part)
    gate_up_sum = reduce_rows(gate_up_part)

    feed_gain_vec = jnp.sum(block_part * state_hat, axis=0)
    state_grad = upstream + rms_backward(hidden_state, state_scale, block_part * one_feed)
    attention_gain_vec = jnp.sum(state_grad * attention_hat, axis=0)
    attention_grad_low = rms_backward(
        attention_raw, attention_scale, state_grad * one_attention
    ).astype(low)
    attention_ring = jnp.concatenate(gather_ring(attention_grad_low), axis=0)
    context_cut = context_low.reshape(row_count, 4, query_width // 4)
    context_ring = jnp.concatenate(
        [pick(context_cut, y, 1)]
        + [give(pick(context_cut, (y + by) % 4, 1), "y", by) for by in (3, 2, 1)],
        axis=0,
    )
    context_grad = jnp.einsum(
        "td,dq->tq", attention_grad_low, full_out, preferred_element_type=jnp.float32
    )
    context_grad_low = context_grad.reshape(row_count, head_count, head_size).astype(low)
    probs_again = jnp.exp(masked_scores() - log_total)
    probs_again_low = probs_again.astype(low)
    prob_grad = jnp.einsum(
        "thd,kd->htk", context_grad_low, values_only, preferred_element_type=jnp.float32
    )
    score_grad = probs_again * (
        prob_grad - jnp.sum(probs_again * prob_grad, axis=-1, keepdims=True)
    )
    score_grad_low = score_grad.astype(low)
    key_rot_rows = (
        jnp.einsum("htk,thd->kd", score_grad_low, query_low, preferred_element_type=jnp.float32)
        * scaling_factor
    )
    value_rows = jnp.einsum(
        "htk,thd->kd", probs_again_low, context_grad_low, preferred_element_type=jnp.float32
    )
    pair_grad = jnp.concatenate([key_rot_rows, value_rows], axis=1)
    local_grad = pair_grad[hop_total * row_count :]
    for distance in range(1, hop_total + 1):
        begin_row = (hop_total - distance) * row_count
        local_grad = local_grad + from_behind(
            pair_grad[begin_row : begin_row + row_count].astype(low), -distance
        ).astype(jnp.float32)
    query_rot_grad = (
        jnp.einsum("htk,kd->thd", score_grad_low, keys_only, preferred_element_type=jnp.float32)
        * scaling_factor
    )
    key_norm_grad = rotate_back(local_grad[:, :head_size], cosine_table, sine_table)
    key_gain_vec = jnp.sum(key_norm_grad * key_hat, axis=0)
    key_raw_low = rms_backward(key_raw, key_scale, key_norm_grad * one_key).astype(low)
    value_raw_low = local_grad[:, head_size:].astype(low)
    query_norm_grad = rotate_back(query_rot_grad, cosine_table[:, None, :], sine_table[:, None, :])
    query_gain_vec = jnp.sum(query_norm_grad * query_hat, axis=(0, 1))
    query_raw_low = (
        rms_backward(query_heads, query_scale, query_norm_grad * one_query)
        .reshape(row_count, query_width)
        .astype(low)
    )
    qkv_grad = jnp.concatenate([query_raw_low, key_raw_low, value_raw_low], axis=1)
    qkv_cut = qkv_grad.reshape(row_count, 4, qkv_grad.shape[1] // 4)
    qkv_ring = jnp.concatenate(
        [pick(qkv_cut, y, 1)]
        + [give(pick(qkv_cut, (y + by) % 4, 1), "y", by) for by in (3, 2, 1)],
        axis=0,
    )
    input_grad = jnp.einsum("tq,dq->td", qkv_grad, full_qkv, preferred_element_type=jnp.float32)
    input_gain_vec = jnp.sum(input_grad * normed_input, axis=0)
    tokens_grad = (state_grad + rms_backward(residual, input_scale, input_grad * one_input)).astype(
        low
    )

    def spread_head(vector):
        return jnp.pad(
            vector.reshape(16, head_shard), ((0, 0), (0, gain_shard - head_shard))
        ).reshape(model_width)

    gain_block = jnp.stack(
        [
            input_gain_vec,
            attention_gain_vec,
            feed_gain_vec,
            output_gain_vec,
            spread_head(query_gain_vec),
            spread_head(key_gain_vec),
        ],
        axis=1,
    )
    gain_block = jnp.pad(gain_block, ((0, 0), (0, 122)))
    qkv_part = jnp.einsum("tc,tq->cq", input_ring, qkv_ring, preferred_element_type=jnp.float32)
    out_part = jnp.einsum(
        "tc,tq->cq", attention_ring, context_ring, preferred_element_type=jnp.float32
    )
    attention_sum = reduce_rows(
        jnp.concatenate([qkv_part, out_part, gain_block], axis=1).astype(low)
    )
    down_blocks = in_order(gather_ring(down_weight_sum))
    gate_up_blocks = in_order(gather_ring(gate_up_sum))
    attention_blocks = in_order(gather_ring(attention_sum))
    down_weight_grad = jnp.concatenate(down_blocks, axis=1)[:, :feed_width]
    gate_weight_grad = jnp.concatenate([b[:, :FEED_SLICE] for b in gate_up_blocks], axis=1)
    up_weight_grad = jnp.concatenate([b[:, FEED_SLICE:] for b in gate_up_blocks], axis=1)
    qkv_cols = qkv_grad.shape[1] // 4
    out_cols = query_width // 4
    qkv_weight_grad = jnp.concatenate([b[:, :qkv_cols] for b in attention_blocks], axis=1)
    out_weight_grad = jnp.concatenate(
        [b[:, qkv_cols : qkv_cols + out_cols] for b in attention_blocks], axis=1
    )
    gain_sum = sum(b[:, qkv_cols + out_cols :] for b in attention_blocks)
    return (
        layer_output,
        tokens_grad,
        qkv_weight_grad[:, :query_width],
        qkv_weight_grad[:, query_width : query_width + head_size],
        qkv_weight_grad[:, query_width + head_size :],
        out_weight_grad,
        gate_weight_grad[:, :feed_width],
        up_weight_grad[:, :feed_width],
        down_weight_grad,
        gain_sum[:, 0],
        gain_sum[:head_shard, 4],
        gain_sum[:head_shard, 5],
        gain_sum[:, 1],
        gain_sum[:, 2],
        gain_sum[:, 3],
    )


def solution(mesh):
    fine = Mesh(mesh.devices.reshape(SIZES), AXES)
    rows = P(AXES, None)
    matrix = P(DP, None)
    vector = P(DP)
    return jax.shard_map(
        local,
        mesh=fine,
        in_specs=(rows, rows, vector) + (matrix,) * 7 + (vector,) * 6,
        out_specs=(rows, rows) + (matrix,) * 7 + (vector,) * 6,
        check_vma=False,
    )
```

```python
import math

import jax
import jax.numpy as jnp
from jax import lax
from jax.sharding import Mesh
from jax.sharding import PartitionSpec as P

WINDOW = 512


EPSILON = 1e-06
GELU_COEFF = 0.044715


AXES = ("z", "xh", "core", "xl", "y")
SIZES = (4, 2, 2, 2, 4)
DP = ("z", "xh", "core")
SEQ = ("xl", "y")
FEED_SLICE = 1792


def from_behind(array, by):
    pairs = [(i, i + by) for i in range(8) if 0 <= i + by < 8]
    return lax.ppermute(array, SEQ, pairs)


def take(array, axis, by):
    count = lax.axis_size(axis)
    return lax.ppermute(array, axis, [((i + by) % count, i) for i in range(count)])


def give(array, axis, by):
    count = lax.axis_size(axis)
    return lax.ppermute(array, axis, [(i, (i + by) % count) for i in range(count)])


def swap_x(array):
    return lax.ppermute(array, ("xh", "xl"), [(0, 3), (3, 0), (1, 2), (2, 1)])


def ordered(value, *after):
    return lax.optimization_barrier((value,) + after)[0]


def gather_rows(block, wait=()):
    rows, width = block.shape
    z = lax.axis_index("z")
    xh = lax.axis_index("xh")
    core = lax.axis_index("core")
    beside = swap_x(block)
    pair = jnp.where(xh == 0, jnp.stack([block, beside]), jnp.stack([beside, block]))
    ring = [(take(pair, "z", by), by) for by in (1, 3, 2)]
    arrived = [piece for piece, _ in ring]
    own = jnp.zeros((4, 2, rows, width), block.dtype)
    own = lax.dynamic_update_slice_in_dim(own, pair[None], z, 0)
    if wait:
        own = ordered(own, *wait)
    for piece, by in ring:
        own = lax.dynamic_update_slice_in_dim(own, piece[None], (z + by) % 4, 0)
    other = give(own, "core", 1)
    both = jnp.where(
        core == 0, jnp.stack([own, other], axis=2), jnp.stack([other, own], axis=2)
    )
    return both.reshape(16 * rows, width), arrived


def core_sum(part):
    core = lax.axis_index("core")
    rows, width = part.shape[0] // 16, part.shape[1]
    by_core = part.reshape(8, 2, rows, width)
    got = give(pick(by_core, 1 - core, 1), "core", 1)
    total = pick(by_core, core, 1).astype(jnp.float32) + got.astype(jnp.float32)
    return total.astype(jnp.bfloat16).reshape(4, 2, rows, width)


def z_sum(chip):
    z = lax.axis_index("z")
    total = pick(chip, z, 0).astype(jnp.float32)
    for by in (1, 3, 2):
        total = total + give(pick(chip, (z + by) % 4, 0), "z", by).astype(jnp.float32)
    return total.astype(jnp.bfloat16)


def x_sum(column):
    xh = lax.axis_index("xh")
    got = swap_x(pick(column, 1 - xh, 0))
    half = (pick(column, xh, 0).astype(jnp.float32) + got.astype(jnp.float32)).astype(jnp.bfloat16)
    got = give(half, "xl", 1)
    return (half.astype(jnp.float32) + got.astype(jnp.float32)).astype(jnp.bfloat16)


def gather_ring(block):
    return [block, take(block, "y", 1), take(block, "y", 2), take(block, "y", 3)]


def sum_ring(parts):
    rows = parts[0].shape[0]
    low = jnp.bfloat16
    others = ((parts[1][:rows], 1), (parts[1][rows:], 3), (parts[2], 2))
    total = parts[0].astype(jnp.float32)
    for part, by in others:
        total = total + give(part.astype(low), "y", by).astype(jnp.float32)
    return total


def in_order(blocks):
    y = lax.axis_index("y")
    placed = []
    for place in range(4):
        value = blocks[(place - 3) % 4]
        for at in range(3):
            value = jnp.where(y == at, blocks[(place - at) % 4], value)
        placed.append(value)
    return placed


def pick(array, index, axis):
    return lax.dynamic_index_in_dim(array, index, axis, keepdims=False)


def inverse_rms(values):
    return lax.rsqrt(jnp.mean(values * values, axis=-1, keepdims=True) + EPSILON)


def rms_backward(values, scaling, upstream):
    inner = jnp.mean(upstream * values, axis=-1, keepdims=True)
    return scaling * (upstream - values * (scaling * scaling) * inner)


def rotary_tables(positions, head_size):
    half_size = head_size // 2
    exponents = lax.iota(jnp.float32, half_size) * (2.0 / head_size)
    frequency = jnp.power(10000.0, -exponents)
    angles = positions.astype(jnp.float32)[:, None] * frequency[None, :]
    return (jnp.cos(angles), jnp.sin(angles))


def rotate(values, cosine_table, sine_table):
    half_size = values.shape[-1] // 2
    first_half = values[..., :half_size]
    second_half = values[..., half_size:]
    return jnp.concatenate(
        [
            first_half * cosine_table - second_half * sine_table,
            second_half * cosine_table + first_half * sine_table,
        ],
        axis=-1,
    )


def rotate_back(upstream, cosine_table, sine_table):
    half_size = upstream.shape[-1] // 2
    first_half = upstream[..., :half_size]
    second_half = upstream[..., half_size:]
    return jnp.concatenate(
        [
            first_half * cosine_table + second_half * sine_table,
            second_half * cosine_table - first_half * sine_table,
        ],
        axis=-1,
    )


def gelu_parts(values):
    root_coeff = math.sqrt(2.0 / math.pi)
    bend = jnp.tanh(root_coeff * (values + GELU_COEFF * values * values * values))
    gelu_value = 0.5 * values * (1.0 + bend)
    gelu_slope = 0.5 * (1.0 + bend) + 0.5 * values * (1.0 - bend * bend) * root_coeff * (
        1.0 + 3.0 * GELU_COEFF * values * values
    )
    return (gelu_value, gelu_slope)


def feed_slice(weight):
    y = lax.axis_index("y")
    padded = jnp.pad(weight, ((0, 0), (0, 4 * FEED_SLICE - weight.shape[1])))
    return lax.dynamic_slice_in_dim(padded, y * FEED_SLICE, FEED_SLICE, 1)


def local(
    tokens,
    cotangent,
    lengths,
    query_weight,
    key_weight,
    value_weight,
    out_weight,
    gate_weight,
    up_weight,
    down_weight,
    input_gain,
    query_gain,
    key_gain,
    attention_gain,
    feedforward_gain,
    output_gain,
):
    low = jnp.bfloat16
    row_count, model_width = tokens.shape
    head_size = key_weight.shape[1]
    head_count = query_weight.shape[1] // head_size
    query_width = head_count * head_size
    feed_width = gate_weight.shape[1]
    gain_shard = input_gain.shape[0]
    head_shard = query_gain.shape[0]
    scaling_factor = head_size ** (-0.5)
    y = lax.axis_index("y")
    seq_index = lax.axis_index("xl") * 4 + y
    positions = seq_index * row_count + lax.iota(jnp.int32, row_count)
    valid_rows = (positions < lengths[0]).astype(jnp.float32)[:, None]
    cosine_table, sine_table = rotary_tables(positions, head_size)
    hop_total = 2

    def spread(vector):
        return jnp.pad(vector, (0, gain_shard - head_shard))

    gain_columns = jnp.stack(
        [
            input_gain,
            attention_gain,
            feedforward_gain,
            output_gain,
            spread(query_gain),
            spread(key_gain),
        ],
        axis=1,
    )
    gain_columns = jnp.pad(gain_columns, ((0, 0), (0, 122)))
    feed_blocks = lax.all_gather(
        jnp.concatenate(
            [feed_slice(gate_weight), feed_slice(up_weight), feed_slice(down_weight)], axis=1
        ),
        DP,
        axis=0,
        tiled=True,
    )
    first, arrived = gather_rows(
        jnp.concatenate([query_weight, key_weight, value_weight, gain_columns], axis=1)
    )
    qkv_width = query_width + 2 * head_size
    full_qkv = first[:, :qkv_width]
    gains = 1.0 + first[:, qkv_width:].astype(jnp.float32)
    gain_rows = gains.T
    one_input = gain_rows[0]
    one_attention = gain_rows[1]
    one_feed = gain_rows[2]
    one_output = gain_rows[3]
    one_query = gain_rows[4].reshape(16, gain_shard)[:, :head_shard].reshape(head_size)
    one_key = gain_rows[5].reshape(16, gain_shard)[:, :head_shard].reshape(head_size)

    residual = tokens.astype(jnp.float32)
    input_scale = inverse_rms(residual)
    normed_input = residual * input_scale
    attention_input = (normed_input * one_input).astype(low)
    qkv_raw = jnp.dot(attention_input, full_qkv, preferred_element_type=jnp.float32)
    query_raw = qkv_raw[:, :query_width]
    key_raw = qkv_raw[:, query_width : query_width + head_size]
    value_raw = qkv_raw[:, query_width + head_size :]
    query_heads = query_raw.reshape(row_count, head_count, head_size)
    query_scale = inverse_rms(query_heads)
    query_hat = query_heads * query_scale
    query_low = rotate(
        query_hat * one_query, cosine_table[:, None, :], sine_table[:, None, :]
    ).astype(low)
    key_scale = inverse_rms(key_raw)
    key_hat = key_raw * key_scale
    key_low = rotate(key_hat * one_key, cosine_table, sine_table).astype(low)
    value_low = value_raw.astype(low)
    local_pair = jnp.concatenate([key_low, value_low], axis=1)
    rim_blocks = [from_behind(local_pair, distance) for distance in (1, 2)]
    input_ring = lax.all_gather(ordered(attention_input, *rim_blocks), "y", axis=0, tiled=True)
    full_out, _ = gather_rows(ordered(out_weight, *arrived), (local_pair,))
    key_rows = jnp.concatenate(rim_blocks[::-1] + [local_pair], axis=0)
    key_count = key_rows.shape[0]
    key_positions = (seq_index - hop_total) * row_count + lax.iota(jnp.int32, key_count)
    offsets = positions[:, None] - key_positions[None, :]
    allowed = (offsets >= 0) & (offsets < WINDOW) & (key_positions[None, :] >= 0)
    keys_only = key_rows[:, :head_size]
    values_only = key_rows[:, head_size:]

    def masked_scores():
        raw_scores = (
            jnp.einsum("thd,kd->htk", query_low, keys_only, preferred_element_type=jnp.float32)
            * scaling_factor
        )
        return jnp.where(allowed[None], raw_scores, -1e30)

    masked = masked_scores()
    row_top = jnp.max(masked, axis=-1, keepdims=True)
    exponent_terms = jnp.exp(masked - row_top)
    row_total = jnp.sum(exponent_terms, axis=-1, keepdims=True)
    log_total = row_top + jnp.log(row_total)
    probs_low = (exponent_terms / row_total).astype(low)
    context = jnp.einsum("htk,kd->thd", probs_low, values_only, preferred_element_type=jnp.float32)
    context_low = context.reshape(row_count, query_width).astype(low)
    attention_raw = jnp.einsum(
        "tq,dq->td", context_low, full_out, preferred_element_type=jnp.float32
    )
    attention_scale = inverse_rms(attention_raw)
    attention_hat = attention_raw * attention_scale
    hidden_state = residual + attention_hat * one_attention
    state_scale = inverse_rms(hidden_state)
    state_hat = hidden_state * state_scale
    feed_input = (state_hat * one_feed).astype(low)

    feed_blocks, feed_input = lax.optimization_barrier((feed_blocks, feed_input))
    gate_up = feed_blocks[:, : 2 * FEED_SLICE]
    down = feed_blocks[:, 2 * FEED_SLICE :]
    _, feed_1, feed_2, feed_3 = gather_ring(feed_input)
    feed_chunks = [feed_input, jnp.concatenate([feed_1, feed_3], axis=0), feed_2]
    kept = []
    parts = []
    for chunk in feed_chunks:
        raw = jnp.dot(chunk, gate_up, preferred_element_type=jnp.float32)
        gate_raw = raw[:, :FEED_SLICE]
        up_raw = raw[:, FEED_SLICE:]
        gelu_value, gelu_slope = gelu_parts(gate_raw)
        hidden = (gelu_value * up_raw).astype(low)
        kept.append((hidden, gelu_value.astype(low), (gelu_slope * up_raw).astype(low)))
        parts.append(jnp.einsum("tf,df->td", hidden, down, preferred_element_type=jnp.float32))
    down_raw = sum_ring(parts)
    down_scale = inverse_rms(down_raw)
    down_hat = down_raw * down_scale
    layer_value = hidden_state + down_hat * one_output
    layer_output = (valid_rows * layer_value).astype(low)
    upstream = cotangent.astype(jnp.float32) * valid_rows
    output_gain_vec = jnp.sum(upstream * down_hat, axis=0)
    down_grad_low = rms_backward(down_raw, down_scale, upstream * one_output).astype(low)

    _, down_1, down_2, down_3 = gather_ring(down_grad_low)
    down_chunks = [down_grad_low, jnp.concatenate([down_1, down_3], axis=0), down_2]
    grads = []
    parts = []
    for chunk, (_, value, slope) in zip(down_chunks, kept):
        hidden_grad = jnp.dot(chunk, down, preferred_element_type=jnp.float32)
        both = jnp.concatenate(
            [
                (hidden_grad * slope.astype(jnp.float32)).astype(low),
                (hidden_grad * value.astype(jnp.float32)).astype(low),
            ],
            axis=1,
        )
        grads.append(both)
        parts.append(jnp.einsum("tf,df->td", both, gate_up, preferred_element_type=jnp.float32))
    block_part = sum_ring(parts)
    down_weight_part = jnp.einsum(
        "tc,tf->cf",
        jnp.concatenate(down_chunks, axis=0),
        jnp.concatenate([hidden for hidden, _, _ in kept], axis=0),
        preferred_element_type=jnp.float32,
    ).astype(low)
    gate_up_part = jnp.einsum(
        "tc,tf->cf",
        jnp.concatenate(feed_chunks, axis=0),
        jnp.concatenate(grads, axis=0),
        preferred_element_type=jnp.float32,
    ).astype(low)
    block_part, down_weight_part, gate_up_part = lax.optimization_barrier(
        (block_part, down_weight_part, gate_up_part)
    )
    down_chip = core_sum(down_weight_part)
    gate_up_chip = core_sum(gate_up_part)

    feed_gain_vec = jnp.sum(block_part * state_hat, axis=0)
    state_grad = upstream + rms_backward(hidden_state, state_scale, block_part * one_feed)
    attention_gain_vec = jnp.sum(state_grad * attention_hat, axis=0)
    attention_grad_low = rms_backward(
        attention_raw, attention_scale, state_grad * one_attention
    ).astype(low)
    attention_grad_low, down_chip, gate_up_chip = lax.optimization_barrier(
        (attention_grad_low, down_chip, gate_up_chip)
    )
    down_column = z_sum(down_chip)
    gate_up_column = z_sum(gate_up_chip)
    out_ring = lax.all_gather(
        jnp.concatenate([attention_grad_low, context_low], axis=1), "y", axis=0, tiled=True
    )
    attention_ring = out_ring[:, :model_width]
    context_ring = lax.dynamic_slice_in_dim(
        out_ring, model_width + y * (query_width // 4), query_width // 4, 1
    )
    context_grad = jnp.einsum(
        "td,dq->tq", attention_grad_low, full_out, preferred_element_type=jnp.float32
    )
    context_grad_low = context_grad.reshape(row_count, head_count, head_size).astype(low)
    probs_again = jnp.exp(masked_scores() - log_total)
    probs_again_low = probs_again.astype(low)
    prob_grad = jnp.einsum(
        "thd,kd->htk", context_grad_low, values_only, preferred_element_type=jnp.float32
    )
    score_grad = probs_again * (
        prob_grad - jnp.sum(probs_again * prob_grad, axis=-1, keepdims=True)
    )
    score_grad_low, down_column = lax.optimization_barrier((score_grad.astype(low), down_column))
    down_weight_sum = x_sum(down_column)
    key_rot_rows = (
        jnp.einsum("htk,thd->kd", score_grad_low, query_low, preferred_element_type=jnp.float32)
        * scaling_factor
    )
    value_rows = jnp.einsum(
        "htk,thd->kd", probs_again_low, context_grad_low, preferred_element_type=jnp.float32
    )
    pair_grad = jnp.concatenate([key_rot_rows, value_rows], axis=1)
    local_grad = pair_grad[hop_total * row_count :]
    for distance in range(1, hop_total + 1):
        begin_row = (hop_total - distance) * row_count
        local_grad = local_grad + from_behind(
            pair_grad[begin_row : begin_row + row_count].astype(low), -distance
        ).astype(jnp.float32)
    query_rot_grad = (
        jnp.einsum("htk,kd->thd", score_grad_low, keys_only, preferred_element_type=jnp.float32)
        * scaling_factor
    )
    key_norm_grad = rotate_back(local_grad[:, :head_size], cosine_table, sine_table)
    key_gain_vec = jnp.sum(key_norm_grad * key_hat, axis=0)
    key_raw_low = rms_backward(key_raw, key_scale, key_norm_grad * one_key).astype(low)
    value_raw_low = local_grad[:, head_size:].astype(low)
    query_norm_grad = rotate_back(query_rot_grad, cosine_table[:, None, :], sine_table[:, None, :])
    query_gain_vec = jnp.sum(query_norm_grad * query_hat, axis=(0, 1))
    query_raw_low = (
        rms_backward(query_heads, query_scale, query_norm_grad * one_query)
        .reshape(row_count, query_width)
        .astype(low)
    )
    qkv_grad = jnp.concatenate([query_raw_low, key_raw_low, value_raw_low], axis=1)
    qkv_grad, gate_up_column = lax.optimization_barrier((qkv_grad, gate_up_column))
    gate_up_sum = x_sum(gate_up_column)
    qkv_cut = qkv_grad.reshape(row_count, 4, qkv_grad.shape[1] // 4)
    qkv_ring = in_order(
        [pick(qkv_cut, y, 1)]
        + [give(pick(qkv_cut, (y + by) % 4, 1), "y", by) for by in (3, 2, 1)]
    )
    qkv_ring = jnp.concatenate(qkv_ring, axis=0)
    input_grad = jnp.einsum("tq,dq->td", qkv_grad, full_qkv, preferred_element_type=jnp.float32)
    input_gain_vec = jnp.sum(input_grad * normed_input, axis=0)
    tokens_grad = (state_grad + rms_backward(residual, input_scale, input_grad * one_input)).astype(
        low
    )

    def spread_head(vector):
        return jnp.pad(
            vector.reshape(16, head_shard), ((0, 0), (0, gain_shard - head_shard))
        ).reshape(model_width)

    gain_block = jnp.stack(
        [
            input_gain_vec,
            attention_gain_vec,
            feed_gain_vec,
            output_gain_vec,
            spread_head(query_gain_vec),
            spread_head(key_gain_vec),
        ],
        axis=1,
    )
    gain_block = jnp.pad(gain_block, ((0, 0), (0, 122))).astype(low)
    qkv_part = jnp.einsum("tc,tq->cq", input_ring, qkv_ring, preferred_element_type=jnp.float32)
    out_part = jnp.einsum(
        "tc,tq->cq", attention_ring, context_ring, preferred_element_type=jnp.float32
    )
    attention_part = jnp.concatenate([qkv_part.astype(low), out_part.astype(low), gain_block], axis=1)
    attention_sum = x_sum(z_sum(core_sum(attention_part)))
    down_blocks = in_order(gather_ring(down_weight_sum))
    gate_up_blocks = in_order(gather_ring(gate_up_sum))
    attention_blocks = in_order(gather_ring(attention_sum))
    down_weight_grad = jnp.concatenate(down_blocks, axis=1)[:, :feed_width]
    gate_weight_grad = jnp.concatenate([b[:, :FEED_SLICE] for b in gate_up_blocks], axis=1)
    up_weight_grad = jnp.concatenate([b[:, FEED_SLICE:] for b in gate_up_blocks], axis=1)
    qkv_cols = qkv_grad.shape[1] // 4
    out_cols = query_width // 4
    qkv_weight_grad = jnp.concatenate([b[:, :qkv_cols] for b in attention_blocks], axis=1)
    out_weight_grad = jnp.concatenate(
        [b[:, qkv_cols : qkv_cols + out_cols] for b in attention_blocks], axis=1
    )
    gain_sum = sum(b[:, qkv_cols + out_cols :].astype(jnp.float32) for b in attention_blocks)
    wide = jnp.float32
    return (
        layer_output,
        tokens_grad,
        qkv_weight_grad[:, :query_width].astype(wide),
        qkv_weight_grad[:, query_width : query_width + head_size].astype(wide),
        qkv_weight_grad[:, query_width + head_size :].astype(wide),
        out_weight_grad.astype(wide),
        gate_weight_grad[:, :feed_width].astype(wide),
        up_weight_grad[:, :feed_width].astype(wide),
        down_weight_grad.astype(wide),
        gain_sum[:, 0],
        gain_sum[:head_shard, 4],
        gain_sum[:head_shard, 5],
        gain_sum[:, 1],
        gain_sum[:, 2],
        gain_sum[:, 3],
    )


def solution(mesh):
    fine = Mesh(mesh.devices.reshape(SIZES), AXES)
    rows = P(AXES, None)
    matrix = P(DP, None)
    vector = P(DP)
    return jax.shard_map(
        local,
        mesh=fine,
        in_specs=(rows, rows, vector) + (matrix,) * 7 + (vector,) * 6,
        out_specs=(rows, rows) + (matrix,) * 7 + (vector,) * 6,
        check_vma=False,
    )
```

```python
import functools
import math

import jax
import jax.numpy as jnp
from jax import lax
from jax.experimental import pallas as pl
from jax.experimental.pallas import tpu as pltpu
from jax.sharding import Mesh
from jax.sharding import PartitionSpec as P

WINDOW = 512


EPSILON = 1e-06
GELU_COEFF = 0.044715


AXES = ("z", "xh", "core", "xl", "y")
SIZES = (4, 2, 2, 2, 4)
DP = ("z", "xh", "core")
SEQ = ("xl", "y")
FEED_SLICE = 1792


def from_behind(array, by):
    pairs = [(i, i + by) for i in range(8) if 0 <= i + by < 8]
    return lax.ppermute(array, SEQ, pairs)


def take(array, axis, by):
    count = lax.axis_size(axis)
    return lax.ppermute(array, axis, [((i + by) % count, i) for i in range(count)])


def give(array, axis, by):
    count = lax.axis_size(axis)
    return lax.ppermute(array, axis, [(i, (i + by) % count) for i in range(count)])


def swap_x(array):
    return lax.ppermute(array, ("xh", "xl"), [(0, 3), (3, 0), (1, 2), (2, 1)])


def ordered(value, *after):
    return lax.optimization_barrier((value,) + after)[0]


def gather_rows(block, wait=()):
    rows, width = block.shape
    z = lax.axis_index("z")
    xh = lax.axis_index("xh")
    core = lax.axis_index("core")
    beside = swap_x(block)
    pair = jnp.where(xh == 0, jnp.stack([block, beside]), jnp.stack([beside, block]))
    ring = [(take(pair, "z", by), by) for by in (1, 3, 2)]
    arrived = [piece for piece, _ in ring]
    own = jnp.zeros((4, 2, rows, width), block.dtype)
    own = lax.dynamic_update_slice_in_dim(own, pair[None], z, 0)
    if wait:
        own = ordered(own, *wait)
    for piece, by in ring:
        own = lax.dynamic_update_slice_in_dim(own, piece[None], (z + by) % 4, 0)
    other = give(own, "core", 1)
    both = jnp.where(
        core == 0, jnp.stack([own, other], axis=2), jnp.stack([other, own], axis=2)
    )
    return both.reshape(16 * rows, width), arrived


def core_sum(part):
    core = lax.axis_index("core")
    rows, width = part.shape[0] // 16, part.shape[1]
    by_core = part.reshape(8, 2, rows, width)
    got = give(pick(by_core, 1 - core, 1), "core", 1)
    total = pick(by_core, core, 1).astype(jnp.float32) + got.astype(jnp.float32)
    return total.astype(jnp.bfloat16).reshape(4, 2, rows, width)


def z_sum(chip):
    z = lax.axis_index("z")
    total = pick(chip, z, 0).astype(jnp.float32)
    for by in (1, 3, 2):
        total = total + give(pick(chip, (z + by) % 4, 0), "z", by).astype(jnp.float32)
    return total.astype(jnp.bfloat16)


def x_sum(column):
    xh = lax.axis_index("xh")
    got = swap_x(pick(column, 1 - xh, 0))
    half = (pick(column, xh, 0).astype(jnp.float32) + got.astype(jnp.float32)).astype(jnp.bfloat16)
    got = give(half, "xl", 1)
    return (half.astype(jnp.float32) + got.astype(jnp.float32)).astype(jnp.bfloat16)


def gather_ring(block):
    return [block, take(block, "y", 1), take(block, "y", 2), take(block, "y", 3)]


def sum_ring(parts):
    rows = parts[0].shape[0]
    low = jnp.bfloat16
    others = ((parts[1][:rows], 1), (parts[1][rows:], 3), (parts[2], 2))
    total = parts[0].astype(jnp.float32)
    for part, by in others:
        total = total + give(part.astype(low), "y", by).astype(jnp.float32)
    return total


def in_order(blocks):
    y = lax.axis_index("y")
    placed = []
    for place in range(4):
        value = blocks[(place - 3) % 4]
        for at in range(3):
            value = jnp.where(y == at, blocks[(place - at) % 4], value)
        placed.append(value)
    return placed


def pick(array, index, axis):
    return lax.dynamic_index_in_dim(array, index, axis, keepdims=False)


def inverse_rms(values):
    return lax.rsqrt(jnp.mean(values * values, axis=-1, keepdims=True) + EPSILON)


def rms_backward(values, scaling, upstream):
    inner = jnp.mean(upstream * values, axis=-1, keepdims=True)
    return scaling * (upstream - values * (scaling * scaling) * inner)


def rotary_tables(positions, head_size):
    half_size = head_size // 2
    exponents = lax.iota(jnp.float32, half_size) * (2.0 / head_size)
    frequency = jnp.power(10000.0, -exponents)
    angles = positions.astype(jnp.float32)[:, None] * frequency[None, :]
    return (jnp.cos(angles), jnp.sin(angles))


def rotate(values, cosine_table, sine_table):
    half_size = values.shape[-1] // 2
    first_half = values[..., :half_size]
    second_half = values[..., half_size:]
    return jnp.concatenate(
        [
            first_half * cosine_table - second_half * sine_table,
            second_half * cosine_table + first_half * sine_table,
        ],
        axis=-1,
    )


def rotate_back(upstream, cosine_table, sine_table):
    half_size = upstream.shape[-1] // 2
    first_half = upstream[..., :half_size]
    second_half = upstream[..., half_size:]
    return jnp.concatenate(
        [
            first_half * cosine_table + second_half * sine_table,
            second_half * cosine_table - first_half * sine_table,
        ],
        axis=-1,
    )


def gelu_parts(values):
    root_coeff = math.sqrt(2.0 / math.pi)
    bend = jnp.tanh(root_coeff * (values + GELU_COEFF * values * values * values))
    gelu_value = 0.5 * values * (1.0 + bend)
    gelu_slope = 0.5 * (1.0 + bend) + 0.5 * values * (1.0 - bend * bend) * root_coeff * (
        1.0 + 3.0 * GELU_COEFF * values * values
    )
    return (gelu_value, gelu_slope)


HEADS = 4
HEAD = 256
SCALE = HEAD**-0.5
ROWS = 256


def dot(left, right, left_axis=1, right_axis=0):
    return lax.dot_general(
        left,
        right,
        (((left_axis,), (right_axis,)), ((), ())),
        preferred_element_type=jnp.float32,
    )


def turn(first, second, cosine, sine):
    return first * cosine - second * sine, second * cosine + first * sine


def turn_back(first, second, cosine, sine):
    return first * cosine + second * sine, second * cosine - first * sine


def rows_call(body, outs, flops, name):
    def call(*operands):
        specs = [
            pl.BlockSpec(memory_space=pltpu.SMEM)
            if operand.dtype == jnp.int32
            else pl.BlockSpec(memory_space=pltpu.VMEM)
            for operand in operands
        ]
        moved = sum(operand.size * operand.dtype.itemsize for operand in operands)
        return pl.pallas_call(
            body,
            out_shape=[jax.ShapeDtypeStruct(shape, dtype) for shape, dtype in outs],
            in_specs=specs,
            out_specs=[pl.BlockSpec(memory_space=pltpu.VMEM) for _ in outs],
            compiler_params=pltpu.CompilerParams(vmem_limit_bytes=48 * 1024 * 1024),
            cost_estimate=pl.CostEstimate(flops=flops, bytes_accessed=moved, transcendentals=0),
            name=name,
        )(*operands)

    return call


def prepare_body(raw, gain, cosine, sine, query, pair):
    cos, sin = cosine[...], sine[...]
    half = HEAD // 2

    def finish(block, gains):
        hat = block * inverse_rms(block) * gains
        first, second = turn(hat[:, :half], hat[:, half:], cos, sin)
        return jnp.concatenate([first, second], axis=1).astype(jnp.bfloat16)

    for head in range(HEADS):
        at = slice(head * HEAD, (head + 1) * HEAD)
        query[:, at] = finish(raw[:, at], gain[0:1, :])
    keys = HEADS * HEAD
    pair[:, :HEAD] = finish(raw[:, keys : keys + HEAD], gain[1:2, :])
    pair[:, HEAD:] = raw[:, keys + HEAD : keys + 2 * HEAD].astype(jnp.bfloat16)


def attend_body(place, query, far, near, own, context, log_total):
    row = lax.broadcasted_iota(jnp.int32, (ROWS, ROWS), 0)
    column = lax.broadcasted_iota(jnp.int32, (ROWS, ROWS), 1)
    seq = place[0]
    allowed = (
        (row < column) & (seq >= 2),
        jnp.full((ROWS, ROWS), seq >= 1),
        column <= row,
    )
    blocks = (far, near, own)
    lane = lax.broadcasted_iota(jnp.int32, (ROWS, 128), 1)
    logs = jnp.zeros((ROWS, 128), jnp.float32)
    for head in range(HEADS):
        at = slice(head * HEAD, (head + 1) * HEAD)
        scores = [
            jnp.where(ok, dot(query[:, at], block[:, :HEAD], 1, 1) * SCALE, -1e30)
            for ok, block in zip(allowed, blocks)
        ]
        top = jnp.max(jnp.maximum(jnp.maximum(scores[0], scores[1]), scores[2]), 1, keepdims=True)
        terms = [jnp.exp(score - top) for score in scores]
        total = jnp.sum(terms[0] + terms[1] + terms[2], 1, keepdims=True)
        share = 1.0 / total
        out = sum(
            dot((term * share).astype(jnp.bfloat16), block[:, HEAD:])
            for term, block in zip(terms, blocks)
        )
        context[:, at] = out.astype(jnp.bfloat16)
        logs = jnp.where(lane == head, top + jnp.log(total), logs)
    log_total[...] = logs.T[:8]


def attend_back_body(
    place,
    upstream,
    out_weight,
    query,
    far,
    near,
    own,
    log_total,
    raw,
    gain,
    cosine,
    sine,
    far_grad,
    near_grad,
    own_grad,
    query_grad,
    gain_grad,
):
    low = jnp.bfloat16
    half = HEAD // 2
    key_at = lax.broadcasted_iota(jnp.int32, (ROWS, ROWS), 0)
    query_at = lax.broadcasted_iota(jnp.int32, (ROWS, ROWS), 1)
    seq = place[0]
    allowed = (
        (query_at < key_at) & (seq >= 2),
        jnp.full((ROWS, ROWS), seq >= 1),
        key_at <= query_at,
    )
    blocks = (far, near, own)
    cos, sin = cosine[...], sine[...]
    key_grads = [0.0, 0.0, 0.0]
    value_grads = [0.0, 0.0, 0.0]
    gain_sum = jnp.zeros((1, HEAD), jnp.float32)
    for head in range(HEADS):
        at = slice(head * HEAD, (head + 1) * HEAD)
        context_grad = dot(upstream[...], out_weight[:, at]).astype(low)
        queries = query[:, at]
        logs = log_total[head : head + 1, :]
        probs = [
            jnp.where(ok, jnp.exp(dot(block[:, :HEAD], queries, 1, 1) * SCALE - logs), 0.0)
            for ok, block in zip(allowed, blocks)
        ]
        prob_grads = [dot(block[:, HEAD:], context_grad, 1, 1) for block in blocks]
        inner = jnp.sum(
            probs[0] * prob_grads[0] + probs[1] * prob_grads[1] + probs[2] * prob_grads[2],
            0,
            keepdims=True,
        )
        query_rot = 0.0
        for at_block, block in enumerate(blocks):
            score_grad = (probs[at_block] * (prob_grads[at_block] - inner)).astype(low)
            query_rot = query_rot + dot(score_grad, block[:, :HEAD], 0, 0)
            key_grads[at_block] = key_grads[at_block] + dot(score_grad, queries)
            value_grads[at_block] = value_grads[at_block] + dot(
                probs[at_block].astype(low), context_grad
            )
        query_rot = query_rot * SCALE
        first, second = turn_back(query_rot[:, :half], query_rot[:, half:], cos, sin)
        upper = jnp.concatenate([first, second], axis=1)
        block = raw[:, at]
        scaling = inverse_rms(block)
        gain_sum = gain_sum + jnp.sum(upper * (block * scaling), 0, keepdims=True)
        query_grad[:, at] = rms_backward(block, scaling, upper * gain[0:1, :]).astype(low)
    gain_grad[...] = jnp.broadcast_to(gain_sum, (8, HEAD))
    far_grad[:, :HEAD] = (key_grads[0] * SCALE).astype(low)
    far_grad[:, HEAD:] = value_grads[0].astype(low)
    near_grad[:, :HEAD] = (key_grads[1] * SCALE).astype(low)
    near_grad[:, HEAD:] = value_grads[1].astype(low)
    own_grad[:, :HEAD] = key_grads[2] * SCALE
    own_grad[:, HEAD:] = value_grads[2]


def pair_back_body(own, near, far, raw, gain, cosine, sine, pair_grad, gain_grad):
    half = HEAD // 2
    low = jnp.bfloat16
    total = own[...] + near[...].astype(jnp.float32) + far[...].astype(jnp.float32)
    first, second = turn_back(total[:, :half], total[:, half:HEAD], cosine[...], sine[...])
    upper = jnp.concatenate([first, second], axis=1)
    block = raw[:, HEADS * HEAD : (HEADS + 1) * HEAD]
    scaling = inverse_rms(block)
    gain_sum = jnp.sum(upper * (block * scaling), 0, keepdims=True)
    gain_grad[...] = jnp.broadcast_to(gain_sum, (8, HEAD))
    pair_grad[:, :HEAD] = rms_backward(block, scaling, upper * gain[1:2, :]).astype(low)
    pair_grad[:, HEAD:] = total[:, HEAD:].astype(low)


def feed_slice(weight):
    y = lax.axis_index("y")
    padded = jnp.pad(weight, ((0, 0), (0, 4 * FEED_SLICE - weight.shape[1])))
    return lax.dynamic_slice_in_dim(padded, y * FEED_SLICE, FEED_SLICE, 1)


def local(
    tokens,
    cotangent,
    lengths,
    query_weight,
    key_weight,
    value_weight,
    out_weight,
    gate_weight,
    up_weight,
    down_weight,
    input_gain,
    query_gain,
    key_gain,
    attention_gain,
    feedforward_gain,
    output_gain,
):
    low = jnp.bfloat16
    row_count, model_width = tokens.shape
    head_size = key_weight.shape[1]
    head_count = query_weight.shape[1] // head_size
    query_width = head_count * head_size
    feed_width = gate_weight.shape[1]
    gain_shard = input_gain.shape[0]
    head_shard = query_gain.shape[0]
    y = lax.axis_index("y")
    seq_index = lax.axis_index("xl") * 4 + y
    positions = seq_index * row_count + lax.iota(jnp.int32, row_count)
    valid_rows = (positions < lengths[0]).astype(jnp.float32)[:, None]
    cosine_table, sine_table = rotary_tables(positions, head_size)

    def spread(vector):
        return jnp.pad(vector, (0, gain_shard - head_shard))

    gain_columns = jnp.stack(
        [
            input_gain,
            attention_gain,
            feedforward_gain,
            output_gain,
            spread(query_gain),
            spread(key_gain),
        ],
        axis=1,
    )
    gain_columns = jnp.pad(gain_columns, ((0, 0), (0, 122)))
    feed_blocks = lax.all_gather(
        jnp.concatenate(
            [feed_slice(gate_weight), feed_slice(up_weight), feed_slice(down_weight)], axis=1
        ),
        DP,
        axis=0,
        tiled=True,
    )
    first, arrived = gather_rows(
        jnp.concatenate([query_weight, key_weight, value_weight, gain_columns], axis=1)
    )
    qkv_width = query_width + 2 * head_size
    full_qkv = first[:, :qkv_width]
    gains = 1.0 + first[:, qkv_width:].astype(jnp.float32)
    gain_rows = gains.T
    one_input = gain_rows[0]
    one_attention = gain_rows[1]
    one_feed = gain_rows[2]
    one_output = gain_rows[3]
    one_query = gain_rows[4].reshape(16, gain_shard)[:, :head_shard].reshape(head_size)
    one_key = gain_rows[5].reshape(16, gain_shard)[:, :head_shard].reshape(head_size)

    residual = tokens.astype(jnp.float32)
    input_scale = inverse_rms(residual)
    normed_input = residual * input_scale
    attention_input = (normed_input * one_input).astype(low)
    qkv_raw = jnp.dot(attention_input, full_qkv, preferred_element_type=jnp.float32)
    head_gain = jnp.pad(jnp.stack([one_query, one_key]), ((0, 6), (0, 0)))
    prepare = rows_call(
        prepare_body,
        [((row_count, query_width), low), ((row_count, 2 * head_size), low)],
        1000000,
        "prepare",
    )
    query_low, local_pair = prepare(qkv_raw, head_gain, cosine_table, sine_table)
    near_pair, far_pair = (from_behind(local_pair, distance) for distance in (1, 2))
    rim_blocks = [near_pair, far_pair]
    input_ring = lax.all_gather(ordered(attention_input, *rim_blocks), "y", axis=0, tiled=True)
    full_out, _ = gather_rows(ordered(out_weight, *arrived), (local_pair,))
    place = seq_index.reshape(1).astype(jnp.int32)
    attend = rows_call(
        attend_body,
        [((row_count, query_width), low), ((8, row_count), jnp.float32)],
        4 * head_count * row_count * 3 * row_count * head_size,
        "attend",
    )
    context_low, log_total = attend(place, query_low, far_pair, near_pair, local_pair)
    attention_raw = jnp.einsum(
        "tq,dq->td", context_low, full_out, preferred_element_type=jnp.float32
    )
    attention_scale = inverse_rms(attention_raw)
    attention_hat = attention_raw * attention_scale
    hidden_state = residual + attention_hat * one_attention
    state_scale = inverse_rms(hidden_state)
    state_hat = hidden_state * state_scale
    feed_input = (state_hat * one_feed).astype(low)

    feed_blocks, feed_input = lax.optimization_barrier((feed_blocks, feed_input))
    gate_up = feed_blocks[:, : 2 * FEED_SLICE]
    down = feed_blocks[:, 2 * FEED_SLICE :]
    _, feed_1, feed_2, feed_3 = gather_ring(feed_input)
    feed_chunks = [feed_input, jnp.concatenate([feed_1, feed_3], axis=0), feed_2]
    kept = []
    parts = []
    for chunk in feed_chunks:
        raw = jnp.dot(chunk, gate_up, preferred_element_type=jnp.float32)
        gate_raw = raw[:, :FEED_SLICE]
        up_raw = raw[:, FEED_SLICE:]
        gelu_value, gelu_slope = gelu_parts(gate_raw)
        hidden = (gelu_value * up_raw).astype(low)
        kept.append((hidden, gelu_value.astype(low), (gelu_slope * up_raw).astype(low)))
        parts.append(jnp.einsum("tf,df->td", hidden, down, preferred_element_type=jnp.float32))
    down_raw = sum_ring(parts)
    down_scale = inverse_rms(down_raw)
    down_hat = down_raw * down_scale
    layer_value = hidden_state + down_hat * one_output
    layer_output = (valid_rows * layer_value).astype(low)
    upstream = cotangent.astype(jnp.float32) * valid_rows
    output_gain_vec = jnp.sum(upstream * down_hat, axis=0)
    down_grad_low = rms_backward(down_raw, down_scale, upstream * one_output).astype(low)

    _, down_1, down_2, down_3 = gather_ring(down_grad_low)
    down_chunks = [down_grad_low, jnp.concatenate([down_1, down_3], axis=0), down_2]
    grads = []
    parts = []
    for chunk, (_, value, slope) in zip(down_chunks, kept):
        hidden_grad = jnp.dot(chunk, down, preferred_element_type=jnp.float32)
        both = jnp.concatenate(
            [
                (hidden_grad * slope.astype(jnp.float32)).astype(low),
                (hidden_grad * value.astype(jnp.float32)).astype(low),
            ],
            axis=1,
        )
        grads.append(both)
        parts.append(jnp.einsum("tf,df->td", both, gate_up, preferred_element_type=jnp.float32))
    block_part = sum_ring(parts)
    down_weight_part = jnp.einsum(
        "tc,tf->cf",
        jnp.concatenate(down_chunks, axis=0),
        jnp.concatenate([hidden for hidden, _, _ in kept], axis=0),
        preferred_element_type=jnp.float32,
    ).astype(low)
    gate_up_part = jnp.einsum(
        "tc,tf->cf",
        jnp.concatenate(feed_chunks, axis=0),
        jnp.concatenate(grads, axis=0),
        preferred_element_type=jnp.float32,
    ).astype(low)
    block_part, down_weight_part, gate_up_part = lax.optimization_barrier(
        (block_part, down_weight_part, gate_up_part)
    )
    down_chip = core_sum(down_weight_part)
    gate_up_chip = core_sum(gate_up_part)

    feed_gain_vec = jnp.sum(block_part * state_hat, axis=0)
    state_grad = upstream + rms_backward(hidden_state, state_scale, block_part * one_feed)
    attention_gain_vec = jnp.sum(state_grad * attention_hat, axis=0)
    attention_grad_low = rms_backward(
        attention_raw, attention_scale, state_grad * one_attention
    ).astype(low)
    attention_grad_low, down_chip, gate_up_chip = lax.optimization_barrier(
        (attention_grad_low, down_chip, gate_up_chip)
    )
    down_column = z_sum(down_chip)
    gate_up_column = z_sum(gate_up_chip)
    out_ring = lax.all_gather(
        jnp.concatenate([attention_grad_low, context_low], axis=1), "y", axis=0, tiled=True
    )
    attention_ring = out_ring[:, :model_width]
    context_ring = lax.dynamic_slice_in_dim(
        out_ring, model_width + y * (query_width // 4), query_width // 4, 1
    )
    attend_back = rows_call(
        attend_back_body,
        [
            ((row_count, 2 * head_size), low),
            ((row_count, 2 * head_size), low),
            ((row_count, 2 * head_size), jnp.float32),
            ((row_count, query_width), low),
            ((8, head_size), jnp.float32),
        ],
        2 * row_count * query_width * (model_width + 15 * row_count),
        "attend_back",
    )
    far_grad, near_grad, own_grad, query_raw_low, query_gain_rows = attend_back(
        place,
        attention_grad_low,
        full_out,
        query_low,
        far_pair,
        near_pair,
        local_pair,
        log_total,
        qkv_raw,
        head_gain,
        cosine_table,
        sine_table,
    )
    far_grad, near_grad, down_column = lax.optimization_barrier((far_grad, near_grad, down_column))
    down_weight_sum = x_sum(down_column)
    pair_back = rows_call(
        pair_back_body,
        [((row_count, 2 * head_size), low), ((8, head_size), jnp.float32)],
        1000000,
        "pair_back",
    )
    pair_raw_low, key_gain_rows = pair_back(
        own_grad,
        from_behind(near_grad, -1),
        from_behind(far_grad, -2),
        qkv_raw,
        head_gain,
        cosine_table,
        sine_table,
    )
    query_gain_vec = query_gain_rows[0]
    key_gain_vec = key_gain_rows[0]
    qkv_grad = jnp.concatenate([query_raw_low, pair_raw_low], axis=1)
    qkv_grad, gate_up_column = lax.optimization_barrier((qkv_grad, gate_up_column))
    gate_up_sum = x_sum(gate_up_column)
    qkv_cut = qkv_grad.reshape(row_count, 4, qkv_grad.shape[1] // 4)
    qkv_ring = in_order(
        [pick(qkv_cut, y, 1)]
        + [give(pick(qkv_cut, (y + by) % 4, 1), "y", by) for by in (3, 2, 1)]
    )
    qkv_ring = jnp.concatenate(qkv_ring, axis=0)
    input_grad = jnp.einsum("tq,dq->td", qkv_grad, full_qkv, preferred_element_type=jnp.float32)
    input_gain_vec = jnp.sum(input_grad * normed_input, axis=0)
    tokens_grad = (state_grad + rms_backward(residual, input_scale, input_grad * one_input)).astype(
        low
    )

    def spread_head(vector):
        return jnp.pad(
            vector.reshape(16, head_shard), ((0, 0), (0, gain_shard - head_shard))
        ).reshape(model_width)

    gain_block = jnp.stack(
        [
            input_gain_vec,
            attention_gain_vec,
            feed_gain_vec,
            output_gain_vec,
            spread_head(query_gain_vec),
            spread_head(key_gain_vec),
        ],
        axis=1,
    )
    gain_block = jnp.pad(gain_block, ((0, 0), (0, 122))).astype(low)
    qkv_part = jnp.einsum("tc,tq->cq", input_ring, qkv_ring, preferred_element_type=jnp.float32)
    out_part = jnp.einsum(
        "tc,tq->cq", attention_ring, context_ring, preferred_element_type=jnp.float32
    )
    attention_part = jnp.concatenate([qkv_part.astype(low), out_part.astype(low), gain_block], axis=1)
    attention_column = z_sum(core_sum(attention_part))
    attention_sum = x_sum(attention_column)
    down_blocks = in_order(gather_ring(down_weight_sum))
    gate_up_pieces = gather_ring(gate_up_sum)
    gate_up_blocks = in_order([ordered(piece, attention_column) for piece in gate_up_pieces])
    attention_blocks = in_order(gather_ring(attention_sum))
    down_weight_grad = jnp.concatenate(down_blocks, axis=1)[:, :feed_width]
    gate_weight_grad = jnp.concatenate([b[:, :FEED_SLICE] for b in gate_up_blocks], axis=1)
    up_weight_grad = jnp.concatenate([b[:, FEED_SLICE:] for b in gate_up_blocks], axis=1)
    qkv_cols = qkv_grad.shape[1] // 4
    out_cols = query_width // 4
    qkv_weight_grad = jnp.concatenate([b[:, :qkv_cols] for b in attention_blocks], axis=1)
    out_weight_grad = jnp.concatenate(
        [b[:, qkv_cols : qkv_cols + out_cols] for b in attention_blocks], axis=1
    )
    gain_sum = sum(b[:, qkv_cols + out_cols :].astype(jnp.float32) for b in attention_blocks)
    wide = jnp.float32
    return (
        layer_output,
        tokens_grad,
        qkv_weight_grad[:, :query_width].astype(wide),
        qkv_weight_grad[:, query_width : query_width + head_size].astype(wide),
        qkv_weight_grad[:, query_width + head_size :].astype(wide),
        out_weight_grad.astype(wide),
        gate_weight_grad[:, :feed_width].astype(wide),
        up_weight_grad[:, :feed_width].astype(wide),
        down_weight_grad.astype(wide),
        gain_sum[:, 0],
        gain_sum[:head_shard, 4],
        gain_sum[:head_shard, 5],
        gain_sum[:, 1],
        gain_sum[:, 2],
        gain_sum[:, 3],
    )


def solution(mesh):
    fine = Mesh(mesh.devices.reshape(SIZES), AXES)
    rows = P(AXES, None)
    matrix = P(DP, None)
    vector = P(DP)
    return jax.shard_map(
        local,
        mesh=fine,
        in_specs=(rows, rows, vector) + (matrix,) * 7 + (vector,) * 6,
        out_specs=(rows, rows) + (matrix,) * 7 + (vector,) * 6,
        check_vma=False,
    )
```

```python
import functools
import math

import jax
import jax.numpy as jnp
from jax import lax
from jax.experimental import pallas as pl
from jax.experimental.pallas import tpu as pltpu
from jax.sharding import Mesh
from jax.sharding import PartitionSpec as P

EPSILON = 1e-06
GELU_COEFF = 0.044715
AXES = ("z", "xh", "core", "xl", "y")
SIZES = (4, 2, 2, 2, 4)
DP = ("z", "xh", "core")
SEQ = ("xl", "y")
FEED_SLICE = 1792
FEED_TILE = 896
HEADS = 4
HEAD = 256
SCALE = HEAD**-0.5
ROWS = 256
VMEM = 16 * 1024 * 1024
LONG = 12 * 10**9
SMALL = pl.CostEstimate(flops=1000, bytes_accessed=1000, transcendentals=0)


def from_behind(array, by):
    pairs = [(i, i + by) for i in range(8) if 0 <= i + by < 8]
    return lax.ppermute(array, SEQ, pairs)


def take(array, axis, by):
    count = lax.axis_size(axis)
    return lax.ppermute(array, axis, [((i + by) % count, i) for i in range(count)])


def give(array, axis, by):
    count = lax.axis_size(axis)
    return lax.ppermute(array, axis, [(i, (i + by) % count) for i in range(count)])


def swap_x(array):
    return lax.ppermute(array, ("xh", "xl"), [(0, 3), (3, 0), (1, 2), (2, 1)])


def ordered(value, *after):
    return lax.optimization_barrier((value,) + after)[0]


def pick(array, index, axis):
    return lax.dynamic_index_in_dim(array, index, axis, keepdims=False)


def with_other_x(block):
    xh = lax.axis_index("xh")
    beside = swap_x(block)
    return jnp.where(xh == 0, jnp.stack([block, beside]), jnp.stack([beside, block])), beside


def gather_rows(pair, wait=()):
    _, rows, width = pair.shape
    z = lax.axis_index("z")
    core = lax.axis_index("core")
    ring = [(take(pair, "z", by), by) for by in (1, 3, 2)]
    arrived = [piece for piece, _ in ring]
    own = jnp.zeros((4, 2, rows, width), pair.dtype)
    own = lax.dynamic_update_slice_in_dim(own, pair[None], z, 0)
    own = ordered(own, *wait)
    for piece, by in ring:
        own = lax.dynamic_update_slice_in_dim(own, piece[None], (z + by) % 4, 0)
    other = give(own, "core", 1)
    both = jnp.where(
        core == 0, jnp.stack([own, other], axis=2), jnp.stack([other, own], axis=2)
    )
    return both.reshape(16 * rows, width), arrived


def small_sum(chip):
    z = lax.axis_index("z")
    xh = lax.axis_index("xh")
    wide = jnp.float32
    total = pick(chip, z, 0).astype(wide)
    for by in (1, 3, 2):
        total = total + give(pick(chip, (z + by) % 4, 0), "z", by).astype(wide)
    column = total.astype(jnp.bfloat16)
    half = pick(column, xh, 0).astype(wide) + swap_x(pick(column, 1 - xh, 0)).astype(wide)
    half = half.astype(jnp.bfloat16)
    whole = (half.astype(wide) + give(half, "xl", 1).astype(wide)).astype(jnp.bfloat16)
    return whole, column


def in_order(blocks):
    y = lax.axis_index("y")
    placed = []
    for place in range(4):
        value = blocks[(place - 3) % 4]
        for at in range(3):
            value = jnp.where(y == at, blocks[(place - at) % 4], value)
        placed.append(value)
    return placed


def inverse_rms(values):
    return lax.rsqrt(jnp.mean(values * values, axis=-1, keepdims=True) + EPSILON)


def rms_backward(values, scaling, upstream):
    inner = jnp.mean(upstream * values, axis=-1, keepdims=True)
    return scaling * (upstream - values * (scaling * scaling) * inner)


def rotary_tables(positions, head_size):
    half_size = head_size // 2
    exponents = lax.iota(jnp.float32, half_size) * (2.0 / head_size)
    frequency = jnp.power(10000.0, -exponents)
    angles = positions.astype(jnp.float32)[:, None] * frequency[None, :]
    return (jnp.cos(angles), jnp.sin(angles))


def gelu_parts(values):
    root_coeff = math.sqrt(2.0 / math.pi)
    square = values * values
    bend = jnp.tanh(values * (root_coeff + (root_coeff * GELU_COEFF) * square))
    part = 0.5 + 0.5 * bend
    gelu_value = values * part
    inner = root_coeff + (3.0 * GELU_COEFF * root_coeff) * square
    gelu_slope = part + gelu_value * (1.0 - bend) * inner
    return (gelu_value, gelu_slope)


def dot(left, right, left_axis=1, right_axis=0):
    return lax.dot_general(
        left,
        right,
        (((left_axis,), (right_axis,)), ((), ())),
        preferred_element_type=jnp.float32,
    )


def turn(first, second, cosine, sine):
    return first * cosine - second * sine, second * cosine + first * sine


def turn_back(first, second, cosine, sine):
    return first * cosine + second * sine, second * cosine - first * sine


def rows_call(body, outs, name):
    def call(*operands):
        specs = [
            pl.BlockSpec(memory_space=pltpu.SMEM)
            if operand.dtype == jnp.int32
            else pl.BlockSpec(memory_space=pltpu.VMEM)
            for operand in operands
        ]
        return pl.pallas_call(
            body,
            out_shape=[jax.ShapeDtypeStruct(shape, dtype) for shape, dtype in outs],
            in_specs=specs,
            out_specs=[pl.BlockSpec(memory_space=pltpu.VMEM) for _ in outs],
            compiler_params=pltpu.CompilerParams(vmem_limit_bytes=VMEM),
            cost_estimate=SMALL,
            name=name,
        )(*operands)

    return call


def prepare_body(raw, gain, cosine, sine, query, pair):
    cos, sin = cosine[...], sine[...]
    half = HEAD // 2

    def finish(block, gains):
        hat = block * inverse_rms(block) * gains
        first, second = turn(hat[:, :half], hat[:, half:], cos, sin)
        return jnp.concatenate([first, second], axis=1).astype(jnp.bfloat16)

    for head in range(HEADS):
        at = slice(head * HEAD, (head + 1) * HEAD)
        query[:, at] = finish(raw[:, at], gain[0:1, :])
    keys = HEADS * HEAD
    pair[:, :HEAD] = finish(raw[:, keys : keys + HEAD], gain[1:2, :])
    pair[:, HEAD:] = raw[:, keys + HEAD : keys + 2 * HEAD].astype(jnp.bfloat16)


def attend_body(place, query, far, near, own, context, log_total):
    row = lax.broadcasted_iota(jnp.int32, (ROWS, ROWS), 0)
    column = lax.broadcasted_iota(jnp.int32, (ROWS, ROWS), 1)
    seq = place[0]
    allowed = (
        (row < column) & (seq >= 2),
        jnp.full((ROWS, ROWS), seq >= 1),
        column <= row,
    )
    blocks = (far, near, own)
    lane = lax.broadcasted_iota(jnp.int32, (ROWS, 128), 1)
    logs = jnp.zeros((ROWS, 128), jnp.float32)
    for head in range(HEADS):
        at = slice(head * HEAD, (head + 1) * HEAD)
        scores = [
            jnp.where(ok, dot(query[:, at], block[:, :HEAD], 1, 1) * SCALE, -1e30)
            for ok, block in zip(allowed, blocks)
        ]
        top = jnp.max(jnp.maximum(jnp.maximum(scores[0], scores[1]), scores[2]), 1, keepdims=True)
        terms = [jnp.exp(score - top) for score in scores]
        total = jnp.sum(terms[0] + terms[1] + terms[2], 1, keepdims=True)
        share = 1.0 / total
        out = sum(
            dot((term * share).astype(jnp.bfloat16), block[:, HEAD:])
            for term, block in zip(terms, blocks)
        )
        context[:, at] = out.astype(jnp.bfloat16)
        logs = jnp.where(lane == head, top + jnp.log(total), logs)
    log_total[...] = logs.T[:8]


def attend_back_body(
    place,
    upstream,
    out_weight,
    query,
    far,
    near,
    own,
    log_total,
    raw,
    gain,
    cosine,
    sine,
    far_grad,
    near_grad,
    own_grad,
    query_grad,
    gain_grad,
):
    low = jnp.bfloat16
    half = HEAD // 2
    key_at = lax.broadcasted_iota(jnp.int32, (ROWS, ROWS), 0)
    query_at = lax.broadcasted_iota(jnp.int32, (ROWS, ROWS), 1)
    seq = place[0]
    allowed = (
        (query_at < key_at) & (seq >= 2),
        jnp.full((ROWS, ROWS), seq >= 1),
        key_at <= query_at,
    )
    blocks = (far, near, own)
    cos, sin = cosine[...], sine[...]
    key_grads = [0.0, 0.0, 0.0]
    value_grads = [0.0, 0.0, 0.0]
    gain_sum = jnp.zeros((1, HEAD), jnp.float32)
    for head in range(HEADS):
        at = slice(head * HEAD, (head + 1) * HEAD)
        context_grad = dot(upstream[...], out_weight[:, at]).astype(low)
        queries = query[:, at]
        logs = log_total[head : head + 1, :]
        probs = [
            jnp.where(ok, jnp.exp(dot(block[:, :HEAD], queries, 1, 1) * SCALE - logs), 0.0)
            for ok, block in zip(allowed, blocks)
        ]
        prob_grads = [dot(block[:, HEAD:], context_grad, 1, 1) for block in blocks]
        inner = jnp.sum(
            probs[0] * prob_grads[0] + probs[1] * prob_grads[1] + probs[2] * prob_grads[2],
            0,
            keepdims=True,
        )
        query_rot = 0.0
        for at_block, block in enumerate(blocks):
            score_grad = (probs[at_block] * (prob_grads[at_block] - inner)).astype(low)
            query_rot = query_rot + dot(score_grad, block[:, :HEAD], 0, 0)
            key_grads[at_block] = key_grads[at_block] + dot(score_grad, queries)
            value_grads[at_block] = value_grads[at_block] + dot(
                probs[at_block].astype(low), context_grad
            )
        query_rot = query_rot * SCALE
        first, second = turn_back(query_rot[:, :half], query_rot[:, half:], cos, sin)
        upper = jnp.concatenate([first, second], axis=1)
        block = raw[:, at]
        scaling = inverse_rms(block)
        gain_sum = gain_sum + jnp.sum(upper * (block * scaling), 0, keepdims=True)
        query_grad[:, at] = rms_backward(block, scaling, upper * gain[0:1, :]).astype(low)
    gain_grad[...] = jnp.broadcast_to(gain_sum, (8, HEAD))
    far_grad[:, :HEAD] = (key_grads[0] * SCALE).astype(low)
    far_grad[:, HEAD:] = value_grads[0].astype(low)
    near_grad[:, :HEAD] = (key_grads[1] * SCALE).astype(low)
    near_grad[:, HEAD:] = value_grads[1].astype(low)
    own_grad[:, :HEAD] = key_grads[2] * SCALE
    own_grad[:, HEAD:] = value_grads[2]


def pair_back_body(query, own, near, far, raw, gain, cosine, sine, pair_grad, cut, gain_grad):
    half = HEAD // 2
    low = jnp.bfloat16
    total = own[...] + near[...].astype(jnp.float32) + far[...].astype(jnp.float32)
    first, second = turn_back(total[:, :half], total[:, half:HEAD], cosine[...], sine[...])
    upper = jnp.concatenate([first, second], axis=1)
    block = raw[:, HEADS * HEAD : (HEADS + 1) * HEAD]
    scaling = inverse_rms(block)
    gain_sum = jnp.sum(upper * (block * scaling), 0, keepdims=True)
    gain_grad[...] = jnp.broadcast_to(gain_sum, (8, HEAD))
    keys = rms_backward(block, scaling, upper * gain[1:2, :]).astype(low)
    values = total[:, HEAD:].astype(low)
    pair_grad[:, :HEAD] = keys
    pair_grad[:, HEAD:] = values
    size = cut.shape[2]
    cut[0] = query[:, :size]
    cut[1] = query[:, size : 2 * size]
    cut[2] = jnp.concatenate([query[:, 2 * size :], keys[:, :half]], axis=1)
    cut[3] = jnp.concatenate([keys[:, half:], values], axis=1)


def residual_body(
    context, out_weight, tokens, attention_gain, feed_gain, raw, state, feed_input
):
    value = dot(context[...], out_weight[...], 1, 1)
    raw[...] = value
    hidden = tokens[...].astype(jnp.float32) + value * inverse_rms(value) * attention_gain[...]
    state[...] = hidden
    feed_input[...] = (hidden * inverse_rms(hidden) * feed_gain[...]).astype(jnp.bfloat16)


def down_body(
    part, near, across, behind, state, cotangent, valid, gain, layer, down_grad, gain_grad
):
    wide = jnp.float32
    raw = (
        part[...].astype(wide)
        + near[...].astype(wide)
        + across[...].astype(wide)
        + behind[...].astype(wide)
    )
    scaling = inverse_rms(raw)
    hat = raw * scaling
    ok = valid[:, :1]
    layer[...] = (ok * (state[...] + hat * gain[...])).astype(jnp.bfloat16)
    upstream = cotangent[...].astype(wide) * ok
    gain_grad[...] = jnp.broadcast_to(
        jnp.sum(upstream * hat, 0, keepdims=True), (8, hat.shape[1])
    )
    down_grad[...] = rms_backward(raw, scaling, upstream * gain[...]).astype(jnp.bfloat16)


def state_body(
    part,
    near,
    across,
    behind,
    state,
    raw,
    cotangent,
    valid,
    feed_gain,
    attention_gain,
    attention_grad,
    state_grad,
    gain_grads,
):
    wide = jnp.float32
    feed_grad = (
        part[...].astype(wide)
        + near[...].astype(wide)
        + across[...].astype(wide)
        + behind[...].astype(wide)
    )
    hidden = state[...]
    scaling = inverse_rms(hidden)
    upstream = cotangent[...].astype(wide) * valid[:, :1]
    total = upstream + rms_backward(hidden, scaling, feed_grad * feed_gain[...])
    state_grad[...] = total
    value = raw[...]
    value_scaling = inverse_rms(value)
    width = value.shape[1]
    gain_grads[:8] = jnp.broadcast_to(
        jnp.sum(feed_grad * (hidden * scaling), 0, keepdims=True), (8, width)
    )
    gain_grads[8:] = jnp.broadcast_to(
        jnp.sum(total * (value * value_scaling), 0, keepdims=True), (8, width)
    )
    attention_grad[...] = rms_backward(value, value_scaling, total * attention_gain[...]).astype(
        jnp.bfloat16
    )


def input_body(
    query_grad, pair_grad, weight, tokens, state_grad, gain, tokens_grad, gain_grad
):
    queries = query_grad.shape[1]
    pairs = pair_grad.shape[1]
    grad = dot(query_grad[...], weight[:, :queries], 1, 1) + dot(
        pair_grad[...], weight[:, queries : queries + pairs], 1, 1
    )
    value = tokens[...].astype(jnp.float32)
    scaling = inverse_rms(value)
    gain_grad[...] = jnp.broadcast_to(
        jnp.sum(grad * (value * scaling), 0, keepdims=True), (8, value.shape[1])
    )
    tokens_grad[...] = (
        state_grad[...] + rms_backward(value, scaling, grad * gain[...])
    ).astype(jnp.bfloat16)


def feed_body(place, rows, weights, *refs):
    hidden_out, value_out, slope_out, part, total = refs[-5:]
    low = jnp.bfloat16
    total[...] = jnp.zeros_like(total)

    @pl.loop(0, FEED_SLICE // FEED_TILE)
    def _(tile):
        gate_at, up_at, down_at = (
            pl.ds(pl.multiple_of(start + tile * FEED_TILE, 128), FEED_TILE)
            for start in (0, FEED_SLICE, 2 * FEED_SLICE)
        )
        to = slice(place, place + rows.shape[0])
        gate_raw = dot(rows[...], weights[:, gate_at])
        up_raw = dot(rows[...], weights[:, up_at])
        value, slope = gelu_parts(gate_raw)
        hidden = (value * up_raw).astype(low)
        hidden_out[to, gate_at] = hidden
        value_out[to, gate_at] = value.astype(low)
        slope_out[to, gate_at] = (slope * up_raw).astype(low)
        total[...] += dot(hidden, weights[:, down_at], 1, 1)

    part[...] = total[...].astype(low)


def feed_back_body(place, rows, weights, value, slope, *refs):
    gate_out, up_out, part, total = refs[-4:]
    low = jnp.bfloat16
    total[...] = jnp.zeros_like(total)

    @pl.loop(0, FEED_SLICE // FEED_TILE)
    def _(tile):
        gate_at, up_at, down_at = (
            pl.ds(pl.multiple_of(start + tile * FEED_TILE, 128), FEED_TILE)
            for start in (0, FEED_SLICE, 2 * FEED_SLICE)
        )
        to = slice(place, place + rows.shape[0])
        hidden_grad = dot(rows[...], weights[:, down_at])
        gate_grad = (hidden_grad * slope[to, gate_at].astype(jnp.float32)).astype(low)
        up_grad = (hidden_grad * value[to, gate_at].astype(jnp.float32)).astype(low)
        gate_out[to, gate_at] = gate_grad
        up_out[to, gate_at] = up_grad
        total[...] += dot(gate_grad, weights[:, gate_at], 1, 1) + dot(
            up_grad, weights[:, up_at], 1, 1
        )

    part[...] = total[...].astype(low)


def feed_call(body, rows, weights, read, kept, place, outs, cost, name):
    count, width = rows.shape
    operands = [rows, weights, *read, *kept]
    whole = pl.BlockSpec(memory_space=pltpu.VMEM)
    first_kept = 2 + len(read)
    return pl.pallas_call(
        functools.partial(body, place),
        in_specs=[whole] * first_kept + [pl.BlockSpec(memory_space=pl.ANY)] * len(kept),
        out_specs=[whole] * (outs + 1),
        out_shape=[jax.ShapeDtypeStruct((4 * ROWS, FEED_SLICE), jnp.bfloat16)] * outs
        + [jax.ShapeDtypeStruct((count, width), jnp.bfloat16)],
        scratch_shapes=[pltpu.VMEM((count, width), jnp.float32)],
        input_output_aliases={first_kept + i: i for i in range(len(kept))},
        compiler_params=pltpu.CompilerParams(vmem_limit_bytes=VMEM),
        cost_estimate=pl.CostEstimate(flops=cost, bytes_accessed=1000, transcendentals=0),
        name=name,
    )(*operands)


def product_body(core, left, right, *refs):
    away, here, total = refs[-3:]
    rows = left.shape[1] // 16
    width = right.shape[1]

    def split(to, first, columns):
        for two in range(4):
            pieces = [
                total[pl.ds(pl.multiple_of((4 * two + 2 * i + first) * rows, 8), rows), :columns]
                for i in (0, 1)
            ]
            yield slice(two * 2 * rows, (two + 1) * 2 * rows), jnp.concatenate(pieces, axis=0)

    for start in range(0, width, total.shape[1]):
        size = min(total.shape[1], width - start)
        at = slice(start, start + size)
        total[:, :size] = dot(left[...], right[:, at], 0, 0)
        for to, first in ((away, 1 - core[0]), (here, core[0])):
            for place, value in split(to, first, size):
                to[place, at] = value.astype(to.dtype)
    if len(refs) > 3:
        extra = refs[0]
        at = slice(width, width + extra.shape[1])
        total[:, : extra.shape[1]] = extra[...]
        for to, first in ((away, 1 - core[0]), (here, core[0])):
            for place, value in split(to, first, extra.shape[1]):
                to[place, at] = value.astype(to.dtype)


def product(core, left, right, *extra):
    width = right.shape[1] + sum(block.shape[1] for block in extra)
    out = jax.ShapeDtypeStruct((left.shape[1] // 2, width), jnp.bfloat16)
    whole = pl.BlockSpec(memory_space=pltpu.VMEM)
    away, here = pl.pallas_call(
        product_body,
        in_specs=[pl.BlockSpec(memory_space=pltpu.SMEM)] + [whole] * (2 + len(extra)),
        out_specs=[whole, whole],
        out_shape=[out, out],
        scratch_shapes=[pltpu.VMEM((left.shape[1], 512), jnp.float32)],
        compiler_params=pltpu.CompilerParams(vmem_limit_bytes=VMEM),
        cost_estimate=SMALL,
        name="product",
    )(core, left, right, *extra)
    return here, give(away, "core", 1)


def added(halves):
    here, got = halves
    return (here.astype(jnp.float32) + got.astype(jnp.float32)).astype(jnp.bfloat16)


def spread_in_body(gate, gate_got, up, up_got, down, down_got, spread):
    rows = spread.shape[1]
    half = FEED_SLICE // 2
    for two in range(4):
        at = slice(two * 2 * rows, (two + 1) * 2 * rows)
        gates, ups, downs = (
            here[at].astype(jnp.float32) + got[at].astype(jnp.float32)
            for here, got in ((gate, gate_got), (up, up_got), (down, down_got))
        )
        for block in range(2):
            of = slice(block * rows, (block + 1) * rows)
            to = 4 * two + 2 * block
            spread[to, :, :FEED_SLICE] = gates[of].astype(spread.dtype)
            spread[to, :, FEED_SLICE:] = downs[of, :half].astype(spread.dtype)
            spread[to + 1, :, :FEED_SLICE] = ups[of].astype(spread.dtype)
            spread[to + 1, :, FEED_SLICE:] = downs[of, half:].astype(spread.dtype)


def spread_out_body(sums, gate, up, down):
    width = gate.shape[1]
    half = FEED_SLICE // 2
    for y in range(4):
        start = y * FEED_SLICE
        size = min(FEED_SLICE, width - start)
        gate[:, start : start + size] = sums[y, :, :size].astype(jnp.float32)
        up[:, start : start + size] = sums[4 + y, :, :size].astype(jnp.float32)
        for xl in range(2):
            first = start + xl * half
            size = min(half, width - first)
            down[:, first : first + size] = sums[
                4 * xl + y, :, FEED_SLICE : FEED_SLICE + size
            ].astype(jnp.float32)


def feed_slice(weight):
    y = lax.axis_index("y")
    padded = jnp.pad(weight, ((0, 0), (0, 4 * FEED_SLICE - weight.shape[1])))
    return lax.dynamic_slice_in_dim(padded, y * FEED_SLICE, FEED_SLICE, 1)


def local(
    tokens,
    cotangent,
    lengths,
    query_weight,
    key_weight,
    value_weight,
    out_weight,
    gate_weight,
    up_weight,
    down_weight,
    input_gain,
    query_gain,
    key_gain,
    attention_gain,
    feedforward_gain,
    output_gain,
):
    low = jnp.bfloat16
    wide = jnp.float32
    row_count, model_width = tokens.shape
    head_size = key_weight.shape[1]
    head_count = query_weight.shape[1] // head_size
    query_width = head_count * head_size
    qkv_width = query_width + 2 * head_size
    feed_width = gate_weight.shape[1]
    gain_shard = input_gain.shape[0]
    head_shard = query_gain.shape[0]
    y = lax.axis_index("y")
    seq_index = lax.axis_index("xl") * 4 + y
    place = seq_index.reshape(1).astype(jnp.int32)
    core = lax.axis_index("core").reshape(1).astype(jnp.int32)
    positions = seq_index * row_count + lax.iota(jnp.int32, row_count)
    valid = jnp.broadcast_to((positions < lengths[0]).astype(wide)[:, None], (row_count, 128))
    cosine, sine = rotary_tables(positions, head_size)

    def spread(vector):
        return jnp.pad(vector, (0, gain_shard - head_shard))

    gain_columns = jnp.stack(
        [
            input_gain,
            attention_gain,
            feedforward_gain,
            output_gain,
            spread(query_gain),
            spread(key_gain),
        ],
        axis=1,
    )
    gain_columns = jnp.pad(gain_columns, ((0, 0), (0, 122)))
    feed_weights = lax.all_gather(
        jnp.concatenate(
            [feed_slice(gate_weight), feed_slice(up_weight), feed_slice(down_weight)], axis=1
        ),
        DP,
        axis=0,
        tiled=True,
    )
    pairs, beside = with_other_x(
        jnp.concatenate([query_weight, key_weight, value_weight, gain_columns, out_weight], axis=1)
    )
    qkv_columns = qkv_width + gain_columns.shape[1]
    full_qkv, arrived = gather_rows(pairs[:, :, :qkv_columns])
    tokens_ring = [take(ordered(tokens, beside), "y", by) for by in (1, 2, 3)]
    gains = 1.0 + full_qkv[:, qkv_width : qkv_width + 8].astype(wide).T
    one_input, one_attention, one_feed, one_output = (gains[i : i + 1] for i in range(4))
    head_gain = gains.reshape(8, 16, gain_shard)[4:6, :, :head_shard].reshape(2, head_size)
    head_gain = jnp.pad(head_gain, ((0, 6), (0, 0)))

    def attention_input_of(rows):
        values = rows.astype(wide)
        return (values * inverse_rms(values) * one_input).astype(low)

    attention_input = attention_input_of(tokens)
    qkv_raw = jnp.dot(attention_input, full_qkv[:, :qkv_width], preferred_element_type=wide)
    prepare = rows_call(
        prepare_body,
        [((row_count, query_width), low), ((row_count, 2 * head_size), low)],
        "prepare",
    )
    query_low, local_pair = prepare(qkv_raw, head_gain, cosine, sine)
    near_pair, far_pair = (from_behind(local_pair, distance) for distance in (1, 2))
    full_out, _ = gather_rows(ordered(pairs[:, :, qkv_columns:], *arrived), (local_pair,))
    input_ring = attention_input_of(jnp.concatenate([tokens] + tokens_ring, axis=0))
    near_pair, far_pair, input_ring = lax.optimization_barrier((near_pair, far_pair, input_ring))
    attend = rows_call(
        attend_body,
        [((row_count, query_width), low), ((8, row_count), wide)],
        "attend",
    )
    context_low, log_total = attend(place, query_low, far_pair, near_pair, local_pair)
    residual = rows_call(
        residual_body,
        [
            ((row_count, model_width), wide),
            ((row_count, model_width), wide),
            ((row_count, model_width), low),
        ],
        "residual",
    )
    attention_raw, state, feed_input = residual(
        context_low, full_out, tokens, one_attention, one_feed
    )

    weights, feed_input = lax.optimization_barrier((feed_weights, feed_input))

    def exchange(rows, run):
        two, one, three = (take(rows, "y", by) for by in (2, 1, 3))
        kept, two_part = run(two, [], 3 * row_count, 1000)
        across = give(two_part, "y", 2)
        both = jnp.concatenate([one, three], axis=0)
        kept, both_part = run(both, kept, 0, LONG)
        from_one = give(both_part[:row_count], "y", 1)
        from_three = give(both_part[row_count:], "y", 3)
        *kept, across, both = lax.optimization_barrier((*kept, across, both))
        kept, own_part = run(rows, kept, 2 * row_count, LONG)
        ring = jnp.concatenate([ordered(both, own_part, from_one, from_three), rows, two], axis=0)
        return kept, [own_part, from_one, across, from_three], ring

    def forward(rows, kept, at, cost):
        *kept, part = feed_call(feed_body, rows, weights, [], kept, at, 3, cost, "feed")
        return kept, part

    kept, terms, feed_ring = exchange(feed_input, forward)
    hidden, value, slope = kept
    finish = rows_call(
        down_body,
        [
            ((row_count, model_width), low),
            ((row_count, model_width), low),
            ((8, model_width), wide),
        ],
        "finish",
    )
    layer_output, down_grad, output_gain_rows = finish(
        *terms, state, cotangent, valid, one_output
    )

    def backward(rows, kept, at, cost):
        *kept, part = feed_call(
            feed_back_body, rows, weights, [value, slope], kept, at, 2, cost, "feed_back"
        )
        return kept, part

    rows72 = gain_shard
    (gate_grad, up_grad), terms, down_ring = exchange(down_grad, backward)
    halves = [
        half
        for left, right in ((feed_ring, gate_grad), (feed_ring, up_grad), (down_ring, hidden))
        for half in product(core, left, right)
    ]
    (spread_in,) = rows_call(
        spread_in_body, [((16, rows72, FEED_SLICE * 3 // 2), low)], "spread_in"
    )(*halves)
    feed_sum = lax.psum_scatter(spread_in, ("z", "xh", "xl"), scatter_dimension=0, tiled=False)
    back = rows_call(
        state_body,
        [
            ((row_count, model_width), low),
            ((row_count, model_width), wide),
            ((16, model_width), wide),
        ],
        "state_back",
    )
    attention_grad, state_grad, state_gain_rows = back(
        *terms, state, attention_raw, cotangent, valid, one_feed, one_attention
    )

    attend_back = rows_call(
        attend_back_body,
        [
            ((row_count, 2 * head_size), low),
            ((row_count, 2 * head_size), low),
            ((row_count, 2 * head_size), wide),
            ((row_count, query_width), low),
            ((8, head_size), wide),
        ],
        "attend_back",
    )
    far_grad, near_grad, own_grad, query_grad, query_gain_rows = attend_back(
        place,
        attention_grad,
        full_out,
        query_low,
        far_pair,
        near_pair,
        local_pair,
        log_total,
        qkv_raw,
        head_gain,
        cosine,
        sine,
    )
    near_back = from_behind(near_grad, -1)
    far_back = from_behind(far_grad, -2)
    out_chip = added(product(core, ordered(attention_grad, near_grad), context_low))
    out_cut = out_chip.reshape(model_width // 2, 4, query_width // 4)
    out_sum = pick(out_cut, y, 1).astype(wide)
    for by in (1, 3, 2):
        out_sum = out_sum + give(pick(out_cut, (y + by) % 4, 1), "y", by).astype(wide)
    pair_back = rows_call(
        pair_back_body,
        [
            ((row_count, 2 * head_size), low),
            ((4, row_count, qkv_width // 4), low),
            ((8, head_size), wide),
        ],
        "pair_back",
    )
    pair_grad, qkv_cut, key_gain_rows = pair_back(
        query_grad, own_grad, near_back, far_back, qkv_raw, head_gain, cosine, sine
    )
    qkv_pieces = [give(pick(qkv_cut, (y + by) % 4, 0), "y", by) for by in (3, 2, 1)]
    qkv_ring = jnp.concatenate([pick(qkv_cut, y, 0)] + qkv_pieces, axis=0)
    input_back = rows_call(
        input_body,
        [((row_count, model_width), low), ((8, model_width), wide)],
        "input_back",
    )
    tokens_grad, input_gain_rows = input_back(
        query_grad, pair_grad, full_qkv, tokens, state_grad, one_input
    )

    def spread_head(vector):
        return jnp.pad(
            vector.reshape(16, head_shard), ((0, 0), (0, gain_shard - head_shard))
        ).reshape(model_width)

    gain_block = jnp.stack(
        [
            input_gain_rows[0],
            state_gain_rows[8],
            state_gain_rows[0],
            output_gain_rows[0],
            spread_head(query_gain_rows[0]),
            spread_head(key_gain_rows[0]),
        ],
        axis=1,
    )
    gain_block = jnp.pad(gain_block, ((0, 0), (0, 122)))
    chip = jnp.concatenate(
        [added(product(core, input_ring, qkv_ring, gain_block)), out_sum.astype(low)], axis=1
    )
    attention_sum, attention_column = small_sum(chip.reshape(4, 2, rows72, chip.shape[1]))
    attention_blocks = in_order(
        [attention_sum] + [take(attention_sum, "y", by) for by in (1, 2, 3)]
    )
    feed_sums = lax.all_gather(ordered(feed_sum, attention_column), SEQ, axis=0, tiled=False)
    gate_weight_grad, up_weight_grad, down_weight_grad = rows_call(
        spread_out_body, [((rows72, feed_width), wide)] * 3, "spread_out"
    )(feed_sums)
    qkv_cols = qkv_width // 4
    out_cols = query_width // 4
    qkv_weight_grad = jnp.concatenate([b[:, :qkv_cols] for b in attention_blocks], axis=1)
    out_weight_grad = jnp.concatenate([b[:, qkv_cols + 128 :] for b in attention_blocks], axis=1)
    gain_sum = sum(b[:, qkv_cols : qkv_cols + 128].astype(wide) for b in attention_blocks)
    return (
        layer_output,
        tokens_grad,
        qkv_weight_grad[:, :query_width].astype(wide),
        qkv_weight_grad[:, query_width : query_width + head_size].astype(wide),
        qkv_weight_grad[:, query_width + head_size :].astype(wide),
        out_weight_grad.astype(wide),
        gate_weight_grad,
        up_weight_grad,
        down_weight_grad,
        gain_sum[:, 0],
        gain_sum[:head_shard, 4],
        gain_sum[:head_shard, 5],
        gain_sum[:, 1],
        gain_sum[:, 2],
        gain_sum[:, 3],
    )


def solution(mesh):
    fine = Mesh(mesh.devices.reshape(SIZES), AXES)
    rows = P(AXES, None)
    matrix = P(DP, None)
    vector = P(DP)
    return jax.shard_map(
        local,
        mesh=fine,
        in_specs=(rows, rows, vector) + (matrix,) * 7 + (vector,) * 6,
        out_specs=(rows, rows) + (matrix,) * 7 + (vector,) * 6,
        check_vma=False,
    )
```

```python
import functools
import math

import jax
import jax.numpy as jnp
from jax import lax
from jax.experimental import pallas as pl
from jax.experimental.pallas import tpu as pltpu
from jax.sharding import Mesh
from jax.sharding import PartitionSpec as P

EPSILON = 1e-06
GELU_COEFF = 0.044715
AXES = ("z", "xh", "core", "xl", "y")
SIZES = (4, 2, 2, 2, 4)
DP = ("z", "xh", "core")
SEQ = ("xl", "y")
FEED_SLICE = 1792
FEED_TILES = ((0, 1024), (1024, 768))
HEADS = 4
HEAD = 256
SCALE = HEAD**-0.5
ROWS = 256
VMEM = 16 * 1024 * 1024
LONG = 12 * 10**9
SMALL = pl.CostEstimate(flops=1000, bytes_accessed=1000, transcendentals=0)


def from_behind(array, by):
    pairs = [(i, i + by) for i in range(8) if 0 <= i + by < 8]
    return lax.ppermute(array, SEQ, pairs)


def take(array, axis, by):
    count = lax.axis_size(axis)
    return lax.ppermute(array, axis, [((i + by) % count, i) for i in range(count)])


def give(array, axis, by):
    count = lax.axis_size(axis)
    return lax.ppermute(array, axis, [(i, (i + by) % count) for i in range(count)])


def swap_x(array):
    return lax.ppermute(array, ("xh", "xl"), [(0, 3), (3, 0), (1, 2), (2, 1)])


def ordered(value, *after):
    return lax.optimization_barrier((value,) + after)[0]


def pick(array, index, axis):
    return lax.dynamic_index_in_dim(array, index, axis, keepdims=False)


def with_other_x(block, beside):
    xh = lax.axis_index("xh")
    return jnp.where(xh == 0, jnp.stack([block, beside]), jnp.stack([beside, block]))


def gather_rows(pair, wait=()):
    _, rows, width = pair.shape
    z = lax.axis_index("z")
    core = lax.axis_index("core")
    ring = [(take(pair, "z", by), by) for by in (1, 3, 2)]
    arrived = [piece for piece, _ in ring]
    own = jnp.zeros((4, 2, rows, width), pair.dtype)
    own = lax.dynamic_update_slice_in_dim(own, pair[None], z, 0)
    own = ordered(own, *wait)
    for piece, by in ring:
        own = lax.dynamic_update_slice_in_dim(own, piece[None], (z + by) % 4, 0)
    other = give(own, "core", 1)
    both = jnp.where(
        core == 0, jnp.stack([own, other], axis=2), jnp.stack([other, own], axis=2)
    )
    return both.reshape(16 * rows, width), arrived


def in_order(blocks):
    y = lax.axis_index("y")
    placed = []
    for place in range(4):
        value = blocks[(place - 3) % 4]
        for at in range(3):
            value = jnp.where(y == at, blocks[(place - at) % 4], value)
        placed.append(value)
    return placed


def inverse_rms(values):
    return lax.rsqrt(jnp.mean(values * values, axis=-1, keepdims=True) + EPSILON)


def rms_backward(values, scaling, upstream):
    inner = jnp.mean(upstream * values, axis=-1, keepdims=True)
    return scaling * (upstream - values * (scaling * scaling) * inner)


def rotary_tables(positions, head_size):
    half_size = head_size // 2
    exponents = lax.iota(jnp.float32, half_size) * (2.0 / head_size)
    frequency = jnp.power(10000.0, -exponents)
    angles = positions.astype(jnp.float32)[:, None] * frequency[None, :]
    return (jnp.cos(angles), jnp.sin(angles))


def gelu_parts(values):
    root_coeff = math.sqrt(2.0 / math.pi)
    square = values * values
    bend = jnp.tanh(values * (root_coeff + (root_coeff * GELU_COEFF) * square))
    part = 0.5 + 0.5 * bend
    gelu_value = values * part
    inner = root_coeff + (3.0 * GELU_COEFF * root_coeff) * square
    gelu_slope = part + gelu_value * (1.0 - bend) * inner
    return (gelu_value, gelu_slope)


def dot(left, right, left_axis=1, right_axis=0):
    return lax.dot_general(
        left,
        right,
        (((left_axis,), (right_axis,)), ((), ())),
        preferred_element_type=jnp.float32,
    )


def turn(first, second, cosine, sine):
    return first * cosine - second * sine, second * cosine + first * sine


def turn_back(first, second, cosine, sine):
    return first * cosine + second * sine, second * cosine - first * sine


def rows_call(body, outs, name):
    def call(*operands):
        specs = [
            pl.BlockSpec(memory_space=pltpu.SMEM)
            if operand.dtype == jnp.int32
            else pl.BlockSpec(memory_space=pltpu.VMEM)
            for operand in operands
        ]
        return pl.pallas_call(
            body,
            out_shape=[jax.ShapeDtypeStruct(shape, dtype) for shape, dtype in outs],
            in_specs=specs,
            out_specs=[pl.BlockSpec(memory_space=pltpu.VMEM) for _ in outs],
            compiler_params=pltpu.CompilerParams(vmem_limit_bytes=VMEM),
            cost_estimate=SMALL,
            name=name,
        )(*operands)

    return call


def blocks_call(body, outs, name, vmem=VMEM):
    steps = 4

    def spec(shape):
        if shape[0] < ROWS:
            return pl.BlockSpec(shape, lambda i: (0, 0))
        return pl.BlockSpec((shape[0] // steps, shape[1]), lambda i: (i, 0))

    def call(*operands):
        return pl.pallas_call(
            body,
            grid=(steps,),
            out_shape=[jax.ShapeDtypeStruct(shape, dtype) for shape, dtype in outs],
            in_specs=[spec(operand.shape) for operand in operands],
            out_specs=[spec(shape) for shape, _ in outs],
            compiler_params=pltpu.CompilerParams(vmem_limit_bytes=vmem),
            cost_estimate=SMALL,
            name=name,
        )(*operands)

    return call


def prepare_body(raw, gain, cosine, sine, query, pair):
    cos, sin = cosine[...], sine[...]
    half = HEAD // 2

    def finish(block, gains):
        hat = block * inverse_rms(block) * gains
        first, second = turn(hat[:, :half], hat[:, half:], cos, sin)
        return jnp.concatenate([first, second], axis=1).astype(jnp.bfloat16)

    for head in range(HEADS):
        at = slice(head * HEAD, (head + 1) * HEAD)
        query[:, at] = finish(raw[:, at], gain[0:1, :])
    keys = HEADS * HEAD
    pair[:, :HEAD] = finish(raw[:, keys : keys + HEAD], gain[1:2, :])
    pair[:, HEAD:] = raw[:, keys + HEAD : keys + 2 * HEAD].astype(jnp.bfloat16)


def attend_body(place, query, far, near, own, context, log_total):
    row = lax.broadcasted_iota(jnp.int32, (ROWS, ROWS), 0)
    column = lax.broadcasted_iota(jnp.int32, (ROWS, ROWS), 1)
    seq = place[0]
    allowed = (
        (row < column) & (seq >= 2),
        jnp.full((ROWS, ROWS), seq >= 1),
        column <= row,
    )
    blocks = (far, near, own)
    lane = lax.broadcasted_iota(jnp.int32, (ROWS, 128), 1)
    logs = jnp.zeros((ROWS, 128), jnp.float32)
    for head in range(HEADS):
        at = slice(head * HEAD, (head + 1) * HEAD)
        scores = [
            jnp.where(ok, dot(query[:, at], block[:, :HEAD], 1, 1) * SCALE, -1e30)
            for ok, block in zip(allowed, blocks)
        ]
        top = jnp.max(jnp.maximum(jnp.maximum(scores[0], scores[1]), scores[2]), 1, keepdims=True)
        terms = [jnp.exp(score - top) for score in scores]
        total = jnp.sum(terms[0] + terms[1] + terms[2], 1, keepdims=True)
        share = 1.0 / total
        out = sum(
            dot((term * share).astype(jnp.bfloat16), block[:, HEAD:])
            for term, block in zip(terms, blocks)
        )
        context[:, at] = out.astype(jnp.bfloat16)
        logs = jnp.where(lane == head, top + jnp.log(total), logs)
    log_total[...] = logs.T[:8]


def attend_back_body(
    place,
    upstream,
    out_weight,
    query,
    far,
    near,
    own,
    log_total,
    raw,
    gain,
    cosine,
    sine,
    far_grad,
    near_grad,
    own_grad,
    query_grad,
    gain_grad,
):
    low = jnp.bfloat16
    half = HEAD // 2
    key_at = lax.broadcasted_iota(jnp.int32, (ROWS, ROWS), 0)
    query_at = lax.broadcasted_iota(jnp.int32, (ROWS, ROWS), 1)
    seq = place[0]
    allowed = (
        (query_at < key_at) & (seq >= 2),
        jnp.full((ROWS, ROWS), seq >= 1),
        key_at <= query_at,
    )
    blocks = (far, near, own)
    cos, sin = cosine[...], sine[...]
    key_grads = [0.0, 0.0, 0.0]
    value_grads = [0.0, 0.0, 0.0]
    gain_sum = jnp.zeros((1, HEAD), jnp.float32)
    for head in range(HEADS):
        at = slice(head * HEAD, (head + 1) * HEAD)
        context_grad = dot(upstream[...], out_weight[:, at]).astype(low)
        queries = query[:, at]
        logs = log_total[head : head + 1, :]
        probs = [
            jnp.where(ok, jnp.exp(dot(block[:, :HEAD], queries, 1, 1) * SCALE - logs), 0.0)
            for ok, block in zip(allowed, blocks)
        ]
        prob_grads = [dot(block[:, HEAD:], context_grad, 1, 1) for block in blocks]
        inner = jnp.sum(
            probs[0] * prob_grads[0] + probs[1] * prob_grads[1] + probs[2] * prob_grads[2],
            0,
            keepdims=True,
        )
        query_rot = 0.0
        for at_block, block in enumerate(blocks):
            score_grad = (probs[at_block] * (prob_grads[at_block] - inner)).astype(low)
            query_rot = query_rot + dot(score_grad, block[:, :HEAD], 0, 0)
            key_grads[at_block] = key_grads[at_block] + dot(score_grad, queries)
            value_grads[at_block] = value_grads[at_block] + dot(
                probs[at_block].astype(low), context_grad
            )
        query_rot = query_rot * SCALE
        first, second = turn_back(query_rot[:, :half], query_rot[:, half:], cos, sin)
        upper = jnp.concatenate([first, second], axis=1)
        block = raw[:, at]
        scaling = inverse_rms(block)
        gain_sum = gain_sum + jnp.sum(upper * (block * scaling), 0, keepdims=True)
        query_grad[:, at] = rms_backward(block, scaling, upper * gain[0:1, :]).astype(low)
    gain_grad[...] = jnp.broadcast_to(gain_sum, (8, HEAD))
    far_grad[:, :HEAD] = (key_grads[0] * SCALE).astype(low)
    far_grad[:, HEAD:] = value_grads[0].astype(low)
    near_grad[:, :HEAD] = (key_grads[1] * SCALE).astype(low)
    near_grad[:, HEAD:] = value_grads[1].astype(low)
    own_grad[:, :HEAD] = key_grads[2] * SCALE
    own_grad[:, HEAD:] = value_grads[2]


def pair_back_body(
    query, own, near, far, raw, gain, cosine, sine, out, out_got, pair_grad, cut, gain_grad
):
    half = HEAD // 2
    low = jnp.bfloat16
    total = own[...] + near[...].astype(jnp.float32) + far[...].astype(jnp.float32)
    first, second = turn_back(total[:, :half], total[:, half:HEAD], cosine[...], sine[...])
    upper = jnp.concatenate([first, second], axis=1)
    block = raw[:, HEADS * HEAD : (HEADS + 1) * HEAD]
    scaling = inverse_rms(block)
    gain_sum = jnp.sum(upper * (block * scaling), 0, keepdims=True)
    gain_grad[...] = jnp.broadcast_to(gain_sum, (8, HEAD))
    keys = rms_backward(block, scaling, upper * gain[1:2, :]).astype(low)
    values = total[:, HEAD:].astype(low)
    pair_grad[:, :HEAD] = keys
    pair_grad[:, HEAD:] = values
    size = cut.shape[2]
    cut[0, :ROWS] = query[:, :size]
    cut[1, :ROWS] = query[:, size : 2 * size]
    cut[2, :ROWS] = jnp.concatenate([query[:, 2 * size :], keys[:, :half]], axis=1)
    cut[3, :ROWS] = jnp.concatenate([keys[:, half:], values], axis=1)
    for part in range(4):
        at = slice(part * HEAD, (part + 1) * HEAD)
        term = (out[:, at].astype(jnp.float32) + out_got[:, at].astype(jnp.float32)).astype(low)
        cut[part, ROWS:, :HEAD] = term[:384]
        cut[part, ROWS : ROWS + 192, HEAD:] = term[384:, :half]
        cut[part, ROWS + 192 :, HEAD:] = term[384:, half:]


def arrive_body(own, one, two, three, ring, out):
    wide = jnp.float32
    half = HEAD // 2
    for at, block in enumerate((own, one, two, three)):
        ring[at * ROWS : (at + 1) * ROWS] = block[:ROWS]
    total = sum(block[ROWS:].astype(wide) for block in (own, one, two, three)).astype(out.dtype)
    out[:384] = total[:, :HEAD]
    out[384:, :half] = total[:192, HEAD:]
    out[384:, half:] = total[192:, HEAD:]


def chip_body(offsets, here, got, out, *refs):
    *parts, total = refs
    wide = jnp.float32
    columns = here.shape[1]
    rows = parts[0].shape[1]
    total[:, :columns] = here[...].astype(wide) + got[...].astype(wide)
    total[:, columns:] = out[...].astype(wide)
    for at, part in enumerate(parts):
        for block in range(2):
            start = pl.multiple_of(offsets[2 * at + block], 8)
            part[block] = total[pl.ds(start, rows), :].astype(part.dtype)


def residual_body(
    context, out_weight, tokens, attention_gain, feed_gain, raw, state, feed_input
):
    value = dot(context[...], out_weight[...], 1, 1)
    raw[...] = value
    hidden = tokens[...].astype(jnp.float32) + value * inverse_rms(value) * attention_gain[...]
    state[...] = hidden
    feed_input[...] = (hidden * inverse_rms(hidden) * feed_gain[...]).astype(jnp.bfloat16)


def down_body(
    part, near, across, behind, state, cotangent, valid, gain, layer, down_grad, gain_grad
):
    wide = jnp.float32
    raw = (
        part[...].astype(wide)
        + near[...].astype(wide)
        + across[...].astype(wide)
        + behind[...].astype(wide)
    )
    scaling = inverse_rms(raw)
    hat = raw * scaling
    ok = valid[:, :1]
    layer[...] = (ok * (state[...] + hat * gain[...])).astype(jnp.bfloat16)
    upstream = cotangent[...].astype(wide) * ok

    @pl.when(pl.program_id(0) == 0)
    def _():
        gain_grad[...] = jnp.zeros_like(gain_grad)

    gain_grad[...] += jnp.broadcast_to(
        jnp.sum(upstream * hat, 0, keepdims=True), (8, hat.shape[1])
    )
    down_grad[...] = rms_backward(raw, scaling, upstream * gain[...]).astype(jnp.bfloat16)


def state_body(
    part,
    near,
    across,
    behind,
    state,
    raw,
    cotangent,
    valid,
    feed_gain,
    attention_gain,
    attention_grad,
    state_grad,
    gain_grads,
):
    wide = jnp.float32
    feed_grad = (
        part[...].astype(wide)
        + near[...].astype(wide)
        + across[...].astype(wide)
        + behind[...].astype(wide)
    )
    hidden = state[...]
    scaling = inverse_rms(hidden)
    upstream = cotangent[...].astype(wide) * valid[:, :1]
    total = upstream + rms_backward(hidden, scaling, feed_grad * feed_gain[...])
    state_grad[...] = total
    value = raw[...]
    value_scaling = inverse_rms(value)
    width = value.shape[1]

    @pl.when(pl.program_id(0) == 0)
    def _():
        gain_grads[...] = jnp.zeros_like(gain_grads)

    gain_grads[:8] += jnp.broadcast_to(
        jnp.sum(feed_grad * (hidden * scaling), 0, keepdims=True), (8, width)
    )
    gain_grads[8:] += jnp.broadcast_to(
        jnp.sum(total * (value * value_scaling), 0, keepdims=True), (8, width)
    )
    attention_grad[...] = rms_backward(value, value_scaling, total * attention_gain[...]).astype(
        jnp.bfloat16
    )


def input_body(
    query_grad, pair_grad, weight, tokens, state_grad, gain, tokens_grad, gain_grad
):
    queries = query_grad.shape[1]
    pairs = pair_grad.shape[1]
    grad = dot(query_grad[...], weight[:, :queries], 1, 1) + dot(
        pair_grad[...], weight[:, queries : queries + pairs], 1, 1
    )
    value = tokens[...].astype(jnp.float32)
    scaling = inverse_rms(value)
    gain_grad[...] = jnp.broadcast_to(
        jnp.sum(grad * (value * scaling), 0, keepdims=True), (8, value.shape[1])
    )
    tokens_grad[...] = (
        state_grad[...] + rms_backward(value, scaling, grad * gain[...])
    ).astype(jnp.bfloat16)


def feed_body(place, rows, weights, *refs):
    hidden_out, value_out, slope_out, part, total = refs[-5:]
    low = jnp.bfloat16
    for first, size in FEED_TILES:
        gate_at, up_at, down_at = (
            slice(start + first, start + first + size) for start in (0, FEED_SLICE, 2 * FEED_SLICE)
        )
        to = slice(place, place + rows.shape[0])
        gate_raw = dot(rows[...], weights[:, gate_at])
        up_raw = dot(rows[...], weights[:, up_at])
        value, slope = gelu_parts(gate_raw)
        hidden = (value * up_raw).astype(low)
        hidden_out[to, gate_at] = hidden
        value_out[to, gate_at] = value.astype(low)
        slope_out[to, gate_at] = (slope * up_raw).astype(low)
        term = dot(hidden, weights[:, down_at], 1, 1)
        total[...] = term if first == 0 else total[...] + term

    part[...] = total[...].astype(low)


def feed_back_body(place, rows, weights, value, slope, *refs):
    gate_out, up_out, part, total = refs[-4:]
    low = jnp.bfloat16
    for first, size in FEED_TILES:
        gate_at, up_at, down_at = (
            slice(start + first, start + first + size) for start in (0, FEED_SLICE, 2 * FEED_SLICE)
        )
        to = slice(place, place + rows.shape[0])
        hidden_grad = dot(rows[...], weights[:, down_at])
        gate_grad = (hidden_grad * slope[to, gate_at].astype(jnp.float32)).astype(low)
        up_grad = (hidden_grad * value[to, gate_at].astype(jnp.float32)).astype(low)
        gate_out[to, gate_at] = gate_grad
        up_out[to, gate_at] = up_grad
        term = dot(gate_grad, weights[:, gate_at], 1, 1) + dot(up_grad, weights[:, up_at], 1, 1)
        total[...] = term if first == 0 else total[...] + term

    part[...] = total[...].astype(low)


def feed_call(body, rows, weights, read, kept, place, outs, cost, name, unread=()):
    count, width = rows.shape
    operands = [rows, weights, *read, *kept, *unread]
    whole = pl.BlockSpec(memory_space=pltpu.VMEM)
    first_kept = 2 + len(read)
    return pl.pallas_call(
        functools.partial(body, place),
        in_specs=[whole] * first_kept
        + [pl.BlockSpec(memory_space=pl.ANY)] * (len(kept) + len(unread)),
        out_specs=[whole] * (outs + 1),
        out_shape=[jax.ShapeDtypeStruct((4 * ROWS, FEED_SLICE), jnp.bfloat16)] * outs
        + [jax.ShapeDtypeStruct((count, width), jnp.bfloat16)],
        scratch_shapes=[pltpu.VMEM((count, width), jnp.float32)],
        input_output_aliases={first_kept + i: i for i in range(len(kept))},
        compiler_params=pltpu.CompilerParams(vmem_limit_bytes=VMEM),
        cost_estimate=pl.CostEstimate(flops=cost, bytes_accessed=1000, transcendentals=0),
        name=name,
    )(*operands)


def product_body(core, left, right, *refs):
    away, here, total = refs[-3:]
    rows = left.shape[1] // 16
    width = right.shape[1]

    def split(to, first, columns):
        for two in range(4):
            pieces = [
                total[pl.ds(pl.multiple_of((4 * two + 2 * i + first) * rows, 8), rows), :columns]
                for i in (0, 1)
            ]
            yield slice(two * 2 * rows, (two + 1) * 2 * rows), jnp.concatenate(pieces, axis=0)

    for start in range(0, width, total.shape[1]):
        size = min(total.shape[1], width - start)
        at = slice(start, start + size)
        total[:, :size] = dot(left[...], right[:, at], 0, 0)
        for to, first in ((away, 1 - core[0]), (here, core[0])):
            for place, value in split(to, first, size):
                to[place, at] = value.astype(to.dtype)
    if len(refs) > 3:
        extra = refs[0]
        at = slice(width, width + extra.shape[1])
        total[:, : extra.shape[1]] = extra[...]
        for to, first in ((away, 1 - core[0]), (here, core[0])):
            for place, value in split(to, first, extra.shape[1]):
                to[place, at] = value.astype(to.dtype)


def product(core, left, right, *extra, cost=1000):
    width = right.shape[1] + sum(block.shape[1] for block in extra)
    out = jax.ShapeDtypeStruct((left.shape[1] // 2, width), jnp.bfloat16)
    whole = pl.BlockSpec(memory_space=pltpu.VMEM)
    away, here = pl.pallas_call(
        product_body,
        in_specs=[pl.BlockSpec(memory_space=pltpu.SMEM)] + [whole] * (2 + len(extra)),
        out_specs=[whole, whole],
        out_shape=[out, out],
        scratch_shapes=[pltpu.VMEM((left.shape[1], 512), jnp.float32)],
        compiler_params=pltpu.CompilerParams(vmem_limit_bytes=VMEM),
        cost_estimate=pl.CostEstimate(flops=cost, bytes_accessed=1000, transcendentals=0),
        name="product",
    )(core, left, right, *extra)
    return here, give(away, "core", 1)


def spread_in_body(gate, gate_got, up, up_got, down, down_got, spread):
    rows = spread.shape[1]
    half = FEED_SLICE // 2
    for two in range(4):
        at = slice(two * 2 * rows, (two + 1) * 2 * rows)
        gates, ups, downs = (
            here[at].astype(jnp.float32) + got[at].astype(jnp.float32)
            for here, got in ((gate, gate_got), (up, up_got), (down, down_got))
        )
        for block in range(2):
            of = slice(block * rows, (block + 1) * rows)
            to = 4 * two + 2 * block
            spread[to, :, :FEED_SLICE] = gates[of].astype(spread.dtype)
            spread[to, :, FEED_SLICE:] = downs[of, :half].astype(spread.dtype)
            spread[to + 1, :, :FEED_SLICE] = ups[of].astype(spread.dtype)
            spread[to + 1, :, FEED_SLICE:] = downs[of, half:].astype(spread.dtype)


def spread_out_body(sums, gate, up, down):
    width = gate.shape[1]
    half = FEED_SLICE // 2
    for y in range(4):
        start = y * FEED_SLICE
        size = min(FEED_SLICE, width - start)
        gate[:, start : start + size] = sums[y, :, :size].astype(jnp.float32)
        up[:, start : start + size] = sums[4 + y, :, :size].astype(jnp.float32)
        for xl in range(2):
            first = start + xl * half
            size = min(half, width - first)
            down[:, first : first + size] = sums[
                4 * xl + y, :, FEED_SLICE : FEED_SLICE + size
            ].astype(jnp.float32)


def feed_slice(weight):
    y = lax.axis_index("y")
    padded = jnp.pad(weight, ((0, 0), (0, 4 * FEED_SLICE - weight.shape[1])))
    return lax.dynamic_slice_in_dim(padded, y * FEED_SLICE, FEED_SLICE, 1)


def local(
    tokens,
    cotangent,
    lengths,
    query_weight,
    key_weight,
    value_weight,
    out_weight,
    gate_weight,
    up_weight,
    down_weight,
    input_gain,
    query_gain,
    key_gain,
    attention_gain,
    feedforward_gain,
    output_gain,
):
    low = jnp.bfloat16
    wide = jnp.float32
    row_count, model_width = tokens.shape
    head_size = key_weight.shape[1]
    head_count = query_weight.shape[1] // head_size
    query_width = head_count * head_size
    qkv_width = query_width + 2 * head_size
    feed_width = gate_weight.shape[1]
    gain_shard = input_gain.shape[0]
    head_shard = query_gain.shape[0]
    y = lax.axis_index("y")
    seq_index = lax.axis_index("xl") * 4 + y
    place = seq_index.reshape(1).astype(jnp.int32)
    core = lax.axis_index("core").reshape(1).astype(jnp.int32)
    positions = seq_index * row_count + lax.iota(jnp.int32, row_count)
    valid = jnp.broadcast_to((positions < lengths[0]).astype(wide)[:, None], (row_count, 128))
    cosine, sine = rotary_tables(positions, head_size)

    def spread(vector):
        return jnp.pad(vector, (0, gain_shard - head_shard))

    gain_columns = jnp.stack(
        [
            input_gain,
            attention_gain,
            feedforward_gain,
            output_gain,
            spread(query_gain),
            spread(key_gain),
        ],
        axis=1,
    )
    gain_columns = jnp.pad(gain_columns, ((0, 0), (0, 122)))
    feed_weights = lax.all_gather(
        jnp.concatenate(
            [feed_slice(gate_weight), feed_slice(up_weight), feed_slice(down_weight)], axis=1
        ),
        DP,
        axis=0,
        tiled=True,
    )
    attention_weights = jnp.concatenate(
        [query_weight, key_weight, value_weight, gain_columns, out_weight], axis=1
    )
    beside = swap_x(attention_weights)
    qkv_columns = qkv_width + gain_columns.shape[1]
    tokens_ring = [take(ordered(tokens, beside), "y", by) for by in (1, 2, 3)]
    full_qkv, arrived = gather_rows(
        with_other_x(attention_weights[:, :qkv_columns], beside[:, :qkv_columns]), tokens_ring
    )
    gains = 1.0 + full_qkv[:, qkv_width : qkv_width + 8].astype(wide).T
    one_input, one_attention, one_feed, one_output = (gains[i : i + 1] for i in range(4))
    head_gain = gains.reshape(8, 16, gain_shard)[4:6, :, :head_shard].reshape(2, head_size)
    head_gain = jnp.pad(head_gain, ((0, 6), (0, 0)))

    def attention_input_of(rows):
        values = rows.astype(wide)
        return (values * inverse_rms(values) * one_input).astype(low)

    attention_input = attention_input_of(tokens)
    qkv_raw = jnp.dot(attention_input, full_qkv[:, :qkv_width], preferred_element_type=wide)
    prepare = rows_call(
        prepare_body,
        [((row_count, query_width), low), ((row_count, 2 * head_size), low)],
        "prepare",
    )
    query_low, local_pair = prepare(qkv_raw, head_gain, cosine, sine)
    near_pair, far_pair = (from_behind(local_pair, distance) for distance in (1, 2))
    input_ring = attention_input_of(jnp.concatenate([tokens] + tokens_ring, axis=0))
    near_pair, far_pair, input_ring = lax.optimization_barrier((near_pair, far_pair, input_ring))
    out_pair = with_other_x(out_weight, beside[:, qkv_columns:])
    full_out, _ = gather_rows(ordered(out_pair, *arrived), (near_pair, far_pair))
    attend = rows_call(
        attend_body,
        [((row_count, query_width), low), ((8, row_count), wide)],
        "attend",
    )
    context_low, log_total = attend(place, query_low, far_pair, near_pair, local_pair)
    residual = rows_call(
        residual_body,
        [
            ((row_count, model_width), wide),
            ((row_count, model_width), wide),
            ((row_count, model_width), low),
        ],
        "residual",
    )
    attention_raw, state, feed_input = residual(
        context_low, full_out, tokens, one_attention, one_feed
    )

    weights, feed_input = lax.optimization_barrier((feed_weights, feed_input))

    def touch(array):
        def body(whole, some):
            some[...] = whole[:16, :128]

        return pl.pallas_call(
            body,
            in_specs=[pl.BlockSpec(memory_space=pltpu.VMEM)],
            out_specs=pl.BlockSpec(memory_space=pltpu.VMEM),
            out_shape=jax.ShapeDtypeStruct((16, 128), array.dtype),
            compiler_params=pltpu.CompilerParams(vmem_limit_bytes=VMEM),
            cost_estimate=pl.CostEstimate(flops=LONG, bytes_accessed=1000, transcendentals=0),
            name="touch",
        )(array)

    def exchange(rows, run):
        two, one, three = (take(rows, "y", by) for by in (2, 1, 3))
        two, touched = lax.optimization_barrier((two, touch(weights)))
        kept, two_part = run(two, [], 3 * row_count, 1000, [touched])
        across = give(two_part, "y", 2)
        both = jnp.concatenate([one, three], axis=0)
        kept, both_part = run(both, kept, 0, LONG)
        from_one = give(both_part[:row_count], "y", 1)
        from_three = give(both_part[row_count:], "y", 3)
        *kept, across, both = lax.optimization_barrier((*kept, across, both))
        kept, own_part = run(rows, kept, 2 * row_count, LONG)
        ring = jnp.concatenate([ordered(both, own_part, from_one, from_three), rows, two], axis=0)
        return kept, [own_part, from_one, across, from_three], ring

    def forward(rows, kept, at, cost, unread=()):
        *kept, part = feed_call(feed_body, rows, weights, [], kept, at, 3, cost, "feed", unread)
        return kept, part

    kept, terms, feed_ring = exchange(feed_input, forward)
    hidden, value, slope = kept
    finish = blocks_call(
        down_body,
        [
            ((row_count, model_width), low),
            ((row_count, model_width), low),
            ((8, model_width), wide),
        ],
        "finish",
    )
    layer_output, down_grad, output_gain_rows = finish(
        *terms, state, cotangent, valid, one_output
    )

    def backward(rows, kept, at, cost):
        *kept, part = feed_call(
            feed_back_body, rows, weights, [value, slope], kept, at, 2, cost, "feed_back"
        )
        return kept, part

    rows72 = gain_shard
    two, one, three = (take(down_grad, "y", by) for by in (2, 1, 3))
    kept, own_part = backward(down_grad, [], 2 * row_count, 1000)
    kept, two_part = backward(two, kept, 3 * row_count, 1000)
    across = give(two_part, "y", 2)
    both = jnp.concatenate([one, three], axis=0)
    (gate_grad, up_grad), both_part = backward(both, kept, 0, LONG)
    from_one = give(both_part[:row_count], "y", 1)
    from_three = give(both_part[row_count:], "y", 3)
    across, both, gate_grad, up_grad = lax.optimization_barrier((across, both, gate_grad, up_grad))
    down_ring = jnp.concatenate([both, down_grad, two], axis=0)
    down_halves = product(core, down_ring, hidden, cost=LONG)
    terms = [own_part, from_one, across, from_three]
    gate_halves = product(core, ordered(feed_ring, down_halves[0]), gate_grad)
    up_halves = product(
        core,
        ordered(feed_ring, gate_halves[0], from_one, from_three, down_halves[1]),
        up_grad,
    )
    halves = [*gate_halves, *up_halves, *down_halves]
    (spread_in,) = rows_call(
        spread_in_body, [((16, rows72, FEED_SLICE * 3 // 2), low)], "spread_in"
    )(*halves)
    feed_sum = lax.psum_scatter(spread_in, ("z", "xh", "xl"), scatter_dimension=0, tiled=False)
    back = blocks_call(
        state_body,
        [
            ((row_count, model_width), low),
            ((row_count, model_width), wide),
            ((16, model_width), wide),
        ],
        "state_back",
        60 * 1024 * 1024,
    )
    attention_grad, state_grad, state_gain_rows = back(
        *terms, state, attention_raw, cotangent, valid, one_feed, one_attention
    )

    attend_back = rows_call(
        attend_back_body,
        [
            ((row_count, 2 * head_size), low),
            ((row_count, 2 * head_size), low),
            ((row_count, 2 * head_size), wide),
            ((row_count, query_width), low),
            ((8, head_size), wide),
        ],
        "attend_back",
    )
    far_grad, near_grad, own_grad, query_grad, query_gain_rows = attend_back(
        place,
        attention_grad,
        full_out,
        query_low,
        far_pair,
        near_pair,
        local_pair,
        log_total,
        qkv_raw,
        head_gain,
        cosine,
        sine,
    )
    near_back = from_behind(near_grad, -1)
    far_back = from_behind(far_grad, -2)
    out_halves = product(core, ordered(attention_grad, near_grad), context_low, cost=LONG)
    pair_back = rows_call(
        pair_back_body,
        [
            ((row_count, 2 * head_size), low),
            ((4, row_count + 384, qkv_width // 4), low),
            ((8, head_size), wide),
        ],
        "pair_back",
    )
    pair_grad, qkv_cut, key_gain_rows = pair_back(
        query_grad, own_grad, near_back, far_back, qkv_raw, head_gain, cosine, sine, *out_halves
    )
    pieces = [give(pick(qkv_cut, (y + by) % 4, 0), "y", by) for by in (3, 2, 1)]
    qkv_ring, out_sum = rows_call(
        arrive_body,
        [((4 * row_count, qkv_width // 4), low), ((model_width // 2, query_width // 4), low)],
        "arrive",
    )(pick(qkv_cut, y, 0), *pieces)
    input_back = rows_call(
        input_body,
        [((row_count, model_width), low), ((8, model_width), wide)],
        "input_back",
    )
    tokens_grad, input_gain_rows = input_back(
        query_grad, pair_grad, full_qkv, tokens, state_grad, one_input
    )

    def spread_head(vector):
        return jnp.pad(
            vector.reshape(16, head_shard), ((0, 0), (0, gain_shard - head_shard))
        ).reshape(model_width)

    gain_block = jnp.stack(
        [
            input_gain_rows[0],
            state_gain_rows[8],
            state_gain_rows[0],
            output_gain_rows[0],
            spread_head(query_gain_rows[0]),
            spread_head(key_gain_rows[0]),
        ],
        axis=1,
    )
    gain_block = jnp.pad(gain_block, ((0, 0), (0, 122)))
    z = lax.axis_index("z")
    xh = lax.axis_index("xh")
    offsets = jnp.stack(
        [(((z + i) % 4) * 2 + (xh + j) % 2) * rows72 for i in range(4) for j in range(2)]
    ).astype(jnp.int32)
    columns = qkv_width // 4 + 128 + query_width // 4
    parts = pl.pallas_call(
        chip_body,
        in_specs=[pl.BlockSpec(memory_space=pltpu.SMEM)]
        + [pl.BlockSpec(memory_space=pltpu.VMEM)] * 3,
        out_specs=[pl.BlockSpec(memory_space=pltpu.VMEM)] * 4,
        out_shape=[jax.ShapeDtypeStruct((2, rows72, columns), low)] * 4,
        scratch_shapes=[pltpu.VMEM((model_width // 2, columns), wide)],
        compiler_params=pltpu.CompilerParams(vmem_limit_bytes=VMEM),
        cost_estimate=SMALL,
        name="chip",
    )(offsets, *product(core, input_ring, qkv_ring, gain_block), out_sum)
    total = parts[0].astype(wide)
    for by in (1, 3, 2):
        total = total + give(parts[by], "z", by).astype(wide)
    attention_column = total.astype(low)
    attention_half = (
        attention_column[0].astype(wide) + swap_x(attention_column[1]).astype(wide)
    ).astype(low)
    attention_sum = (
        attention_half.astype(wide) + give(attention_half, "xl", 1).astype(wide)
    ).astype(low)
    attention_blocks = in_order(
        [attention_sum] + [take(attention_sum, "y", by) for by in (1, 2, 3)]
    )
    feed_sums = lax.all_gather(ordered(feed_sum, parts[0]), SEQ, axis=0, tiled=False)
    gate_weight_grad, up_weight_grad, down_weight_grad = rows_call(
        spread_out_body, [((rows72, feed_width), wide)] * 3, "spread_out"
    )(feed_sums)
    qkv_cols = qkv_width // 4
    out_cols = query_width // 4
    qkv_weight_grad = jnp.concatenate([b[:, :qkv_cols] for b in attention_blocks], axis=1)
    out_weight_grad = jnp.concatenate([b[:, qkv_cols + 128 :] for b in attention_blocks], axis=1)
    gain_sum = sum(b[:, qkv_cols : qkv_cols + 128].astype(wide) for b in attention_blocks)
    return (
        layer_output,
        tokens_grad,
        qkv_weight_grad[:, :query_width].astype(wide),
        qkv_weight_grad[:, query_width : query_width + head_size].astype(wide),
        qkv_weight_grad[:, query_width + head_size :].astype(wide),
        out_weight_grad.astype(wide),
        gate_weight_grad,
        up_weight_grad,
        down_weight_grad,
        gain_sum[:, 0],
        gain_sum[:head_shard, 4],
        gain_sum[:head_shard, 5],
        gain_sum[:, 1],
        gain_sum[:, 2],
        gain_sum[:, 3],
    )


def solution(mesh):
    fine = Mesh(mesh.devices.reshape(SIZES), AXES)
    rows = P(AXES, None)
    matrix = P(DP, None)
    vector = P(DP)
    return jax.shard_map(
        local,
        mesh=fine,
        in_specs=(rows, rows, vector) + (matrix,) * 7 + (vector,) * 6,
        out_specs=(rows, rows) + (matrix,) * 7 + (vector,) * 6,
        check_vma=False,
    )
```

```python
import functools
import math

import jax
import jax.numpy as jnp
from jax import lax
from jax.experimental import pallas as pl
from jax.experimental.pallas import tpu as pltpu
from jax.sharding import Mesh
from jax.sharding import PartitionSpec as P

EPSILON = 1e-06
GELU_COEFF = 0.044715
AXES = ("z", "xh", "core", "xl", "y")
SIZES = (4, 2, 2, 2, 4)
DP = ("z", "xh", "core")
SEQ = ("xl", "y")
FEED_SLICE = 1792
FEED_TILES = ((0, 1024), (1024, 768))
HEADS = 4
HEAD = 256
SCALE = HEAD**-0.5
ROWS = 256
VMEM = 16 * 1024 * 1024
MOST = 56 * 1024 * 1024
LONG = 12 * 10**9
SMALL = pl.CostEstimate(flops=1000, bytes_accessed=1000, transcendentals=0)


def from_behind(array, by):
    pairs = [(i, i + by) for i in range(8) if 0 <= i + by < 8]
    return lax.ppermute(array, SEQ, pairs)


def take(array, axis, by):
    count = lax.axis_size(axis)
    return lax.ppermute(array, axis, [((i + by) % count, i) for i in range(count)])


def give(array, axis, by):
    count = lax.axis_size(axis)
    return lax.ppermute(array, axis, [(i, (i + by) % count) for i in range(count)])


def swap_x(array):
    return lax.ppermute(array, ("xh", "xl"), [(0, 3), (3, 0), (1, 2), (2, 1)])


def ordered(value, *after):
    return lax.optimization_barrier((value,) + after)[0]


def pick(array, index, axis):
    return lax.dynamic_index_in_dim(array, index, axis, keepdims=False)


def with_other_x(block, beside):
    xh = lax.axis_index("xh")
    return jnp.where(xh == 0, jnp.stack([block, beside]), jnp.stack([beside, block]))


def gather_rows(pair, wait=()):
    _, rows, width = pair.shape
    z = lax.axis_index("z")
    core = lax.axis_index("core")
    ring = [(take(pair, "z", by), by) for by in (1, 3, 2)]
    arrived = [piece for piece, _ in ring]
    own = jnp.zeros((4, 2, rows, width), pair.dtype)
    own = lax.dynamic_update_slice_in_dim(own, pair[None], z, 0)
    own = ordered(own, *wait)
    for piece, by in ring:
        own = lax.dynamic_update_slice_in_dim(own, piece[None], (z + by) % 4, 0)
    other = give(own, "core", 1)
    both = jnp.where(
        core == 0, jnp.stack([own, other], axis=2), jnp.stack([other, own], axis=2)
    )
    return both.reshape(16 * rows, width), arrived


def in_order(blocks):
    y = lax.axis_index("y")
    placed = []
    for place in range(4):
        value = blocks[(place - 3) % 4]
        for at in range(3):
            value = jnp.where(y == at, blocks[(place - at) % 4], value)
        placed.append(value)
    return placed


def inverse_rms(values):
    return lax.rsqrt(jnp.mean(values * values, axis=-1, keepdims=True) + EPSILON)


def rms_backward(values, scaling, upstream):
    inner = jnp.mean(upstream * values, axis=-1, keepdims=True)
    return scaling * (upstream - values * (scaling * scaling) * inner)


def rotary_tables(positions, head_size):
    half_size = head_size // 2
    exponents = lax.iota(jnp.float32, half_size) * (2.0 / head_size)
    frequency = jnp.power(10000.0, -exponents)
    angles = positions.astype(jnp.float32)[:, None] * frequency[None, :]
    return (jnp.cos(angles), jnp.sin(angles))


def gelu_parts(values):
    root_coeff = math.sqrt(2.0 / math.pi)
    square = values * values
    bend = jnp.tanh(values * (root_coeff + (root_coeff * GELU_COEFF) * square))
    part = 0.5 + 0.5 * bend
    gelu_value = values * part
    inner = root_coeff + (3.0 * GELU_COEFF * root_coeff) * square
    gelu_slope = part + gelu_value * (1.0 - bend) * inner
    return (gelu_value, gelu_slope)


def dot(left, right, left_axis=1, right_axis=0):
    return lax.dot_general(
        left,
        right,
        (((left_axis,), (right_axis,)), ((), ())),
        preferred_element_type=jnp.float32,
    )


def turn(first, second, cosine, sine):
    return first * cosine - second * sine, second * cosine + first * sine


def turn_back(first, second, cosine, sine):
    return first * cosine + second * sine, second * cosine - first * sine


def rows_call(body, outs, name, cost=1000):
    def call(*operands):
        specs = [
            pl.BlockSpec(memory_space=pltpu.SMEM)
            if operand.dtype == jnp.int32
            else pl.BlockSpec(memory_space=pltpu.VMEM)
            for operand in operands
        ]
        return pl.pallas_call(
            body,
            out_shape=[jax.ShapeDtypeStruct(shape, dtype) for shape, dtype in outs],
            in_specs=specs,
            out_specs=[pl.BlockSpec(memory_space=pltpu.VMEM) for _ in outs],
            compiler_params=pltpu.CompilerParams(vmem_limit_bytes=VMEM),
            cost_estimate=pl.CostEstimate(flops=cost, bytes_accessed=1000, transcendentals=0),
            name=name,
        )(*operands)

    return call


def blocks_call(body, outs, name, vmem=VMEM, cost=1000):
    steps = 4

    def spec(shape):
        if shape[0] < ROWS:
            return pl.BlockSpec(shape, lambda i: (0, 0))
        return pl.BlockSpec((shape[0] // steps, shape[1]), lambda i: (i, 0))

    def call(*operands):
        return pl.pallas_call(
            body,
            grid=(steps,),
            out_shape=[jax.ShapeDtypeStruct(shape, dtype) for shape, dtype in outs],
            in_specs=[spec(operand.shape) for operand in operands],
            out_specs=[spec(shape) for shape, _ in outs],
            compiler_params=pltpu.CompilerParams(vmem_limit_bytes=vmem),
            cost_estimate=pl.CostEstimate(flops=cost, bytes_accessed=1000, transcendentals=0),
            name=name,
        )(*operands)

    return call


def prepare_body(raw, gain, cosine, sine, query, pair):
    cos, sin = cosine[...], sine[...]
    half = HEAD // 2

    def finish(block, gains):
        hat = block * inverse_rms(block) * gains
        first, second = turn(hat[:, :half], hat[:, half:], cos, sin)
        return jnp.concatenate([first, second], axis=1).astype(jnp.bfloat16)

    for head in range(HEADS):
        at = slice(head * HEAD, (head + 1) * HEAD)
        query[:, at] = finish(raw[:, at], gain[0:1, :])
    keys = HEADS * HEAD
    pair[:, :HEAD] = finish(raw[:, keys : keys + HEAD], gain[1:2, :])
    pair[:, HEAD:] = raw[:, keys + HEAD : keys + 2 * HEAD].astype(jnp.bfloat16)


def attend_body(place, query, far, near, own, context, log_total):
    row = lax.broadcasted_iota(jnp.int32, (ROWS, ROWS), 0)
    column = lax.broadcasted_iota(jnp.int32, (ROWS, ROWS), 1)
    seq = place[0]
    allowed = (
        (row < column) & (seq >= 2),
        jnp.full((ROWS, ROWS), seq >= 1),
        column <= row,
    )
    blocks = (far, near, own)
    lane = lax.broadcasted_iota(jnp.int32, (ROWS, 128), 1)
    logs = jnp.zeros((ROWS, 128), jnp.float32)
    for head in range(HEADS):
        at = slice(head * HEAD, (head + 1) * HEAD)
        scores = [
            jnp.where(ok, dot(query[:, at], block[:, :HEAD], 1, 1) * SCALE, -1e30)
            for ok, block in zip(allowed, blocks)
        ]
        top = jnp.max(jnp.maximum(jnp.maximum(scores[0], scores[1]), scores[2]), 1, keepdims=True)
        terms = [jnp.exp(score - top) for score in scores]
        total = jnp.sum(terms[0] + terms[1] + terms[2], 1, keepdims=True)
        share = 1.0 / total
        out = sum(
            dot((term * share).astype(jnp.bfloat16), block[:, HEAD:])
            for term, block in zip(terms, blocks)
        )
        context[:, at] = out.astype(jnp.bfloat16)
        logs = jnp.where(lane == head, top + jnp.log(total), logs)
    log_total[...] = logs.T[:8]


def attend_back_body(
    place,
    upstream,
    out_weight,
    query,
    far,
    near,
    own,
    log_total,
    raw,
    gain,
    cosine,
    sine,
    far_grad,
    near_grad,
    own_grad,
    query_grad,
    gain_grad,
    key_sums,
    value_sums,
):
    low = jnp.bfloat16
    half = HEAD // 2
    head = pl.program_id(0)

    @pl.when(head == 0)
    def _():
        key_sums[...] = jnp.zeros_like(key_sums)
        value_sums[...] = jnp.zeros_like(value_sums)
        gain_grad[...] = jnp.zeros_like(gain_grad)

    key_at = lax.broadcasted_iota(jnp.int32, (ROWS, ROWS), 0)
    query_at = lax.broadcasted_iota(jnp.int32, (ROWS, ROWS), 1)
    seq = place[0]
    allowed = (
        (query_at < key_at) & (seq >= 2),
        jnp.full((ROWS, ROWS), seq >= 1),
        key_at <= query_at,
    )
    blocks = (far, near, own)
    context_grad = dot(upstream[...], out_weight[...]).astype(low)
    queries = query[...]
    logs = log_total[pl.ds(head, 1), :]
    probs = [
        jnp.where(ok, jnp.exp(dot(block[:, :HEAD], queries, 1, 1) * SCALE - logs), 0.0)
        for ok, block in zip(allowed, blocks)
    ]
    prob_grads = [dot(block[:, HEAD:], context_grad, 1, 1) for block in blocks]
    inner = jnp.sum(
        probs[0] * prob_grads[0] + probs[1] * prob_grads[1] + probs[2] * prob_grads[2],
        0,
        keepdims=True,
    )
    query_rot = 0.0
    for at_block, block in enumerate(blocks):
        score_grad = (probs[at_block] * (prob_grads[at_block] - inner)).astype(low)
        query_rot = query_rot + dot(score_grad, block[:, :HEAD], 0, 0)
        key_sums[at_block] += dot(score_grad, queries)
        value_sums[at_block] += dot(probs[at_block].astype(low), context_grad)
    query_rot = query_rot * SCALE
    first, second = turn_back(query_rot[:, :half], query_rot[:, half:], cosine[...], sine[...])
    upper = jnp.concatenate([first, second], axis=1)
    block = raw[...]
    scaling = inverse_rms(block)
    gain_grad[...] += jnp.broadcast_to(
        jnp.sum(upper * (block * scaling), 0, keepdims=True), (8, HEAD)
    )
    query_grad[...] = rms_backward(block, scaling, upper * gain[0:1, :]).astype(low)

    @pl.when(head == HEADS - 1)
    def _():
        for at_block, grad in enumerate((far_grad, near_grad, own_grad)):
            grad[:, :HEAD] = (key_sums[at_block] * SCALE).astype(grad.dtype)
            grad[:, HEAD:] = value_sums[at_block].astype(grad.dtype)


def pair_back_body(
    query, own, near, far, raw, gain, cosine, sine, out, out_got, pair_grad, cut, gain_grad
):
    half = HEAD // 2
    low = jnp.bfloat16
    total = own[...] + near[...].astype(jnp.float32) + far[...].astype(jnp.float32)
    first, second = turn_back(total[:, :half], total[:, half:HEAD], cosine[...], sine[...])
    upper = jnp.concatenate([first, second], axis=1)
    block = raw[...]
    scaling = inverse_rms(block)
    gain_sum = jnp.sum(upper * (block * scaling), 0, keepdims=True)
    gain_grad[...] = jnp.broadcast_to(gain_sum, (8, HEAD))
    keys = rms_backward(block, scaling, upper * gain[1:2, :]).astype(low)
    values = total[:, HEAD:].astype(low)
    pair_grad[:, :HEAD] = keys
    pair_grad[:, HEAD:] = values
    size = cut.shape[2]
    cut[0, :ROWS] = query[:, :size]
    cut[1, :ROWS] = query[:, size : 2 * size]
    cut[2, :ROWS] = jnp.concatenate([query[:, 2 * size :], keys[:, :half]], axis=1)
    cut[3, :ROWS] = jnp.concatenate([keys[:, half:], values], axis=1)
    for part in range(4):
        at = slice(part * HEAD, (part + 1) * HEAD)
        term = (out[:, at].astype(jnp.float32) + out_got[:, at].astype(jnp.float32)).astype(low)
        cut[part, ROWS:, :HEAD] = term[:384]
        cut[part, ROWS : ROWS + 192, HEAD:] = term[384:, :half]
        cut[part, ROWS + 192 :, HEAD:] = term[384:, half:]


def arrive_body(own, one, two, three, ring, out):
    wide = jnp.float32
    half = HEAD // 2
    for at, block in enumerate((own, one, two, three)):
        ring[at * ROWS : (at + 1) * ROWS] = block[:ROWS]
    total = sum(block[ROWS:].astype(wide) for block in (own, one, two, three)).astype(out.dtype)
    out[:384] = total[:, :HEAD]
    out[384:, :half] = total[:192, HEAD:]
    out[384:, half:] = total[192:, HEAD:]


def chip_body(offsets, here, got, out, *refs):
    *parts, total = refs
    wide = jnp.float32
    columns = here.shape[1]
    rows = parts[0].shape[1]
    total[:, :columns] = here[...].astype(wide) + got[...].astype(wide)
    total[:, columns:] = out[...].astype(wide)
    for at, part in enumerate(parts):
        for block in range(2):
            start = pl.multiple_of(offsets[2 * at + block], 8)
            part[block] = total[pl.ds(start, rows), :].astype(part.dtype)


def residual_body(
    context, out_weight, tokens, attention_gain, feed_gain, raw, state, feed_input
):
    value = dot(context[...], out_weight[...], 1, 1)
    raw[...] = value
    hidden = tokens[...].astype(jnp.float32) + value * inverse_rms(value) * attention_gain[...]
    state[...] = hidden
    feed_input[...] = (hidden * inverse_rms(hidden) * feed_gain[...]).astype(jnp.bfloat16)


def down_body(
    part, near, across, behind, state, cotangent, valid, gain, layer, down_grad, gain_grad
):
    wide = jnp.float32
    raw = (
        part[...].astype(wide)
        + near[...].astype(wide)
        + across[...].astype(wide)
        + behind[...].astype(wide)
    )
    scaling = inverse_rms(raw)
    hat = raw * scaling
    ok = valid[:, :1]
    layer[...] = (ok * (state[...] + hat * gain[...])).astype(jnp.bfloat16)
    upstream = cotangent[...].astype(wide) * ok

    @pl.when(pl.program_id(0) == 0)
    def _():
        gain_grad[...] = jnp.zeros_like(gain_grad)

    gain_grad[...] += jnp.broadcast_to(
        jnp.sum(upstream * hat, 0, keepdims=True), (8, hat.shape[1])
    )
    down_grad[...] = rms_backward(raw, scaling, upstream * gain[...]).astype(jnp.bfloat16)


def state_body(
    part,
    near,
    across,
    behind,
    state,
    raw,
    cotangent,
    valid,
    feed_gain,
    attention_gain,
    attention_grad,
    state_grad,
    gain_grads,
):
    wide = jnp.float32
    feed_grad = (
        part[...].astype(wide)
        + near[...].astype(wide)
        + across[...].astype(wide)
        + behind[...].astype(wide)
    )
    hidden = state[...]
    scaling = inverse_rms(hidden)
    upstream = cotangent[...].astype(wide) * valid[:, :1]
    total = upstream + rms_backward(hidden, scaling, feed_grad * feed_gain[...])
    state_grad[...] = total
    value = raw[...]
    value_scaling = inverse_rms(value)
    width = value.shape[1]

    @pl.when(pl.program_id(0) == 0)
    def _():
        gain_grads[...] = jnp.zeros_like(gain_grads)

    gain_grads[:8] += jnp.broadcast_to(
        jnp.sum(feed_grad * (hidden * scaling), 0, keepdims=True), (8, width)
    )
    gain_grads[8:] += jnp.broadcast_to(
        jnp.sum(total * (value * value_scaling), 0, keepdims=True), (8, width)
    )
    attention_grad[...] = rms_backward(value, value_scaling, total * attention_gain[...]).astype(
        jnp.bfloat16
    )


def input_body(
    query_grad, pair_grad, weight, tokens, state_grad, gain, tokens_grad, gain_grad
):
    queries = query_grad.shape[1]
    pairs = pair_grad.shape[1]
    grad = dot(query_grad[...], weight[:, :queries], 1, 1) + dot(
        pair_grad[...], weight[:, queries : queries + pairs], 1, 1
    )
    value = tokens[...].astype(jnp.float32)
    scaling = inverse_rms(value)
    gain_grad[...] = jnp.broadcast_to(
        jnp.sum(grad * (value * scaling), 0, keepdims=True), (8, value.shape[1])
    )
    tokens_grad[...] = (
        state_grad[...] + rms_backward(value, scaling, grad * gain[...])
    ).astype(jnp.bfloat16)


def feed_body(place, rows, weights, *refs):
    hidden_out, value_out, slope_out, part, total = refs[-5:]
    low = jnp.bfloat16
    for first, size in FEED_TILES:
        gate_at, up_at, down_at = (
            slice(start + first, start + first + size) for start in (0, FEED_SLICE, 2 * FEED_SLICE)
        )
        to = slice(place, place + rows.shape[0])
        gate_raw = dot(rows[...], weights[:, gate_at])
        up_raw = dot(rows[...], weights[:, up_at])
        value, slope = gelu_parts(gate_raw)
        hidden = (value * up_raw).astype(low)
        hidden_out[to, gate_at] = hidden
        value_out[to, gate_at] = value.astype(low)
        slope_out[to, gate_at] = (slope * up_raw).astype(low)
        term = dot(hidden, weights[:, down_at], 1, 1)
        total[...] = term if first == 0 else total[...] + term

    part[...] = total[...].astype(low)


def feed_back_body(place, rows, weights, value, slope, *refs):
    gate_out, up_out, part, total = refs[-4:]
    low = jnp.bfloat16
    for first, size in FEED_TILES:
        gate_at, up_at, down_at = (
            slice(start + first, start + first + size) for start in (0, FEED_SLICE, 2 * FEED_SLICE)
        )
        to = slice(place, place + rows.shape[0])
        hidden_grad = dot(rows[...], weights[:, down_at])
        gate_grad = (hidden_grad * slope[to, gate_at].astype(jnp.float32)).astype(low)
        up_grad = (hidden_grad * value[to, gate_at].astype(jnp.float32)).astype(low)
        gate_out[to, gate_at] = gate_grad
        up_out[to, gate_at] = up_grad
        term = dot(gate_grad, weights[:, gate_at], 1, 1) + dot(up_grad, weights[:, up_at], 1, 1)
        total[...] = term if first == 0 else total[...] + term

    part[...] = total[...].astype(low)


def feed_call(body, rows, weights, read, kept, place, outs, cost, name, unread=()):
    count, width = rows.shape
    operands = [rows, weights, *read, *kept, *unread]
    whole = pl.BlockSpec(memory_space=pltpu.VMEM)
    first_kept = 2 + len(read)
    return pl.pallas_call(
        functools.partial(body, place),
        in_specs=[whole] * first_kept
        + [pl.BlockSpec(memory_space=pl.ANY)] * (len(kept) + len(unread)),
        out_specs=[whole] * (outs + 1),
        out_shape=[jax.ShapeDtypeStruct((4 * ROWS, FEED_SLICE), jnp.bfloat16)] * outs
        + [jax.ShapeDtypeStruct((count, width), jnp.bfloat16)],
        scratch_shapes=[pltpu.VMEM((count, width), jnp.float32)],
        input_output_aliases={first_kept + i: i for i in range(len(kept))},
        compiler_params=pltpu.CompilerParams(vmem_limit_bytes=VMEM),
        cost_estimate=pl.CostEstimate(flops=cost, bytes_accessed=1000, transcendentals=0),
        name=name,
    )(*operands)


def product_body(core, left, right, *refs):
    away, here, total = refs[-3:]
    rows = left.shape[1] // 16
    width = right.shape[1]

    def split(to, first, columns):
        for two in range(4):
            pieces = [
                total[pl.ds(pl.multiple_of((4 * two + 2 * i + first) * rows, 8), rows), :columns]
                for i in (0, 1)
            ]
            yield slice(two * 2 * rows, (two + 1) * 2 * rows), jnp.concatenate(pieces, axis=0)

    for start in range(0, width, total.shape[1]):
        size = min(total.shape[1], width - start)
        at = slice(start, start + size)
        total[:, :size] = dot(left[...], right[:, at], 0, 0)
        for to, first in ((away, 1 - core[0]), (here, core[0])):
            for place, value in split(to, first, size):
                to[place, at] = value.astype(to.dtype)
    if len(refs) > 3:
        extra = refs[0]
        at = slice(width, width + extra.shape[1])
        total[:, : extra.shape[1]] = extra[...]
        for to, first in ((away, 1 - core[0]), (here, core[0])):
            for place, value in split(to, first, extra.shape[1]):
                to[place, at] = value.astype(to.dtype)


def product(core, left, right, *extra, cost=1000):
    width = right.shape[1] + sum(block.shape[1] for block in extra)
    out = jax.ShapeDtypeStruct((left.shape[1] // 2, width), jnp.bfloat16)
    whole = pl.BlockSpec(memory_space=pltpu.VMEM)
    away, here = pl.pallas_call(
        product_body,
        in_specs=[pl.BlockSpec(memory_space=pltpu.SMEM)] + [whole] * (2 + len(extra)),
        out_specs=[whole, whole],
        out_shape=[out, out],
        scratch_shapes=[pltpu.VMEM((left.shape[1], 512), jnp.float32)],
        compiler_params=pltpu.CompilerParams(vmem_limit_bytes=VMEM),
        cost_estimate=pl.CostEstimate(flops=cost, bytes_accessed=1000, transcendentals=0),
        name="product",
    )(core, left, right, *extra)
    return here, give(away, "core", 1)


def spread_in_body(gate, gate_got, up, up_got, down, down_got, spread):
    rows = spread.shape[1]
    half = FEED_SLICE // 2
    gates, ups, downs = (
        here[...].astype(jnp.float32) + got[...].astype(jnp.float32)
        for here, got in ((gate, gate_got), (up, up_got), (down, down_got))
    )
    for block in range(2):
        of = slice(block * rows, (block + 1) * rows)
        to = 2 * block
        spread[to, :, :FEED_SLICE] = gates[of].astype(spread.dtype)
        spread[to, :, FEED_SLICE:] = downs[of, :half].astype(spread.dtype)
        spread[to + 1, :, :FEED_SLICE] = ups[of].astype(spread.dtype)
        spread[to + 1, :, FEED_SLICE:] = downs[of, half:].astype(spread.dtype)


def spread_out_body(sums, gate, up, down):
    width = gate.shape[1]
    half = FEED_SLICE // 2
    for y in range(4):
        start = y * FEED_SLICE
        size = min(FEED_SLICE, width - start)
        gate[:, start : start + size] = sums[y, :, :size].astype(jnp.float32)
        up[:, start : start + size] = sums[4 + y, :, :size].astype(jnp.float32)
        for xl in range(2):
            first = start + xl * half
            size = min(half, width - first)
            down[:, first : first + size] = sums[
                4 * xl + y, :, FEED_SLICE : FEED_SLICE + size
            ].astype(jnp.float32)


def feed_slice(weight):
    y = lax.axis_index("y")
    padded = jnp.pad(weight, ((0, 0), (0, 4 * FEED_SLICE - weight.shape[1])))
    return lax.dynamic_slice_in_dim(padded, y * FEED_SLICE, FEED_SLICE, 1)


def local(
    tokens,
    cotangent,
    lengths,
    query_weight,
    key_weight,
    value_weight,
    out_weight,
    gate_weight,
    up_weight,
    down_weight,
    input_gain,
    query_gain,
    key_gain,
    attention_gain,
    feedforward_gain,
    output_gain,
):
    low = jnp.bfloat16
    wide = jnp.float32
    row_count, model_width = tokens.shape
    head_size = key_weight.shape[1]
    head_count = query_weight.shape[1] // head_size
    query_width = head_count * head_size
    qkv_width = query_width + 2 * head_size
    feed_width = gate_weight.shape[1]
    gain_shard = input_gain.shape[0]
    head_shard = query_gain.shape[0]
    y = lax.axis_index("y")
    seq_index = lax.axis_index("xl") * 4 + y
    place = seq_index.reshape(1).astype(jnp.int32)
    core = lax.axis_index("core").reshape(1).astype(jnp.int32)
    positions = seq_index * row_count + lax.iota(jnp.int32, row_count)
    valid = jnp.broadcast_to((positions < lengths[0]).astype(wide)[:, None], (row_count, 128))
    cosine, sine = rotary_tables(positions, head_size)

    def spread(vector):
        return jnp.pad(vector, (0, gain_shard - head_shard))

    gain_columns = jnp.stack(
        [
            input_gain,
            attention_gain,
            feedforward_gain,
            output_gain,
            spread(query_gain),
            spread(key_gain),
        ],
        axis=1,
    )
    gain_columns = jnp.pad(gain_columns, ((0, 0), (0, 122)))
    feed_weights = lax.all_gather(
        jnp.concatenate(
            [feed_slice(gate_weight), feed_slice(up_weight), feed_slice(down_weight)], axis=1
        ),
        DP,
        axis=0,
        tiled=True,
    )
    attention_weights = jnp.concatenate(
        [query_weight, key_weight, value_weight, gain_columns, out_weight], axis=1
    )
    beside = swap_x(attention_weights)
    qkv_columns = qkv_width + gain_columns.shape[1]
    tokens_ring = [take(ordered(tokens, beside), "y", by) for by in (1, 2, 3)]
    full_qkv, arrived = gather_rows(
        with_other_x(attention_weights[:, :qkv_columns], beside[:, :qkv_columns]), tokens_ring
    )
    gains = 1.0 + full_qkv[:, qkv_width : qkv_width + 8].astype(wide).T
    one_input, one_attention, one_feed, one_output = (gains[i : i + 1] for i in range(4))
    head_gain = gains.reshape(8, 16, gain_shard)[4:6, :, :head_shard].reshape(2, head_size)
    head_gain = jnp.pad(head_gain, ((0, 6), (0, 0)))

    def attention_input_of(rows):
        values = rows.astype(wide)
        return (values * inverse_rms(values) * one_input).astype(low)

    attention_input = attention_input_of(tokens)
    qkv_raw = jnp.dot(attention_input, full_qkv[:, :qkv_width], preferred_element_type=wide)
    prepare = rows_call(
        prepare_body,
        [((row_count, query_width), low), ((row_count, 2 * head_size), low)],
        "prepare",
    )
    query_low, local_pair = prepare(qkv_raw, head_gain, cosine, sine)
    near_pair, far_pair = (from_behind(local_pair, distance) for distance in (1, 2))
    input_ring = attention_input_of(jnp.concatenate([tokens] + tokens_ring, axis=0))
    near_pair, far_pair, input_ring = lax.optimization_barrier((near_pair, far_pair, input_ring))
    out_pair = with_other_x(out_weight, beside[:, qkv_columns:])
    full_out, _ = gather_rows(ordered(out_pair, *arrived), (near_pair, far_pair))
    attend = rows_call(
        attend_body,
        [((row_count, query_width), low), ((8, row_count), wide)],
        "attend",
    )
    context_low, log_total = attend(place, query_low, far_pair, near_pair, local_pair)
    residual = rows_call(
        residual_body,
        [
            ((row_count, model_width), wide),
            ((row_count, model_width), wide),
            ((row_count, model_width), low),
        ],
        "residual",
    )
    attention_raw, state, feed_input = residual(
        context_low, full_out, tokens, one_attention, one_feed
    )

    weights, feed_input = lax.optimization_barrier((feed_weights, feed_input))

    def touch(array):
        def body(whole, some):
            some[...] = whole[:16, :128]

        return pl.pallas_call(
            body,
            in_specs=[pl.BlockSpec(memory_space=pltpu.VMEM)],
            out_specs=pl.BlockSpec(memory_space=pltpu.VMEM),
            out_shape=jax.ShapeDtypeStruct((16, 128), array.dtype),
            compiler_params=pltpu.CompilerParams(vmem_limit_bytes=VMEM),
            cost_estimate=pl.CostEstimate(flops=LONG, bytes_accessed=1000, transcendentals=0),
            name="touch",
        )(array)

    def exchange(rows, run):
        two, one, three = (take(rows, "y", by) for by in (2, 1, 3))
        two, touched = lax.optimization_barrier((two, touch(weights)))
        kept, two_part = run(two, [], 3 * row_count, 1000, [touched])
        across = give(two_part, "y", 2)
        both = jnp.concatenate([one, three], axis=0)
        kept, both_part = run(both, kept, 0, LONG)
        from_one = give(both_part[:row_count], "y", 1)
        from_three = give(both_part[row_count:], "y", 3)
        *kept, across, both = lax.optimization_barrier((*kept, across, both))
        kept, own_part = run(rows, kept, 2 * row_count, LONG)
        ring = jnp.concatenate([ordered(both, own_part, from_one, from_three), rows, two], axis=0)
        return kept, [own_part, from_one, across, from_three], ring

    def forward(rows, kept, at, cost, unread=()):
        *kept, part = feed_call(feed_body, rows, weights, [], kept, at, 3, cost, "feed", unread)
        return kept, part

    kept, terms, feed_ring = exchange(feed_input, forward)
    hidden, value, slope = kept
    finish = blocks_call(
        down_body,
        [
            ((row_count, model_width), low),
            ((row_count, model_width), low),
            ((8, model_width), wide),
        ],
        "finish",
    )
    layer_output, down_grad, output_gain_rows = finish(
        *terms, state, cotangent, valid, one_output
    )

    def backward(rows, kept, at, cost):
        *kept, part = feed_call(
            feed_back_body, rows, weights, [value, slope], kept, at, 2, cost, "feed_back"
        )
        return kept, part

    rows72 = gain_shard
    two, one, three = (take(down_grad, "y", by) for by in (2, 1, 3))
    kept, own_part = backward(down_grad, [], 2 * row_count, 1000)
    kept, two_part = backward(two, kept, 3 * row_count, 1000)
    across = give(two_part, "y", 2)
    both = jnp.concatenate([one, three], axis=0)
    (gate_grad, up_grad), both_part = backward(both, kept, 0, LONG)
    from_one = give(both_part[:row_count], "y", 1)
    from_three = give(both_part[row_count:], "y", 3)
    across, both, gate_grad, up_grad = lax.optimization_barrier((across, both, gate_grad, up_grad))
    down_ring = jnp.concatenate([both, down_grad, two], axis=0)
    down_halves = product(core, down_ring, hidden)
    terms = [own_part, from_one, across, from_three]
    gate_halves = product(core, ordered(feed_ring, down_halves[0]), gate_grad)
    up_halves = product(
        core,
        ordered(feed_ring, gate_halves[0]),
        up_grad,
    )
    halves = [*gate_halves, *up_halves, *down_halves]
    spread_shape = (16, rows72, FEED_SLICE * 3 // 2)
    spread_in = pl.pallas_call(
        spread_in_body,
        grid=(4,),
        in_specs=[pl.BlockSpec((2 * rows72, FEED_SLICE), lambda i: (i, 0))] * 6,
        out_specs=pl.BlockSpec((4, *spread_shape[1:]), lambda i: (i, 0, 0)),
        out_shape=jax.ShapeDtypeStruct(spread_shape, low),
        compiler_params=pltpu.CompilerParams(vmem_limit_bytes=VMEM),
        cost_estimate=SMALL,
        name="spread_in",
    )(*halves)
    feed_sum = lax.psum_scatter(spread_in, ("z", "xh", "xl"), scatter_dimension=0, tiled=False)
    back = blocks_call(
        state_body,
        [
            ((row_count, model_width), low),
            ((row_count, model_width), wide),
            ((16, model_width), wide),
        ],
        "state_back",
        VMEM,
        36000000000,
    )
    attention_grad, state_grad, state_gain_rows = back(
        *terms, state, attention_raw, cotangent, valid, one_feed, one_attention
    )

    def whole(shape):
        return pl.BlockSpec(shape, lambda i: (0,) * len(shape))

    def head_columns(rows):
        return pl.BlockSpec((rows, head_size), lambda i: (0, i))

    smem = pl.BlockSpec(memory_space=pltpu.SMEM)
    pair_block = whole((row_count, 2 * head_size))
    table = whole((row_count, head_size // 2))
    attend_back = pl.pallas_call(
        attend_back_body,
        grid=(head_count,),
        in_specs=[
            smem,
            whole((row_count, model_width)),
            head_columns(model_width),
            head_columns(row_count),
            pair_block,
            pair_block,
            pair_block,
            whole((8, row_count)),
            head_columns(row_count),
            whole((8, head_size)),
            table,
            table,
        ],
        out_specs=[
            pair_block,
            pair_block,
            pair_block,
            head_columns(row_count),
            whole((8, head_size)),
        ],
        out_shape=[
            jax.ShapeDtypeStruct((row_count, 2 * head_size), low),
            jax.ShapeDtypeStruct((row_count, 2 * head_size), low),
            jax.ShapeDtypeStruct((row_count, 2 * head_size), wide),
            jax.ShapeDtypeStruct((row_count, query_width), low),
            jax.ShapeDtypeStruct((8, head_size), wide),
        ],
        scratch_shapes=[pltpu.VMEM((3, row_count, head_size), wide)] * 2,
        compiler_params=pltpu.CompilerParams(vmem_limit_bytes=MOST),
        cost_estimate=pl.CostEstimate(flops=100 * 10**9, bytes_accessed=1000, transcendentals=0),
        name="attend_back",
    )
    far_grad, near_grad, own_grad, query_grad, query_gain_rows = attend_back(
        place,
        attention_grad,
        full_out,
        query_low,
        far_pair,
        near_pair,
        local_pair,
        log_total,
        qkv_raw,
        head_gain,
        cosine,
        sine,
    )
    near_back = from_behind(near_grad, -1)
    far_back = from_behind(far_grad, -2)
    out_halves = product(core, ordered(attention_grad, near_grad), context_low, cost=LONG)
    out_block = whole((model_width // 2, query_width))
    cut_shape = (4, row_count + 384, qkv_width // 4)
    pair_back = pl.pallas_call(
        pair_back_body,
        grid=(1,),
        in_specs=[
            whole((row_count, query_width)),
            pair_block,
            pair_block,
            pair_block,
            pl.BlockSpec((row_count, head_size), lambda i: (0, head_count)),
            whole((8, head_size)),
            table,
            table,
            out_block,
            out_block,
        ],
        out_specs=[pair_block, whole(cut_shape), whole((8, head_size))],
        out_shape=[
            jax.ShapeDtypeStruct((row_count, 2 * head_size), low),
            jax.ShapeDtypeStruct(cut_shape, low),
            jax.ShapeDtypeStruct((8, head_size), wide),
        ],
        compiler_params=pltpu.CompilerParams(vmem_limit_bytes=MOST),
        cost_estimate=SMALL,
        name="pair_back",
    )
    pair_grad, qkv_cut, key_gain_rows = pair_back(
        query_grad, own_grad, near_back, far_back, qkv_raw, head_gain, cosine, sine, *out_halves
    )
    pieces = [give(pick(qkv_cut, (y + by) % 4, 0), "y", by) for by in (3, 2, 1)]
    qkv_ring, out_sum = rows_call(
        arrive_body,
        [((4 * row_count, qkv_width // 4), low), ((model_width // 2, query_width // 4), low)],
        "arrive",
    )(pick(qkv_cut, y, 0), *pieces)
    input_back = rows_call(
        input_body,
        [((row_count, model_width), low), ((8, model_width), wide)],
        "input_back",
    )
    tokens_grad, input_gain_rows = input_back(
        query_grad, pair_grad, full_qkv, tokens, state_grad, one_input
    )

    def spread_head(vector):
        return jnp.pad(
            vector.reshape(16, head_shard), ((0, 0), (0, gain_shard - head_shard))
        ).reshape(model_width)

    gain_block = jnp.stack(
        [
            input_gain_rows[0],
            state_gain_rows[8],
            state_gain_rows[0],
            output_gain_rows[0],
            spread_head(query_gain_rows[0]),
            spread_head(key_gain_rows[0]),
        ],
        axis=1,
    )
    gain_block = jnp.pad(gain_block, ((0, 0), (0, 122)))
    z = lax.axis_index("z")
    xh = lax.axis_index("xh")
    offsets = jnp.stack(
        [(((z + i) % 4) * 2 + (xh + j) % 2) * rows72 for i in range(4) for j in range(2)]
    ).astype(jnp.int32)
    columns = qkv_width // 4 + 128 + query_width // 4
    parts = pl.pallas_call(
        chip_body,
        in_specs=[pl.BlockSpec(memory_space=pltpu.SMEM)]
        + [pl.BlockSpec(memory_space=pltpu.VMEM)] * 3,
        out_specs=[pl.BlockSpec(memory_space=pltpu.VMEM)] * 4,
        out_shape=[jax.ShapeDtypeStruct((2, rows72, columns), low)] * 4,
        scratch_shapes=[pltpu.VMEM((model_width // 2, columns), wide)],
        compiler_params=pltpu.CompilerParams(vmem_limit_bytes=VMEM),
        cost_estimate=SMALL,
        name="chip",
    )(offsets, *product(core, input_ring, qkv_ring, gain_block), out_sum)
    total = parts[0].astype(wide)
    for by in (1, 3, 2):
        total = total + give(parts[by], "z", by).astype(wide)
    attention_column = total.astype(low)
    attention_half = (
        attention_column[0].astype(wide) + swap_x(attention_column[1]).astype(wide)
    ).astype(low)
    attention_sum = (
        attention_half.astype(wide) + give(attention_half, "xl", 1).astype(wide)
    ).astype(low)
    attention_blocks = in_order(
        [attention_sum] + [take(attention_sum, "y", by) for by in (1, 2, 3)]
    )
    feed_sums = lax.all_gather(ordered(feed_sum, parts[0]), SEQ, axis=0, tiled=False)
    gate_weight_grad, up_weight_grad, down_weight_grad = rows_call(
        spread_out_body, [((rows72, feed_width), wide)] * 3, "spread_out"
    )(feed_sums)
    qkv_cols = qkv_width // 4
    out_cols = query_width // 4
    qkv_weight_grad = jnp.concatenate([b[:, :qkv_cols] for b in attention_blocks], axis=1)
    out_weight_grad = jnp.concatenate([b[:, qkv_cols + 128 :] for b in attention_blocks], axis=1)
    gain_sum = sum(b[:, qkv_cols : qkv_cols + 128].astype(wide) for b in attention_blocks)
    return (
        layer_output,
        tokens_grad,
        qkv_weight_grad[:, :query_width].astype(wide),
        qkv_weight_grad[:, query_width : query_width + head_size].astype(wide),
        qkv_weight_grad[:, query_width + head_size :].astype(wide),
        out_weight_grad.astype(wide),
        gate_weight_grad,
        up_weight_grad,
        down_weight_grad,
        gain_sum[:, 0],
        gain_sum[:head_shard, 4],
        gain_sum[:head_shard, 5],
        gain_sum[:, 1],
        gain_sum[:, 2],
        gain_sum[:, 3],
    )


def solution(mesh):
    fine = Mesh(mesh.devices.reshape(SIZES), AXES)
    rows = P(AXES, None)
    matrix = P(DP, None)
    vector = P(DP)
    return jax.shard_map(
        local,
        mesh=fine,
        in_specs=(rows, rows, vector) + (matrix,) * 7 + (vector,) * 6,
        out_specs=(rows, rows) + (matrix,) * 7 + (vector,) * 6,
        check_vma=False,
    )
```

```python
import functools
import math

import jax
import jax.numpy as jnp
from jax import lax
from jax.experimental import pallas as pl
from jax.experimental.pallas import tpu as pltpu
from jax.sharding import Mesh
from jax.sharding import PartitionSpec as P

EPSILON = 1e-06
GELU_COEFF = 0.044715
AXES = ("z", "xh", "core", "xl", "y")
SIZES = (4, 2, 2, 2, 4)
DP = ("z", "xh", "core")
SEQ = ("xl", "y")
FEED_SLICE = 1792
FEED_TILES = ((0, 1024), (1024, 768))
HEADS = 4
HEAD = 256
SCALE = HEAD**-0.5
ROWS = 256
VMEM = 16 * 1024 * 1024
MOST = 56 * 1024 * 1024
LONG = 12 * 10**9
SMALL = pl.CostEstimate(flops=1000, bytes_accessed=1000, transcendentals=0)


def from_behind(array, by):
    pairs = [(i, i + by) for i in range(8) if 0 <= i + by < 8]
    return lax.ppermute(array, SEQ, pairs)


def take(array, axis, by):
    count = lax.axis_size(axis)
    return lax.ppermute(array, axis, [((i + by) % count, i) for i in range(count)])


def give(array, axis, by):
    count = lax.axis_size(axis)
    return lax.ppermute(array, axis, [(i, (i + by) % count) for i in range(count)])


def swap_x(array):
    return lax.ppermute(array, ("xh", "xl"), [(0, 3), (3, 0), (1, 2), (2, 1)])


def ordered(value, *after):
    return lax.optimization_barrier((value,) + after)[0]


def pick(array, index, axis):
    return lax.dynamic_index_in_dim(array, index, axis, keepdims=False)


def with_other_x(block, beside):
    xh = lax.axis_index("xh")
    return jnp.where(xh == 0, jnp.stack([block, beside]), jnp.stack([beside, block]))


def gather_rows(pair, wait=()):
    _, rows, width = pair.shape
    z = lax.axis_index("z")
    core = lax.axis_index("core")
    ring = [(take(pair, "z", by), by) for by in (1, 3, 2)]
    arrived = [piece for piece, _ in ring]
    own = jnp.zeros((4, 2, rows, width), pair.dtype)
    own = lax.dynamic_update_slice_in_dim(own, pair[None], z, 0)
    own = ordered(own, *wait)
    for piece, by in ring:
        own = lax.dynamic_update_slice_in_dim(own, piece[None], (z + by) % 4, 0)
    other = give(own, "core", 1)
    both = jnp.where(
        core == 0, jnp.stack([own, other], axis=2), jnp.stack([other, own], axis=2)
    )
    return both.reshape(16 * rows, width), arrived


def in_order(blocks):
    y = lax.axis_index("y")
    placed = []
    for place in range(4):
        value = blocks[(place - 3) % 4]
        for at in range(3):
            value = jnp.where(y == at, blocks[(place - at) % 4], value)
        placed.append(value)
    return placed


def inverse_rms(values):
    return lax.rsqrt(jnp.mean(values * values, axis=-1, keepdims=True) + EPSILON)


def rms_backward(values, scaling, upstream):
    inner = jnp.mean(upstream * values, axis=-1, keepdims=True)
    return scaling * (upstream - values * (scaling * scaling) * inner)


def rotary_tables(positions, head_size):
    half_size = head_size // 2
    exponents = lax.iota(jnp.float32, half_size) * (2.0 / head_size)
    frequency = jnp.power(10000.0, -exponents)
    angles = positions.astype(jnp.float32)[:, None] * frequency[None, :]
    return (jnp.cos(angles), jnp.sin(angles))


def gelu_parts(values):
    root_coeff = math.sqrt(2.0 / math.pi)
    square = values * values
    bend = jnp.tanh(values * (root_coeff + (root_coeff * GELU_COEFF) * square))
    part = 0.5 + 0.5 * bend
    gelu_value = values * part
    inner = root_coeff + (3.0 * GELU_COEFF * root_coeff) * square
    gelu_slope = part + gelu_value * (1.0 - bend) * inner
    return (gelu_value, gelu_slope)


def dot(left, right, left_axis=1, right_axis=0):
    return lax.dot_general(
        left,
        right,
        (((left_axis,), (right_axis,)), ((), ())),
        preferred_element_type=jnp.float32,
    )


def turn(first, second, cosine, sine):
    return first * cosine - second * sine, second * cosine + first * sine


def turn_back(first, second, cosine, sine):
    return first * cosine + second * sine, second * cosine - first * sine


def rows_call(body, outs, name, cost=1000):
    def call(*operands):
        specs = [
            pl.BlockSpec(memory_space=pltpu.SMEM)
            if operand.dtype == jnp.int32
            else pl.BlockSpec(memory_space=pltpu.VMEM)
            for operand in operands
        ]
        return pl.pallas_call(
            body,
            out_shape=[jax.ShapeDtypeStruct(shape, dtype) for shape, dtype in outs],
            in_specs=specs,
            out_specs=[pl.BlockSpec(memory_space=pltpu.VMEM) for _ in outs],
            compiler_params=pltpu.CompilerParams(vmem_limit_bytes=VMEM),
            cost_estimate=pl.CostEstimate(flops=cost, bytes_accessed=1000, transcendentals=0),
            name=name,
        )(*operands)

    return call


def blocks_call(body, outs, name, vmem=VMEM, cost=1000):
    steps = 4

    def spec(shape):
        if shape[0] < ROWS:
            return pl.BlockSpec(shape, lambda i: (0, 0))
        return pl.BlockSpec((shape[0] // steps, shape[1]), lambda i: (i, 0))

    def call(*operands):
        return pl.pallas_call(
            body,
            grid=(steps,),
            out_shape=[jax.ShapeDtypeStruct(shape, dtype) for shape, dtype in outs],
            in_specs=[spec(operand.shape) for operand in operands],
            out_specs=[spec(shape) for shape, _ in outs],
            compiler_params=pltpu.CompilerParams(vmem_limit_bytes=vmem),
            cost_estimate=pl.CostEstimate(flops=cost, bytes_accessed=1000, transcendentals=0),
            name=name,
        )(*operands)

    return call


def prepare_body(raw, gain, cosine, sine, query, pair):
    cos, sin = cosine[...], sine[...]
    half = HEAD // 2

    def finish(block, gains):
        hat = block * inverse_rms(block) * gains
        first, second = turn(hat[:, :half], hat[:, half:], cos, sin)
        return jnp.concatenate([first, second], axis=1).astype(jnp.bfloat16)

    for head in range(HEADS):
        at = slice(head * HEAD, (head + 1) * HEAD)
        query[:, at] = finish(raw[:, at], gain[0:1, :])
    keys = HEADS * HEAD
    pair[:, :HEAD] = finish(raw[:, keys : keys + HEAD], gain[1:2, :])
    pair[:, HEAD:] = raw[:, keys + HEAD : keys + 2 * HEAD].astype(jnp.bfloat16)


def attend_body(place, query, far, near, own, context, log_total):
    row = lax.broadcasted_iota(jnp.int32, (ROWS, ROWS), 0)
    column = lax.broadcasted_iota(jnp.int32, (ROWS, ROWS), 1)
    seq = place[0]
    allowed = (
        (row < column) & (seq >= 2),
        jnp.full((ROWS, ROWS), seq >= 1),
        column <= row,
    )
    blocks = (far, near, own)
    lane = lax.broadcasted_iota(jnp.int32, (ROWS, 128), 1)
    logs = jnp.zeros((ROWS, 128), jnp.float32)
    for head in range(HEADS):
        at = slice(head * HEAD, (head + 1) * HEAD)
        scores = [
            jnp.where(ok, dot(query[:, at], block[:, :HEAD], 1, 1) * SCALE, -1e30)
            for ok, block in zip(allowed, blocks)
        ]
        top = jnp.max(jnp.maximum(jnp.maximum(scores[0], scores[1]), scores[2]), 1, keepdims=True)
        terms = [jnp.exp(score - top) for score in scores]
        total = jnp.sum(terms[0] + terms[1] + terms[2], 1, keepdims=True)
        share = 1.0 / total
        out = sum(
            dot((term * share).astype(jnp.bfloat16), block[:, HEAD:])
            for term, block in zip(terms, blocks)
        )
        context[:, at] = out.astype(jnp.bfloat16)
        logs = jnp.where(lane == head, top + jnp.log(total), logs)
    log_total[...] = logs.T[:8]


def attend_back_body(
    place,
    upstream,
    out_weight,
    query,
    far,
    near,
    own,
    log_total,
    raw,
    gain,
    cosine,
    sine,
    far_grad,
    near_grad,
    own_grad,
    query_grad,
    gain_grad,
    key_sums,
    value_sums,
):
    low = jnp.bfloat16
    half = HEAD // 2
    head = pl.program_id(0)

    @pl.when(head == 0)
    def _():
        key_sums[...] = jnp.zeros_like(key_sums)
        value_sums[...] = jnp.zeros_like(value_sums)
        gain_grad[...] = jnp.zeros_like(gain_grad)

    key_at = lax.broadcasted_iota(jnp.int32, (ROWS, ROWS), 0)
    query_at = lax.broadcasted_iota(jnp.int32, (ROWS, ROWS), 1)
    seq = place[0]
    allowed = (
        (query_at < key_at) & (seq >= 2),
        jnp.full((ROWS, ROWS), seq >= 1),
        key_at <= query_at,
    )
    blocks = (far, near, own)
    context_grad = dot(upstream[...], out_weight[...]).astype(low)
    queries = query[...]
    logs = log_total[pl.ds(head, 1), :]
    probs = [
        jnp.where(ok, jnp.exp(dot(block[:, :HEAD], queries, 1, 1) * SCALE - logs), 0.0)
        for ok, block in zip(allowed, blocks)
    ]
    prob_grads = [dot(block[:, HEAD:], context_grad, 1, 1) for block in blocks]
    inner = jnp.sum(
        probs[0] * prob_grads[0] + probs[1] * prob_grads[1] + probs[2] * prob_grads[2],
        0,
        keepdims=True,
    )
    query_rot = 0.0
    for at_block, block in enumerate(blocks):
        score_grad = (probs[at_block] * (prob_grads[at_block] - inner)).astype(low)
        query_rot = query_rot + dot(score_grad, block[:, :HEAD], 0, 0)
        key_sums[at_block] += dot(score_grad, queries)
        value_sums[at_block] += dot(probs[at_block].astype(low), context_grad)
    query_rot = query_rot * SCALE
    first, second = turn_back(query_rot[:, :half], query_rot[:, half:], cosine[...], sine[...])
    upper = jnp.concatenate([first, second], axis=1)
    block = raw[...]
    scaling = inverse_rms(block)
    gain_grad[...] += jnp.broadcast_to(
        jnp.sum(upper * (block * scaling), 0, keepdims=True), (8, HEAD)
    )
    query_grad[...] = rms_backward(block, scaling, upper * gain[0:1, :]).astype(low)

    @pl.when(head == HEADS - 1)
    def _():
        for at_block, grad in enumerate((far_grad, near_grad, own_grad)):
            grad[:, :HEAD] = (key_sums[at_block] * SCALE).astype(grad.dtype)
            grad[:, HEAD:] = value_sums[at_block].astype(grad.dtype)


def pair_back_body(
    query, own, near, far, raw, gain, cosine, sine, out, out_got, pair_grad, cut, gain_grad
):
    half = HEAD // 2
    low = jnp.bfloat16
    total = own[...] + near[...].astype(jnp.float32) + far[...].astype(jnp.float32)
    first, second = turn_back(total[:, :half], total[:, half:HEAD], cosine[...], sine[...])
    upper = jnp.concatenate([first, second], axis=1)
    block = raw[...]
    scaling = inverse_rms(block)
    gain_sum = jnp.sum(upper * (block * scaling), 0, keepdims=True)
    gain_grad[...] = jnp.broadcast_to(gain_sum, (8, HEAD))
    keys = rms_backward(block, scaling, upper * gain[1:2, :]).astype(low)
    values = total[:, HEAD:].astype(low)
    pair_grad[:, :HEAD] = keys
    pair_grad[:, HEAD:] = values
    size = cut.shape[2]
    cut[0, :ROWS] = query[:, :size]
    cut[1, :ROWS] = query[:, size : 2 * size]
    cut[2, :ROWS] = jnp.concatenate([query[:, 2 * size :], keys[:, :half]], axis=1)
    cut[3, :ROWS] = jnp.concatenate([keys[:, half:], values], axis=1)
    for part in range(4):
        at = slice(part * HEAD, (part + 1) * HEAD)
        term = (out[:, at].astype(jnp.float32) + out_got[:, at].astype(jnp.float32)).astype(low)
        cut[part, ROWS:, :HEAD] = term[:384]
        cut[part, ROWS : ROWS + 192, HEAD:] = term[384:, :half]
        cut[part, ROWS + 192 :, HEAD:] = term[384:, half:]


def arrive_body(own, one, two, three, ring, out):
    wide = jnp.float32
    half = HEAD // 2
    for at, block in enumerate((own, one, two, three)):
        ring[at * ROWS : (at + 1) * ROWS] = block[:ROWS]
    total = sum(block[ROWS:].astype(wide) for block in (own, one, two, three)).astype(out.dtype)
    out[:384] = total[:, :HEAD]
    out[384:, :half] = total[:192, HEAD:]
    out[384:, half:] = total[192:, HEAD:]


def chip_body(offsets, here, got, out, *refs):
    *parts, total = refs
    wide = jnp.float32
    columns = here.shape[1]
    rows = parts[0].shape[1]
    total[:, :columns] = here[...].astype(wide) + got[...].astype(wide)
    total[:, columns:] = out[...].astype(wide)
    for at, part in enumerate(parts):
        for block in range(2):
            start = pl.multiple_of(offsets[2 * at + block], 8)
            part[block] = total[pl.ds(start, rows), :].astype(part.dtype)


def residual_body(
    context, out_weight, tokens, attention_gain, feed_gain, raw, state, feed_input
):
    value = dot(context[...], out_weight[...], 1, 1)
    raw[...] = value
    hidden = tokens[...].astype(jnp.float32) + value * inverse_rms(value) * attention_gain[...]
    state[...] = hidden
    feed_input[...] = (hidden * inverse_rms(hidden) * feed_gain[...]).astype(jnp.bfloat16)


def down_body(
    part, near, across, behind, state, cotangent, valid, gain, layer, down_grad, gain_grad
):
    wide = jnp.float32
    raw = (
        part[...].astype(wide)
        + near[...].astype(wide)
        + across[...].astype(wide)
        + behind[...].astype(wide)
    )
    scaling = inverse_rms(raw)
    hat = raw * scaling
    ok = valid[:, :1]
    layer[...] = (ok * (state[...] + hat * gain[...])).astype(jnp.bfloat16)
    upstream = cotangent[...].astype(wide) * ok

    @pl.when(pl.program_id(0) == 0)
    def _():
        gain_grad[...] = jnp.zeros_like(gain_grad)

    gain_grad[...] += jnp.broadcast_to(
        jnp.sum(upstream * hat, 0, keepdims=True), (8, hat.shape[1])
    )
    down_grad[...] = rms_backward(raw, scaling, upstream * gain[...]).astype(jnp.bfloat16)


def state_body(
    part,
    near,
    across,
    behind,
    state,
    raw,
    cotangent,
    valid,
    feed_gain,
    attention_gain,
    attention_grad,
    state_grad,
    gain_grads,
):
    wide = jnp.float32
    feed_grad = (
        part[...].astype(wide)
        + near[...].astype(wide)
        + across[...].astype(wide)
        + behind[...].astype(wide)
    )
    hidden = state[...]
    scaling = inverse_rms(hidden)
    upstream = cotangent[...].astype(wide) * valid[:, :1]
    total = upstream + rms_backward(hidden, scaling, feed_grad * feed_gain[...])
    state_grad[...] = total
    value = raw[...]
    value_scaling = inverse_rms(value)
    width = value.shape[1]

    @pl.when(pl.program_id(0) == 0)
    def _():
        gain_grads[...] = jnp.zeros_like(gain_grads)

    gain_grads[:8] += jnp.broadcast_to(
        jnp.sum(feed_grad * (hidden * scaling), 0, keepdims=True), (8, width)
    )
    gain_grads[8:] += jnp.broadcast_to(
        jnp.sum(total * (value * value_scaling), 0, keepdims=True), (8, width)
    )
    attention_grad[...] = rms_backward(value, value_scaling, total * attention_gain[...]).astype(
        jnp.bfloat16
    )


def input_body(
    query_grad, pair_grad, weight, tokens, state_grad, gain, tokens_grad, gain_grad
):
    queries = query_grad.shape[1]
    pairs = pair_grad.shape[1]
    grad = dot(query_grad[...], weight[:, :queries], 1, 1) + dot(
        pair_grad[...], weight[:, queries : queries + pairs], 1, 1
    )
    value = tokens[...].astype(jnp.float32)
    scaling = inverse_rms(value)
    gain_grad[...] = jnp.broadcast_to(
        jnp.sum(grad * (value * scaling), 0, keepdims=True), (8, value.shape[1])
    )
    tokens_grad[...] = (
        state_grad[...] + rms_backward(value, scaling, grad * gain[...])
    ).astype(jnp.bfloat16)


def feed_body(place, rows, weights, *refs):
    hidden_out, value_out, slope_out, part, total = refs[-5:]
    low = jnp.bfloat16
    for first, size in FEED_TILES:
        gate_at, up_at, down_at = (
            slice(start + first, start + first + size) for start in (0, FEED_SLICE, 2 * FEED_SLICE)
        )
        to = slice(place, place + rows.shape[0])
        gate_raw = dot(rows[...], weights[:, gate_at])
        up_raw = dot(rows[...], weights[:, up_at])
        value, slope = gelu_parts(gate_raw)
        hidden = (value * up_raw).astype(low)
        hidden_out[to, gate_at] = hidden
        value_out[to, gate_at] = value.astype(low)
        slope_out[to, gate_at] = (slope * up_raw).astype(low)
        term = dot(hidden, weights[:, down_at], 1, 1)
        total[...] = term if first == 0 else total[...] + term

    part[...] = total[...].astype(low)


def feed_back_body(place, rows, weights, value, slope, *refs):
    gate_out, up_out, part, total = refs[-4:]
    low = jnp.bfloat16
    for first, size in FEED_TILES:
        gate_at, up_at, down_at = (
            slice(start + first, start + first + size) for start in (0, FEED_SLICE, 2 * FEED_SLICE)
        )
        to = slice(place, place + rows.shape[0])
        hidden_grad = dot(rows[...], weights[:, down_at])
        gate_grad = (hidden_grad * slope[to, gate_at].astype(jnp.float32)).astype(low)
        up_grad = (hidden_grad * value[to, gate_at].astype(jnp.float32)).astype(low)
        gate_out[to, gate_at] = gate_grad
        up_out[to, gate_at] = up_grad
        term = dot(gate_grad, weights[:, gate_at], 1, 1) + dot(up_grad, weights[:, up_at], 1, 1)
        total[...] = term if first == 0 else total[...] + term

    part[...] = total[...].astype(low)


def feed_call(body, rows, weights, read, kept, place, outs, cost, name, unread=()):
    count, width = rows.shape
    operands = [rows, weights, *read, *kept, *unread]
    whole = pl.BlockSpec(memory_space=pltpu.VMEM)
    first_kept = 2 + len(read)
    return pl.pallas_call(
        functools.partial(body, place),
        in_specs=[whole] * first_kept
        + [pl.BlockSpec(memory_space=pl.ANY)] * (len(kept) + len(unread)),
        out_specs=[whole] * (outs + 1),
        out_shape=[jax.ShapeDtypeStruct((4 * ROWS, FEED_SLICE), jnp.bfloat16)] * outs
        + [jax.ShapeDtypeStruct((count, width), jnp.bfloat16)],
        scratch_shapes=[pltpu.VMEM((count, width), jnp.float32)],
        input_output_aliases={first_kept + i: i for i in range(len(kept))},
        compiler_params=pltpu.CompilerParams(vmem_limit_bytes=VMEM),
        cost_estimate=pl.CostEstimate(flops=cost, bytes_accessed=1000, transcendentals=0),
        name=name,
    )(*operands)


def product_body(core, left, right, *refs):
    away, here, total = refs[-3:]
    rows = left.shape[1] // 16
    width = right.shape[1]

    def split(to, first, columns):
        for two in range(4):
            pieces = [
                total[pl.ds(pl.multiple_of((4 * two + 2 * i + first) * rows, 8), rows), :columns]
                for i in (0, 1)
            ]
            yield slice(two * 2 * rows, (two + 1) * 2 * rows), jnp.concatenate(pieces, axis=0)

    for start in range(0, width, total.shape[1]):
        size = min(total.shape[1], width - start)
        at = slice(start, start + size)
        total[:, :size] = dot(left[...], right[:, at], 0, 0)
        for to, first in ((away, 1 - core[0]), (here, core[0])):
            for place, value in split(to, first, size):
                to[place, at] = value.astype(to.dtype)
    if len(refs) > 3:
        extra = refs[0]
        at = slice(width, width + extra.shape[1])
        total[:, : extra.shape[1]] = extra[...]
        for to, first in ((away, 1 - core[0]), (here, core[0])):
            for place, value in split(to, first, extra.shape[1]):
                to[place, at] = value.astype(to.dtype)


def product(core, left, right, *extra, cost=1000):
    width = right.shape[1] + sum(block.shape[1] for block in extra)
    out = jax.ShapeDtypeStruct((left.shape[1] // 2, width), jnp.bfloat16)
    whole = pl.BlockSpec(memory_space=pltpu.VMEM)
    away, here = pl.pallas_call(
        product_body,
        in_specs=[pl.BlockSpec(memory_space=pltpu.SMEM)] + [whole] * (2 + len(extra)),
        out_specs=[whole, whole],
        out_shape=[out, out],
        scratch_shapes=[pltpu.VMEM((left.shape[1], 512), jnp.float32)],
        compiler_params=pltpu.CompilerParams(vmem_limit_bytes=VMEM),
        cost_estimate=pl.CostEstimate(flops=cost, bytes_accessed=1000, transcendentals=0),
        name="product",
    )(core, left, right, *extra)
    return here, give(away, "core", 1)


def spread_in_body(gate, gate_got, up, up_got, down, down_got, spread):
    rows = spread.shape[1]
    half = FEED_SLICE // 2
    gates, ups, downs = (
        here[...].astype(jnp.float32) + got[...].astype(jnp.float32)
        for here, got in ((gate, gate_got), (up, up_got), (down, down_got))
    )
    for block in range(2):
        of = slice(block * rows, (block + 1) * rows)
        to = 2 * block
        spread[to, :, :FEED_SLICE] = gates[of].astype(spread.dtype)
        spread[to, :, FEED_SLICE:] = downs[of, :half].astype(spread.dtype)
        spread[to + 1, :, :FEED_SLICE] = ups[of].astype(spread.dtype)
        spread[to + 1, :, FEED_SLICE:] = downs[of, half:].astype(spread.dtype)


def spread_out_body(sums, gate, up, down):
    width = gate.shape[1]
    half = FEED_SLICE // 2
    for y in range(4):
        start = y * FEED_SLICE
        size = min(FEED_SLICE, width - start)
        gate[:, start : start + size] = sums[y, :, :size].astype(jnp.float32)
        up[:, start : start + size] = sums[4 + y, :, :size].astype(jnp.float32)
        for xl in range(2):
            first = start + xl * half
            size = min(half, width - first)
            down[:, first : first + size] = sums[
                4 * xl + y, :, FEED_SLICE : FEED_SLICE + size
            ].astype(jnp.float32)


def feed_slice(weight):
    y = lax.axis_index("y")
    padded = jnp.pad(weight, ((0, 0), (0, 4 * FEED_SLICE - weight.shape[1])))
    return lax.dynamic_slice_in_dim(padded, y * FEED_SLICE, FEED_SLICE, 1)


def local(
    tokens,
    cotangent,
    lengths,
    query_weight,
    key_weight,
    value_weight,
    out_weight,
    gate_weight,
    up_weight,
    down_weight,
    input_gain,
    query_gain,
    key_gain,
    attention_gain,
    feedforward_gain,
    output_gain,
):
    low = jnp.bfloat16
    wide = jnp.float32
    row_count, model_width = tokens.shape
    head_size = key_weight.shape[1]
    head_count = query_weight.shape[1] // head_size
    query_width = head_count * head_size
    qkv_width = query_width + 2 * head_size
    feed_width = gate_weight.shape[1]
    gain_shard = input_gain.shape[0]
    head_shard = query_gain.shape[0]
    y = lax.axis_index("y")
    seq_index = lax.axis_index("xl") * 4 + y
    place = seq_index.reshape(1).astype(jnp.int32)
    core = lax.axis_index("core").reshape(1).astype(jnp.int32)
    positions = seq_index * row_count + lax.iota(jnp.int32, row_count)
    valid = jnp.broadcast_to((positions < lengths[0]).astype(wide)[:, None], (row_count, 128))
    cosine, sine = rotary_tables(positions, head_size)

    def spread(vector):
        return jnp.pad(vector, (0, gain_shard - head_shard))

    gain_columns = jnp.stack(
        [
            input_gain,
            attention_gain,
            feedforward_gain,
            output_gain,
            spread(query_gain),
            spread(key_gain),
        ],
        axis=1,
    )
    gain_columns = jnp.pad(gain_columns, ((0, 0), (0, 122)))
    feed_weights = lax.all_gather(
        jnp.concatenate(
            [feed_slice(gate_weight), feed_slice(up_weight), feed_slice(down_weight)], axis=1
        ),
        DP,
        axis=0,
        tiled=True,
    )
    attention_weights = jnp.concatenate(
        [query_weight, key_weight, value_weight, gain_columns, out_weight], axis=1
    )
    beside = swap_x(attention_weights)
    qkv_columns = qkv_width + gain_columns.shape[1]
    tokens_ring = [take(ordered(tokens, beside), "y", by) for by in (1, 2, 3)]
    full_qkv, arrived = gather_rows(
        with_other_x(attention_weights[:, :qkv_columns], beside[:, :qkv_columns]), tokens_ring
    )
    gains = 1.0 + full_qkv[:, qkv_width : qkv_width + 8].astype(wide).T
    one_input, one_attention, one_feed, one_output = (gains[i : i + 1] for i in range(4))
    head_gain = gains.reshape(8, 16, gain_shard)[4:6, :, :head_shard].reshape(2, head_size)
    head_gain = jnp.pad(head_gain, ((0, 6), (0, 0)))

    def attention_input_of(rows):
        values = rows.astype(wide)
        return (values * inverse_rms(values) * one_input).astype(low)

    attention_input = attention_input_of(tokens)
    qkv_raw = jnp.dot(attention_input, full_qkv[:, :qkv_width], preferred_element_type=wide)
    prepare = rows_call(
        prepare_body,
        [((row_count, query_width), low), ((row_count, 2 * head_size), low)],
        "prepare",
    )
    query_low, local_pair = prepare(qkv_raw, head_gain, cosine, sine)
    near_pair, far_pair = (from_behind(local_pair, distance) for distance in (1, 2))
    input_ring = attention_input_of(
        jnp.concatenate([ordered(tokens, local_pair)] + tokens_ring, axis=0)
    )
    out_pair = with_other_x(out_weight, beside[:, qkv_columns:])
    full_out, _ = gather_rows(ordered(out_pair, *arrived), (input_ring,))
    near_pair, far_pair, input_ring = lax.optimization_barrier((near_pair, far_pair, input_ring))
    attend = rows_call(
        attend_body,
        [((row_count, query_width), low), ((8, row_count), wide)],
        "attend",
        12 * 10**9,
    )
    context_low, log_total = attend(place, query_low, far_pair, near_pair, local_pair)
    residual = rows_call(
        residual_body,
        [
            ((row_count, model_width), wide),
            ((row_count, model_width), wide),
            ((row_count, model_width), low),
        ],
        "residual",
    )
    attention_raw, state, feed_input = residual(
        context_low, full_out, tokens, one_attention, one_feed
    )

    weights, feed_input = lax.optimization_barrier((feed_weights, feed_input))

    def touch(array):
        def body(whole, some):
            some[...] = whole[:16, :128]

        return pl.pallas_call(
            body,
            in_specs=[pl.BlockSpec(memory_space=pltpu.VMEM)],
            out_specs=pl.BlockSpec(memory_space=pltpu.VMEM),
            out_shape=jax.ShapeDtypeStruct((16, 128), array.dtype),
            compiler_params=pltpu.CompilerParams(vmem_limit_bytes=VMEM),
            cost_estimate=pl.CostEstimate(flops=LONG, bytes_accessed=1000, transcendentals=0),
            name="touch",
        )(array)

    def exchange(rows, run):
        two, one, three = (take(rows, "y", by) for by in (2, 1, 3))
        two, touched = lax.optimization_barrier((two, touch(weights)))
        kept, two_part = run(two, [], 3 * row_count, 1000, [touched])
        across = give(two_part, "y", 2)
        both = jnp.concatenate([one, three], axis=0)
        kept, both_part = run(both, kept, 0, LONG)
        from_one = give(both_part[:row_count], "y", 1)
        from_three = give(both_part[row_count:], "y", 3)
        *kept, across, both = lax.optimization_barrier((*kept, across, both))
        kept, own_part = run(rows, kept, 2 * row_count, LONG)
        ring = jnp.concatenate([ordered(both, own_part, from_one, from_three), rows, two], axis=0)
        return kept, [own_part, from_one, across, from_three], ring

    def forward(rows, kept, at, cost, unread=()):
        *kept, part = feed_call(feed_body, rows, weights, [], kept, at, 3, cost, "feed", unread)
        return kept, part

    kept, terms, feed_ring = exchange(feed_input, forward)
    hidden, value, slope = kept
    finish = blocks_call(
        down_body,
        [
            ((row_count, model_width), low),
            ((row_count, model_width), low),
            ((8, model_width), wide),
        ],
        "finish",
    )
    layer_output, down_grad, output_gain_rows = finish(
        *terms, state, cotangent, valid, one_output
    )

    def backward(rows, kept, at, cost):
        *kept, part = feed_call(
            feed_back_body, rows, weights, [value, slope], kept, at, 2, cost, "feed_back"
        )
        return kept, part

    rows72 = gain_shard
    two, one, three = (take(down_grad, "y", by) for by in (2, 1, 3))
    kept, own_part = backward(down_grad, [], 2 * row_count, 1000)
    kept, two_part = backward(two, kept, 3 * row_count, 1000)
    across = give(two_part, "y", 2)
    both = jnp.concatenate([one, three], axis=0)
    (gate_grad, up_grad), both_part = backward(both, kept, 0, LONG)
    from_one = give(both_part[:row_count], "y", 1)
    from_three = give(both_part[row_count:], "y", 3)
    across, both, gate_grad, up_grad = lax.optimization_barrier((across, both, gate_grad, up_grad))
    down_ring = jnp.concatenate([both, down_grad, two], axis=0)
    down_halves = product(core, down_ring, hidden)
    terms = [own_part, from_one, across, from_three]
    gate_halves = product(core, ordered(feed_ring, down_halves[0]), gate_grad)
    up_halves = product(
        core,
        ordered(feed_ring, gate_halves[0]),
        up_grad,
    )
    halves = [*gate_halves, *up_halves, *down_halves]
    spread_shape = (16, rows72, FEED_SLICE * 3 // 2)
    spread_in = pl.pallas_call(
        spread_in_body,
        grid=(4,),
        in_specs=[pl.BlockSpec((2 * rows72, FEED_SLICE), lambda i: (i, 0))] * 6,
        out_specs=pl.BlockSpec((4, *spread_shape[1:]), lambda i: (i, 0, 0)),
        out_shape=jax.ShapeDtypeStruct(spread_shape, low),
        compiler_params=pltpu.CompilerParams(vmem_limit_bytes=VMEM),
        cost_estimate=SMALL,
        name="spread_in",
    )(*halves)
    feed_sum = lax.psum_scatter(spread_in, ("z", "xh", "xl"), scatter_dimension=0, tiled=False)
    back = blocks_call(
        state_body,
        [
            ((row_count, model_width), low),
            ((row_count, model_width), wide),
            ((16, model_width), wide),
        ],
        "state_back",
        VMEM,
        36000000000,
    )
    attention_grad, state_grad, state_gain_rows = back(
        *terms, state, attention_raw, cotangent, valid, one_feed, one_attention
    )

    def whole(shape):
        return pl.BlockSpec(shape, lambda i: (0,) * len(shape))

    def head_columns(rows):
        return pl.BlockSpec((rows, head_size), lambda i: (0, i))

    smem = pl.BlockSpec(memory_space=pltpu.SMEM)
    pair_block = whole((row_count, 2 * head_size))
    table = whole((row_count, head_size // 2))
    attend_back = pl.pallas_call(
        attend_back_body,
        grid=(head_count,),
        in_specs=[
            smem,
            whole((row_count, model_width)),
            head_columns(model_width),
            head_columns(row_count),
            pair_block,
            pair_block,
            pair_block,
            whole((8, row_count)),
            head_columns(row_count),
            whole((8, head_size)),
            table,
            table,
        ],
        out_specs=[
            pair_block,
            pair_block,
            pair_block,
            head_columns(row_count),
            whole((8, head_size)),
        ],
        out_shape=[
            jax.ShapeDtypeStruct((row_count, 2 * head_size), low),
            jax.ShapeDtypeStruct((row_count, 2 * head_size), low),
            jax.ShapeDtypeStruct((row_count, 2 * head_size), wide),
            jax.ShapeDtypeStruct((row_count, query_width), low),
            jax.ShapeDtypeStruct((8, head_size), wide),
        ],
        scratch_shapes=[pltpu.VMEM((3, row_count, head_size), wide)] * 2,
        compiler_params=pltpu.CompilerParams(vmem_limit_bytes=MOST),
        cost_estimate=pl.CostEstimate(flops=100 * 10**9, bytes_accessed=1000, transcendentals=0),
        name="attend_back",
    )
    far_grad, near_grad, own_grad, query_grad, query_gain_rows = attend_back(
        place,
        attention_grad,
        full_out,
        query_low,
        far_pair,
        near_pair,
        local_pair,
        log_total,
        qkv_raw,
        head_gain,
        cosine,
        sine,
    )
    near_back = from_behind(near_grad, -1)
    far_back = from_behind(far_grad, -2)
    out_halves = product(core, ordered(attention_grad, near_grad), context_low, cost=LONG)
    out_block = whole((model_width // 2, query_width))
    cut_shape = (4, row_count + 384, qkv_width // 4)
    pair_back = pl.pallas_call(
        pair_back_body,
        grid=(1,),
        in_specs=[
            whole((row_count, query_width)),
            pair_block,
            pair_block,
            pair_block,
            pl.BlockSpec((row_count, head_size), lambda i: (0, head_count)),
            whole((8, head_size)),
            table,
            table,
            out_block,
            out_block,
        ],
        out_specs=[pair_block, whole(cut_shape), whole((8, head_size))],
        out_shape=[
            jax.ShapeDtypeStruct((row_count, 2 * head_size), low),
            jax.ShapeDtypeStruct(cut_shape, low),
            jax.ShapeDtypeStruct((8, head_size), wide),
        ],
        compiler_params=pltpu.CompilerParams(vmem_limit_bytes=MOST),
        cost_estimate=SMALL,
        name="pair_back",
    )
    pair_grad, qkv_cut, key_gain_rows = pair_back(
        query_grad, own_grad, near_back, far_back, qkv_raw, head_gain, cosine, sine, *out_halves
    )
    pieces = [give(pick(qkv_cut, (y + by) % 4, 0), "y", by) for by in (3, 2, 1)]
    qkv_ring, out_sum = rows_call(
        arrive_body,
        [((4 * row_count, qkv_width // 4), low), ((model_width // 2, query_width // 4), low)],
        "arrive",
    )(pick(qkv_cut, y, 0), *pieces)
    input_back = rows_call(
        input_body,
        [((row_count, model_width), low), ((8, model_width), wide)],
        "input_back",
    )
    tokens_grad, input_gain_rows = input_back(
        query_grad, pair_grad, full_qkv, tokens, state_grad, one_input
    )

    def spread_head(vector):
        return jnp.pad(
            vector.reshape(16, head_shard), ((0, 0), (0, gain_shard - head_shard))
        ).reshape(model_width)

    gain_block = jnp.stack(
        [
            input_gain_rows[0],
            state_gain_rows[8],
            state_gain_rows[0],
            output_gain_rows[0],
            spread_head(query_gain_rows[0]),
            spread_head(key_gain_rows[0]),
        ],
        axis=1,
    )
    gain_block = jnp.pad(gain_block, ((0, 0), (0, 122)))
    z = lax.axis_index("z")
    xh = lax.axis_index("xh")
    offsets = jnp.stack(
        [(((z + i) % 4) * 2 + (xh + j) % 2) * rows72 for i in range(4) for j in range(2)]
    ).astype(jnp.int32)
    columns = qkv_width // 4 + 128 + query_width // 4
    parts = pl.pallas_call(
        chip_body,
        in_specs=[pl.BlockSpec(memory_space=pltpu.SMEM)]
        + [pl.BlockSpec(memory_space=pltpu.VMEM)] * 3,
        out_specs=[pl.BlockSpec(memory_space=pltpu.VMEM)] * 4,
        out_shape=[jax.ShapeDtypeStruct((2, rows72, columns), low)] * 4,
        scratch_shapes=[pltpu.VMEM((model_width // 2, columns), wide)],
        compiler_params=pltpu.CompilerParams(vmem_limit_bytes=VMEM),
        cost_estimate=SMALL,
        name="chip",
    )(offsets, *product(core, input_ring, qkv_ring, gain_block), out_sum)
    total = parts[0].astype(wide)
    for by in (1, 3, 2):
        total = total + give(parts[by], "z", by).astype(wide)
    attention_column = total.astype(low)
    attention_half = (
        attention_column[0].astype(wide) + swap_x(attention_column[1]).astype(wide)
    ).astype(low)
    attention_sum = (
        attention_half.astype(wide) + give(attention_half, "xl", 1).astype(wide)
    ).astype(low)
    attention_blocks = in_order(
        [attention_sum] + [take(attention_sum, "y", by) for by in (1, 2, 3)]
    )
    feed_sums = lax.all_gather(ordered(feed_sum, parts[0]), SEQ, axis=0, tiled=False)
    gate_weight_grad, up_weight_grad, down_weight_grad = rows_call(
        spread_out_body, [((rows72, feed_width), wide)] * 3, "spread_out"
    )(feed_sums)
    qkv_cols = qkv_width // 4
    out_cols = query_width // 4
    qkv_weight_grad = jnp.concatenate([b[:, :qkv_cols] for b in attention_blocks], axis=1)
    out_weight_grad = jnp.concatenate([b[:, qkv_cols + 128 :] for b in attention_blocks], axis=1)
    gain_sum = sum(b[:, qkv_cols : qkv_cols + 128].astype(wide) for b in attention_blocks)
    return (
        layer_output,
        tokens_grad,
        qkv_weight_grad[:, :query_width].astype(wide),
        qkv_weight_grad[:, query_width : query_width + head_size].astype(wide),
        qkv_weight_grad[:, query_width + head_size :].astype(wide),
        out_weight_grad.astype(wide),
        gate_weight_grad,
        up_weight_grad,
        down_weight_grad,
        gain_sum[:, 0],
        gain_sum[:head_shard, 4],
        gain_sum[:head_shard, 5],
        gain_sum[:, 1],
        gain_sum[:, 2],
        gain_sum[:, 3],
    )


def solution(mesh):
    fine = Mesh(mesh.devices.reshape(SIZES), AXES)
    rows = P(AXES, None)
    matrix = P(DP, None)
    vector = P(DP)
    return jax.shard_map(
        local,
        mesh=fine,
        in_specs=(rows, rows, vector) + (matrix,) * 7 + (vector,) * 6,
        out_specs=(rows, rows) + (matrix,) * 7 + (vector,) * 6,
        check_vma=False,
    )
```

```python
import functools
import math

import jax
import jax.numpy as jnp
from jax import lax
from jax.experimental import pallas as pl
from jax.experimental.pallas import tpu as pltpu
from jax.sharding import Mesh
from jax.sharding import PartitionSpec as P

EPSILON = 1e-06
GELU_COEFF = 0.044715
AXES = ("z", "xh", "core", "xl", "y")
SIZES = (4, 2, 2, 2, 4)
DP = ("z", "xh", "core")
SEQ = ("xl", "y")
FEED_SLICE = 1792
FEED_TILES = ((0, 1024), (1024, 768))
HEADS = 4
HEAD = 256
SCALE = HEAD**-0.5
ROWS = 256
VMEM = 16 * 1024 * 1024
MOST = 56 * 1024 * 1024
LONG = 12 * 10**9
SMALL = pl.CostEstimate(flops=1000, bytes_accessed=1000, transcendentals=0)


def from_behind(array, by):
    pairs = [(i, i + by) for i in range(8) if 0 <= i + by < 8]
    return lax.ppermute(array, SEQ, pairs)


def take(array, axis, by):
    count = lax.axis_size(axis)
    return lax.ppermute(array, axis, [((i + by) % count, i) for i in range(count)])


def give(array, axis, by):
    count = lax.axis_size(axis)
    return lax.ppermute(array, axis, [(i, (i + by) % count) for i in range(count)])


def swap_x(array):
    return lax.ppermute(array, ("xh", "xl"), [(0, 3), (3, 0), (1, 2), (2, 1)])


def ordered(value, *after):
    return lax.optimization_barrier((value,) + after)[0]


def pick(array, index, axis):
    return lax.dynamic_index_in_dim(array, index, axis, keepdims=False)


def with_other_x(block, beside):
    xh = lax.axis_index("xh")
    return jnp.where(xh == 0, jnp.stack([block, beside]), jnp.stack([beside, block]))


def gather_rows(pair, wait=()):
    _, rows, width = pair.shape
    z = lax.axis_index("z")
    core = lax.axis_index("core")
    ring = [(take(pair, "z", by), by) for by in (1, 3, 2)]
    arrived = [piece for piece, _ in ring]
    own = jnp.zeros((4, 2, rows, width), pair.dtype)
    own = lax.dynamic_update_slice_in_dim(own, pair[None], z, 0)
    own = ordered(own, *wait)
    for piece, by in ring:
        own = lax.dynamic_update_slice_in_dim(own, piece[None], (z + by) % 4, 0)
    other = give(own, "core", 1)
    both = jnp.where(
        core == 0, jnp.stack([own, other], axis=2), jnp.stack([other, own], axis=2)
    )
    return both.reshape(16 * rows, width), arrived


def in_order(blocks):
    y = lax.axis_index("y")
    placed = []
    for place in range(4):
        value = blocks[(place - 3) % 4]
        for at in range(3):
            value = jnp.where(y == at, blocks[(place - at) % 4], value)
        placed.append(value)
    return placed


def inverse_rms(values):
    return lax.rsqrt(jnp.mean(values * values, axis=-1, keepdims=True) + EPSILON)


def rms_backward(values, scaling, upstream):
    inner = jnp.mean(upstream * values, axis=-1, keepdims=True)
    return scaling * (upstream - values * (scaling * scaling) * inner)


def rotary_tables(positions, head_size):
    half_size = head_size // 2
    exponents = lax.iota(jnp.float32, half_size) * (2.0 / head_size)
    frequency = jnp.power(10000.0, -exponents)
    angles = positions.astype(jnp.float32)[:, None] * frequency[None, :]
    return (jnp.cos(angles), jnp.sin(angles))


def gelu_parts(values):
    root_coeff = math.sqrt(2.0 / math.pi)
    square = values * values
    bend = jnp.tanh(values * (root_coeff + (root_coeff * GELU_COEFF) * square))
    part = 0.5 + 0.5 * bend
    gelu_value = values * part
    inner = root_coeff + (3.0 * GELU_COEFF * root_coeff) * square
    gelu_slope = part + gelu_value * (1.0 - bend) * inner
    return (gelu_value, gelu_slope)


def dot(left, right, left_axis=1, right_axis=0):
    return lax.dot_general(
        left,
        right,
        (((left_axis,), (right_axis,)), ((), ())),
        preferred_element_type=jnp.float32,
    )


def turn(first, second, cosine, sine):
    return first * cosine - second * sine, second * cosine + first * sine


def turn_back(first, second, cosine, sine):
    return first * cosine + second * sine, second * cosine - first * sine


def rows_call(body, outs, name, cost=1000):
    def call(*operands):
        specs = [
            pl.BlockSpec(memory_space=pltpu.SMEM)
            if operand.dtype == jnp.int32
            else pl.BlockSpec(memory_space=pltpu.VMEM)
            for operand in operands
        ]
        return pl.pallas_call(
            body,
            out_shape=[jax.ShapeDtypeStruct(shape, dtype) for shape, dtype in outs],
            in_specs=specs,
            out_specs=[pl.BlockSpec(memory_space=pltpu.VMEM) for _ in outs],
            compiler_params=pltpu.CompilerParams(vmem_limit_bytes=VMEM),
            cost_estimate=pl.CostEstimate(flops=cost, bytes_accessed=1000, transcendentals=0),
            name=name,
        )(*operands)

    return call


def blocks_call(body, outs, name, vmem=VMEM, cost=1000):
    steps = 4

    def spec(shape):
        if shape[0] < ROWS:
            return pl.BlockSpec(shape, lambda i: (0, 0))
        return pl.BlockSpec((shape[0] // steps, shape[1]), lambda i: (i, 0))

    def call(*operands):
        return pl.pallas_call(
            body,
            grid=(steps,),
            out_shape=[jax.ShapeDtypeStruct(shape, dtype) for shape, dtype in outs],
            in_specs=[spec(operand.shape) for operand in operands],
            out_specs=[spec(shape) for shape, _ in outs],
            compiler_params=pltpu.CompilerParams(vmem_limit_bytes=vmem),
            cost_estimate=pl.CostEstimate(flops=cost, bytes_accessed=1000, transcendentals=0),
            name=name,
        )(*operands)

    return call


def prepare_body(raw, gain, cosine, sine, query, pair):
    cos, sin = cosine[...], sine[...]
    half = HEAD // 2

    def finish(block, gains):
        hat = block * inverse_rms(block) * gains
        first, second = turn(hat[:, :half], hat[:, half:], cos, sin)
        return jnp.concatenate([first, second], axis=1).astype(jnp.bfloat16)

    for head in range(HEADS):
        at = slice(head * HEAD, (head + 1) * HEAD)
        query[:, at] = finish(raw[:, at], gain[0:1, :])
    keys = HEADS * HEAD
    pair[:, :HEAD] = finish(raw[:, keys : keys + HEAD], gain[1:2, :])
    pair[:, HEAD:] = raw[:, keys + HEAD : keys + 2 * HEAD].astype(jnp.bfloat16)


def attend_body(place, query, far, near, own, context, log_total):
    row = lax.broadcasted_iota(jnp.int32, (ROWS, ROWS), 0)
    column = lax.broadcasted_iota(jnp.int32, (ROWS, ROWS), 1)
    seq = place[0]
    allowed = (
        (row < column) & (seq >= 2),
        jnp.full((ROWS, ROWS), seq >= 1),
        column <= row,
    )
    blocks = (far, near, own)
    lane = lax.broadcasted_iota(jnp.int32, (ROWS, 128), 1)
    logs = jnp.zeros((ROWS, 128), jnp.float32)
    for head in range(HEADS):
        at = slice(head * HEAD, (head + 1) * HEAD)
        scores = [
            jnp.where(ok, dot(query[:, at], block[:, :HEAD], 1, 1) * SCALE, -1e30)
            for ok, block in zip(allowed, blocks)
        ]
        top = jnp.max(jnp.maximum(jnp.maximum(scores[0], scores[1]), scores[2]), 1, keepdims=True)
        terms = [jnp.exp(score - top) for score in scores]
        total = jnp.sum(terms[0] + terms[1] + terms[2], 1, keepdims=True)
        share = 1.0 / total
        out = sum(
            dot((term * share).astype(jnp.bfloat16), block[:, HEAD:])
            for term, block in zip(terms, blocks)
        )
        context[:, at] = out.astype(jnp.bfloat16)
        logs = jnp.where(lane == head, top + jnp.log(total), logs)
    log_total[...] = logs.T[:8]


def attend_back_body(
    place,
    upstream,
    out_weight,
    query,
    far,
    near,
    own,
    log_total,
    raw,
    gain,
    cosine,
    sine,
    far_grad,
    near_grad,
    own_grad,
    query_grad,
    gain_grad,
    key_sums,
    value_sums,
):
    low = jnp.bfloat16
    half = HEAD // 2
    head = pl.program_id(0)

    @pl.when(head == 0)
    def _():
        key_sums[...] = jnp.zeros_like(key_sums)
        value_sums[...] = jnp.zeros_like(value_sums)
        gain_grad[...] = jnp.zeros_like(gain_grad)

    key_at = lax.broadcasted_iota(jnp.int32, (ROWS, ROWS), 0)
    query_at = lax.broadcasted_iota(jnp.int32, (ROWS, ROWS), 1)
    seq = place[0]
    allowed = (
        (query_at < key_at) & (seq >= 2),
        jnp.full((ROWS, ROWS), seq >= 1),
        key_at <= query_at,
    )
    blocks = (far, near, own)
    context_grad = dot(upstream[...], out_weight[...]).astype(low)
    queries = query[...]
    logs = log_total[pl.ds(head, 1), :]
    probs = [
        jnp.where(ok, jnp.exp(dot(block[:, :HEAD], queries, 1, 1) * SCALE - logs), 0.0)
        for ok, block in zip(allowed, blocks)
    ]
    prob_grads = [dot(block[:, HEAD:], context_grad, 1, 1) for block in blocks]
    inner = jnp.sum(
        probs[0] * prob_grads[0] + probs[1] * prob_grads[1] + probs[2] * prob_grads[2],
        0,
        keepdims=True,
    )
    query_rot = 0.0
    for at_block, block in enumerate(blocks):
        score_grad = (probs[at_block] * (prob_grads[at_block] - inner)).astype(low)
        query_rot = query_rot + dot(score_grad, block[:, :HEAD], 0, 0)
        key_sums[at_block] += dot(score_grad, queries)
        value_sums[at_block] += dot(probs[at_block].astype(low), context_grad)
    query_rot = query_rot * SCALE
    first, second = turn_back(query_rot[:, :half], query_rot[:, half:], cosine[...], sine[...])
    upper = jnp.concatenate([first, second], axis=1)
    block = raw[...]
    scaling = inverse_rms(block)
    gain_grad[...] += jnp.broadcast_to(
        jnp.sum(upper * (block * scaling), 0, keepdims=True), (8, HEAD)
    )
    query_grad[...] = rms_backward(block, scaling, upper * gain[0:1, :]).astype(low)

    @pl.when(head == HEADS - 1)
    def _():
        for at_block, grad in enumerate((far_grad, near_grad, own_grad)):
            grad[:, :HEAD] = (key_sums[at_block] * SCALE).astype(grad.dtype)
            grad[:, HEAD:] = value_sums[at_block].astype(grad.dtype)


def pair_back_body(
    query, own, near, far, raw, gain, cosine, sine, out, out_got, pair_grad, cut, gain_grad
):
    half = HEAD // 2
    low = jnp.bfloat16
    total = own[...] + near[...].astype(jnp.float32) + far[...].astype(jnp.float32)
    first, second = turn_back(total[:, :half], total[:, half:HEAD], cosine[...], sine[...])
    upper = jnp.concatenate([first, second], axis=1)
    block = raw[...]
    scaling = inverse_rms(block)
    gain_sum = jnp.sum(upper * (block * scaling), 0, keepdims=True)
    gain_grad[...] = jnp.broadcast_to(gain_sum, (8, HEAD))
    keys = rms_backward(block, scaling, upper * gain[1:2, :]).astype(low)
    values = total[:, HEAD:].astype(low)
    pair_grad[:, :HEAD] = keys
    pair_grad[:, HEAD:] = values
    size = cut.shape[2]
    cut[0, :ROWS] = query[:, :size]
    cut[1, :ROWS] = query[:, size : 2 * size]
    cut[2, :ROWS] = jnp.concatenate([query[:, 2 * size :], keys[:, :half]], axis=1)
    cut[3, :ROWS] = jnp.concatenate([keys[:, half:], values], axis=1)
    for part in range(4):
        at = slice(part * HEAD, (part + 1) * HEAD)
        term = (out[:, at].astype(jnp.float32) + out_got[:, at].astype(jnp.float32)).astype(low)
        cut[part, ROWS:, :HEAD] = term[:384]
        cut[part, ROWS : ROWS + 192, HEAD:] = term[384:, :half]
        cut[part, ROWS + 192 :, HEAD:] = term[384:, half:]


def arrive_body(own, one, two, three, ring, out):
    wide = jnp.float32
    half = HEAD // 2
    for at, block in enumerate((own, one, two, three)):
        ring[at * ROWS : (at + 1) * ROWS] = block[:ROWS]
    total = sum(block[ROWS:].astype(wide) for block in (own, one, two, three)).astype(out.dtype)
    out[:384] = total[:, :HEAD]
    out[384:, :half] = total[:192, HEAD:]
    out[384:, half:] = total[192:, HEAD:]


def chip_body(offsets, here, got, out, *refs):
    *parts, total = refs
    wide = jnp.float32
    columns = here.shape[1]
    rows = parts[0].shape[1]
    total[:, :columns] = here[...].astype(wide) + got[...].astype(wide)
    total[:, columns:] = out[...].astype(wide)
    for at, part in enumerate(parts):
        for block in range(2):
            start = pl.multiple_of(offsets[2 * at + block], 8)
            part[block] = total[pl.ds(start, rows), :].astype(part.dtype)


def residual_body(
    context, out_weight, tokens, attention_gain, feed_gain, raw, state, feed_input
):
    value = dot(context[...], out_weight[...], 1, 1)
    raw[...] = value
    hidden = tokens[...].astype(jnp.float32) + value * inverse_rms(value) * attention_gain[...]
    state[...] = hidden
    feed_input[...] = (hidden * inverse_rms(hidden) * feed_gain[...]).astype(jnp.bfloat16)


def down_body(
    part, near, across, behind, state, cotangent, valid, gain, layer, down_grad, gain_grad
):
    wide = jnp.float32
    raw = (
        part[...].astype(wide)
        + near[...].astype(wide)
        + across[...].astype(wide)
        + behind[...].astype(wide)
    )
    scaling = inverse_rms(raw)
    hat = raw * scaling
    ok = valid[:, :1]
    layer[...] = (ok * (state[...] + hat * gain[...])).astype(jnp.bfloat16)
    upstream = cotangent[...].astype(wide) * ok

    @pl.when(pl.program_id(0) == 0)
    def _():
        gain_grad[...] = jnp.zeros_like(gain_grad)

    gain_grad[...] += jnp.broadcast_to(
        jnp.sum(upstream * hat, 0, keepdims=True), (8, hat.shape[1])
    )
    down_grad[...] = rms_backward(raw, scaling, upstream * gain[...]).astype(jnp.bfloat16)


def state_body(
    part,
    near,
    across,
    behind,
    state,
    raw,
    cotangent,
    valid,
    feed_gain,
    attention_gain,
    attention_grad,
    state_grad,
    gain_grads,
):
    wide = jnp.float32
    feed_grad = (
        part[...].astype(wide)
        + near[...].astype(wide)
        + across[...].astype(wide)
        + behind[...].astype(wide)
    )
    hidden = state[...]
    scaling = inverse_rms(hidden)
    upstream = cotangent[...].astype(wide) * valid[:, :1]
    total = upstream + rms_backward(hidden, scaling, feed_grad * feed_gain[...])
    state_grad[...] = total
    value = raw[...]
    value_scaling = inverse_rms(value)
    width = value.shape[1]

    @pl.when(pl.program_id(0) == 0)
    def _():
        gain_grads[...] = jnp.zeros_like(gain_grads)

    gain_grads[:8] += jnp.broadcast_to(
        jnp.sum(feed_grad * (hidden * scaling), 0, keepdims=True), (8, width)
    )
    gain_grads[8:] += jnp.broadcast_to(
        jnp.sum(total * (value * value_scaling), 0, keepdims=True), (8, width)
    )
    attention_grad[...] = rms_backward(value, value_scaling, total * attention_gain[...]).astype(
        jnp.bfloat16
    )


def input_body(
    query_grad, pair_grad, weight, tokens, state_grad, gain, tokens_grad, gain_grad
):
    queries = query_grad.shape[1]
    pairs = pair_grad.shape[1]
    grad = dot(query_grad[...], weight[:, :queries], 1, 1) + dot(
        pair_grad[...], weight[:, queries : queries + pairs], 1, 1
    )
    value = tokens[...].astype(jnp.float32)
    scaling = inverse_rms(value)
    gain_grad[...] = jnp.broadcast_to(
        jnp.sum(grad * (value * scaling), 0, keepdims=True), (8, value.shape[1])
    )
    tokens_grad[...] = (
        state_grad[...] + rms_backward(value, scaling, grad * gain[...])
    ).astype(jnp.bfloat16)


def feed_body(place, rows, weights, *refs):
    hidden_out, value_out, slope_out, part, total = refs[-5:]
    low = jnp.bfloat16
    for first, size in FEED_TILES:
        gate_at, up_at, down_at = (
            slice(start + first, start + first + size) for start in (0, FEED_SLICE, 2 * FEED_SLICE)
        )
        to = slice(place, place + rows.shape[0])
        gate_raw = dot(rows[...], weights[:, gate_at])
        up_raw = dot(rows[...], weights[:, up_at])
        value, slope = gelu_parts(gate_raw)
        hidden = (value * up_raw).astype(low)
        hidden_out[to, gate_at] = hidden
        value_out[to, gate_at] = value.astype(low)
        slope_out[to, gate_at] = (slope * up_raw).astype(low)
        term = dot(hidden, weights[:, down_at], 1, 1)
        total[...] = term if first == 0 else total[...] + term

    part[...] = total[...].astype(low)


def feed_back_body(place, rows, weights, value, slope, *refs):
    gate_out, up_out, part, total = refs[-4:]
    low = jnp.bfloat16
    for first, size in FEED_TILES:
        gate_at, up_at, down_at = (
            slice(start + first, start + first + size) for start in (0, FEED_SLICE, 2 * FEED_SLICE)
        )
        to = slice(place, place + rows.shape[0])
        hidden_grad = dot(rows[...], weights[:, down_at])
        gate_grad = (hidden_grad * slope[to, gate_at].astype(jnp.float32)).astype(low)
        up_grad = (hidden_grad * value[to, gate_at].astype(jnp.float32)).astype(low)
        gate_out[to, gate_at] = gate_grad
        up_out[to, gate_at] = up_grad
        term = dot(gate_grad, weights[:, gate_at], 1, 1) + dot(up_grad, weights[:, up_at], 1, 1)
        total[...] = term if first == 0 else total[...] + term

    part[...] = total[...].astype(low)


def feed_call(body, rows, weights, read, kept, place, outs, cost, name, unread=()):
    count, width = rows.shape
    operands = [rows, weights, *read, *kept, *unread]
    whole = pl.BlockSpec(memory_space=pltpu.VMEM)
    first_kept = 2 + len(read)
    return pl.pallas_call(
        functools.partial(body, place),
        in_specs=[whole] * first_kept
        + [pl.BlockSpec(memory_space=pl.ANY)] * (len(kept) + len(unread)),
        out_specs=[whole] * (outs + 1),
        out_shape=[jax.ShapeDtypeStruct((4 * ROWS, FEED_SLICE), jnp.bfloat16)] * outs
        + [jax.ShapeDtypeStruct((count, width), jnp.bfloat16)],
        scratch_shapes=[pltpu.VMEM((count, width), jnp.float32)],
        input_output_aliases={first_kept + i: i for i in range(len(kept))},
        compiler_params=pltpu.CompilerParams(vmem_limit_bytes=VMEM),
        cost_estimate=pl.CostEstimate(flops=cost, bytes_accessed=1000, transcendentals=0),
        name=name,
    )(*operands)


def product_body(core, left, right, *refs):
    away, here, total = refs[-3:]
    rows = left.shape[1] // 16
    width = right.shape[1]

    def split(to, first, columns):
        for two in range(4):
            pieces = [
                total[pl.ds(pl.multiple_of((4 * two + 2 * i + first) * rows, 8), rows), :columns]
                for i in (0, 1)
            ]
            yield slice(two * 2 * rows, (two + 1) * 2 * rows), jnp.concatenate(pieces, axis=0)

    for start in range(0, width, total.shape[1]):
        size = min(total.shape[1], width - start)
        at = slice(start, start + size)
        total[:, :size] = dot(left[...], right[:, at], 0, 0)
        for to, first in ((away, 1 - core[0]), (here, core[0])):
            for place, value in split(to, first, size):
                to[place, at] = value.astype(to.dtype)
    if len(refs) > 3:
        extra = refs[0]
        at = slice(width, width + extra.shape[1])
        total[:, : extra.shape[1]] = extra[...]
        for to, first in ((away, 1 - core[0]), (here, core[0])):
            for place, value in split(to, first, extra.shape[1]):
                to[place, at] = value.astype(to.dtype)


def product(core, left, right, *extra, cost=1000):
    width = right.shape[1] + sum(block.shape[1] for block in extra)
    out = jax.ShapeDtypeStruct((left.shape[1] // 2, width), jnp.bfloat16)
    whole = pl.BlockSpec(memory_space=pltpu.VMEM)
    away, here = pl.pallas_call(
        product_body,
        in_specs=[pl.BlockSpec(memory_space=pltpu.SMEM)] + [whole] * (2 + len(extra)),
        out_specs=[whole, whole],
        out_shape=[out, out],
        scratch_shapes=[pltpu.VMEM((left.shape[1], 512), jnp.float32)],
        compiler_params=pltpu.CompilerParams(vmem_limit_bytes=VMEM),
        cost_estimate=pl.CostEstimate(flops=cost, bytes_accessed=1000, transcendentals=0),
        name="product",
    )(core, left, right, *extra)
    return here, give(away, "core", 1)


def spread_in_body(gate, gate_got, up, up_got, down, down_got, spread):
    rows = spread.shape[1]
    half = FEED_SLICE // 2
    gates, ups, downs = (
        here[...].astype(jnp.float32) + got[...].astype(jnp.float32)
        for here, got in ((gate, gate_got), (up, up_got), (down, down_got))
    )
    for block in range(2):
        of = slice(block * rows, (block + 1) * rows)
        to = 2 * block
        spread[to, :, :FEED_SLICE] = gates[of].astype(spread.dtype)
        spread[to, :, FEED_SLICE:] = downs[of, :half].astype(spread.dtype)
        spread[to + 1, :, :FEED_SLICE] = ups[of].astype(spread.dtype)
        spread[to + 1, :, FEED_SLICE:] = downs[of, half:].astype(spread.dtype)


def spread_out_body(sums, gate, up, down):
    width = gate.shape[1]
    half = FEED_SLICE // 2
    for y in range(4):
        start = y * FEED_SLICE
        size = min(FEED_SLICE, width - start)
        gate[:, start : start + size] = sums[y, :, :size].astype(jnp.float32)
        up[:, start : start + size] = sums[4 + y, :, :size].astype(jnp.float32)
        for xl in range(2):
            first = start + xl * half
            size = min(half, width - first)
            down[:, first : first + size] = sums[
                4 * xl + y, :, FEED_SLICE : FEED_SLICE + size
            ].astype(jnp.float32)


def feed_slice(weight):
    y = lax.axis_index("y")
    padded = jnp.pad(weight, ((0, 0), (0, 4 * FEED_SLICE - weight.shape[1])))
    return lax.dynamic_slice_in_dim(padded, y * FEED_SLICE, FEED_SLICE, 1)


def local(
    tokens,
    cotangent,
    lengths,
    query_weight,
    key_weight,
    value_weight,
    out_weight,
    gate_weight,
    up_weight,
    down_weight,
    input_gain,
    query_gain,
    key_gain,
    attention_gain,
    feedforward_gain,
    output_gain,
):
    low = jnp.bfloat16
    wide = jnp.float32
    row_count, model_width = tokens.shape
    head_size = key_weight.shape[1]
    head_count = query_weight.shape[1] // head_size
    query_width = head_count * head_size
    qkv_width = query_width + 2 * head_size
    feed_width = gate_weight.shape[1]
    gain_shard = input_gain.shape[0]
    head_shard = query_gain.shape[0]
    y = lax.axis_index("y")
    seq_index = lax.axis_index("xl") * 4 + y
    place = seq_index.reshape(1).astype(jnp.int32)
    core = lax.axis_index("core").reshape(1).astype(jnp.int32)
    positions = seq_index * row_count + lax.iota(jnp.int32, row_count)
    valid = jnp.broadcast_to((positions < lengths[0]).astype(wide)[:, None], (row_count, 128))
    cosine, sine = rotary_tables(positions, head_size)

    def spread(vector):
        return jnp.pad(vector, (0, gain_shard - head_shard))

    gain_columns = jnp.stack(
        [
            input_gain,
            attention_gain,
            feedforward_gain,
            output_gain,
            spread(query_gain),
            spread(key_gain),
        ],
        axis=1,
    )
    gain_columns = jnp.pad(gain_columns, ((0, 0), (0, 122)))
    feed_weights = lax.all_gather(
        jnp.concatenate(
            [feed_slice(gate_weight), feed_slice(up_weight), feed_slice(down_weight)], axis=1
        ),
        DP,
        axis=0,
        tiled=True,
    )
    attention_weights = jnp.concatenate(
        [query_weight, key_weight, value_weight, gain_columns, out_weight], axis=1
    )
    beside = swap_x(attention_weights)
    qkv_columns = qkv_width + gain_columns.shape[1]
    tokens_ring = [take(ordered(tokens, beside), "y", by) for by in (1, 2, 3)]
    full_qkv, arrived = gather_rows(
        with_other_x(attention_weights[:, :qkv_columns], beside[:, :qkv_columns]), tokens_ring
    )
    gains = 1.0 + full_qkv[:, qkv_width : qkv_width + 8].astype(wide).T
    one_input, one_attention, one_feed, one_output = (gains[i : i + 1] for i in range(4))
    head_gain = gains.reshape(8, 16, gain_shard)[4:6, :, :head_shard].reshape(2, head_size)
    head_gain = jnp.pad(head_gain, ((0, 6), (0, 0)))

    def attention_input_of(rows):
        values = rows.astype(wide)
        return (values * inverse_rms(values) * one_input).astype(low)

    attention_input = attention_input_of(tokens)
    qkv_raw = jnp.dot(attention_input, full_qkv[:, :qkv_width], preferred_element_type=wide)
    prepare = rows_call(
        prepare_body,
        [((row_count, query_width), low), ((row_count, 2 * head_size), low)],
        "prepare",
    )
    query_low, local_pair = prepare(qkv_raw, head_gain, cosine, sine)
    near_pair, far_pair = (from_behind(local_pair, distance) for distance in (1, 2))
    input_ring = attention_input_of(
        jnp.concatenate([ordered(tokens, local_pair)] + tokens_ring, axis=0)
    )
    out_pair = with_other_x(out_weight, beside[:, qkv_columns:])
    full_out, _ = gather_rows(ordered(out_pair, *arrived), (input_ring,))
    near_pair, far_pair, input_ring = lax.optimization_barrier((near_pair, far_pair, input_ring))
    attend = rows_call(
        attend_body,
        [((row_count, query_width), low), ((8, row_count), wide)],
        "attend",
        12 * 10**9,
    )
    context_low, log_total = attend(place, query_low, far_pair, near_pair, local_pair)
    residual = rows_call(
        residual_body,
        [
            ((row_count, model_width), wide),
            ((row_count, model_width), wide),
            ((row_count, model_width), low),
        ],
        "residual",
    )
    attention_raw, state, feed_input = residual(
        context_low, full_out, tokens, one_attention, one_feed
    )

    weights, feed_input = lax.optimization_barrier((feed_weights, feed_input))

    def touch(array):
        def body(whole, some):
            some[...] = whole[:16, :128]

        return pl.pallas_call(
            body,
            in_specs=[pl.BlockSpec(memory_space=pltpu.VMEM)],
            out_specs=pl.BlockSpec(memory_space=pltpu.VMEM),
            out_shape=jax.ShapeDtypeStruct((16, 128), array.dtype),
            compiler_params=pltpu.CompilerParams(vmem_limit_bytes=VMEM),
            cost_estimate=pl.CostEstimate(flops=LONG, bytes_accessed=1000, transcendentals=0),
            name="touch",
        )(array)

    def exchange(rows, run):
        two, one, three = (take(rows, "y", by) for by in (2, 1, 3))
        two, touched = lax.optimization_barrier((two, touch(weights)))
        kept, two_part = run(two, [], 3 * row_count, 1000, [touched])
        across = give(two_part, "y", 2)
        both = jnp.concatenate([one, three], axis=0)
        kept, both_part = run(both, kept, 0, LONG)
        from_one = give(both_part[:row_count], "y", 1)
        from_three = give(both_part[row_count:], "y", 3)
        *kept, across, both = lax.optimization_barrier((*kept, across, both))
        kept, own_part = run(rows, kept, 2 * row_count, LONG)
        ring = jnp.concatenate([ordered(both, own_part, from_one, from_three), rows, two], axis=0)
        return kept, [own_part, from_one, across, from_three], ring

    def forward(rows, kept, at, cost, unread=()):
        *kept, part = feed_call(feed_body, rows, weights, [], kept, at, 3, cost, "feed", unread)
        return kept, part

    kept, terms, feed_ring = exchange(feed_input, forward)
    hidden, value, slope = kept
    finish = blocks_call(
        down_body,
        [
            ((row_count, model_width), low),
            ((row_count, model_width), low),
            ((8, model_width), wide),
        ],
        "finish",
    )
    layer_output, down_grad, output_gain_rows = finish(
        *terms, state, cotangent, valid, one_output
    )

    def backward(rows, kept, at, cost):
        *kept, part = feed_call(
            feed_back_body, rows, weights, [value, slope], kept, at, 2, cost, "feed_back"
        )
        return kept, part

    rows72 = gain_shard
    two, one, three = (take(down_grad, "y", by) for by in (2, 1, 3))
    kept, own_part = backward(down_grad, [], 2 * row_count, 1000)
    kept, two_part = backward(two, kept, 3 * row_count, 1000)
    across = give(two_part, "y", 2)
    both = jnp.concatenate([one, three], axis=0)
    (gate_grad, up_grad), both_part = backward(both, kept, 0, LONG)
    from_one = give(both_part[:row_count], "y", 1)
    from_three = give(both_part[row_count:], "y", 3)
    across, both, gate_grad, up_grad = lax.optimization_barrier((across, both, gate_grad, up_grad))
    down_ring = jnp.concatenate([both, down_grad, two], axis=0)
    down_halves = product(core, down_ring, hidden)
    terms = [own_part, from_one, across, from_three]
    gate_halves = product(core, ordered(feed_ring, down_halves[0]), gate_grad)
    up_halves = product(
        core,
        ordered(feed_ring, gate_halves[0], down_halves[1]),
        up_grad,
    )
    halves = [*gate_halves, *up_halves, *down_halves]
    spread_shape = (16, rows72, FEED_SLICE * 3 // 2)
    spread_in = pl.pallas_call(
        spread_in_body,
        grid=(4,),
        in_specs=[pl.BlockSpec((2 * rows72, FEED_SLICE), lambda i: (i, 0))] * 6,
        out_specs=pl.BlockSpec((4, *spread_shape[1:]), lambda i: (i, 0, 0)),
        out_shape=jax.ShapeDtypeStruct(spread_shape, low),
        compiler_params=pltpu.CompilerParams(vmem_limit_bytes=VMEM),
        cost_estimate=SMALL,
        name="spread_in",
    )(*halves)
    feed_sum = lax.psum_scatter(spread_in, ("z", "xh", "xl"), scatter_dimension=0, tiled=False)
    back = blocks_call(
        state_body,
        [
            ((row_count, model_width), low),
            ((row_count, model_width), wide),
            ((16, model_width), wide),
        ],
        "state_back",
        VMEM,
        36000000000,
    )
    attention_grad, state_grad, state_gain_rows = back(
        *terms, state, attention_raw, cotangent, valid, one_feed, one_attention
    )

    def whole(shape):
        return pl.BlockSpec(shape, lambda i: (0,) * len(shape))

    def head_columns(rows):
        return pl.BlockSpec((rows, head_size), lambda i: (0, i))

    smem = pl.BlockSpec(memory_space=pltpu.SMEM)
    pair_block = whole((row_count, 2 * head_size))
    table = whole((row_count, head_size // 2))
    attend_back = pl.pallas_call(
        attend_back_body,
        grid=(head_count,),
        in_specs=[
            smem,
            whole((row_count, model_width)),
            head_columns(model_width),
            head_columns(row_count),
            pair_block,
            pair_block,
            pair_block,
            whole((8, row_count)),
            head_columns(row_count),
            whole((8, head_size)),
            table,
            table,
        ],
        out_specs=[
            pair_block,
            pair_block,
            pair_block,
            head_columns(row_count),
            whole((8, head_size)),
        ],
        out_shape=[
            jax.ShapeDtypeStruct((row_count, 2 * head_size), low),
            jax.ShapeDtypeStruct((row_count, 2 * head_size), low),
            jax.ShapeDtypeStruct((row_count, 2 * head_size), wide),
            jax.ShapeDtypeStruct((row_count, query_width), low),
            jax.ShapeDtypeStruct((8, head_size), wide),
        ],
        scratch_shapes=[pltpu.VMEM((3, row_count, head_size), wide)] * 2,
        compiler_params=pltpu.CompilerParams(vmem_limit_bytes=MOST),
        cost_estimate=pl.CostEstimate(flops=100 * 10**9, bytes_accessed=1000, transcendentals=0),
        name="attend_back",
    )
    far_grad, near_grad, own_grad, query_grad, query_gain_rows = attend_back(
        place,
        attention_grad,
        full_out,
        query_low,
        far_pair,
        near_pair,
        local_pair,
        log_total,
        qkv_raw,
        head_gain,
        cosine,
        sine,
    )
    near_back = from_behind(near_grad, -1)
    far_back = from_behind(far_grad, -2)
    out_halves = product(core, ordered(attention_grad, near_grad), context_low, cost=LONG)
    out_block = whole((model_width // 2, query_width))
    cut_shape = (4, row_count + 384, qkv_width // 4)
    pair_back = pl.pallas_call(
        pair_back_body,
        grid=(1,),
        in_specs=[
            whole((row_count, query_width)),
            pair_block,
            pair_block,
            pair_block,
            pl.BlockSpec((row_count, head_size), lambda i: (0, head_count)),
            whole((8, head_size)),
            table,
            table,
            out_block,
            out_block,
        ],
        out_specs=[pair_block, whole(cut_shape), whole((8, head_size))],
        out_shape=[
            jax.ShapeDtypeStruct((row_count, 2 * head_size), low),
            jax.ShapeDtypeStruct(cut_shape, low),
            jax.ShapeDtypeStruct((8, head_size), wide),
        ],
        compiler_params=pltpu.CompilerParams(vmem_limit_bytes=MOST),
        cost_estimate=SMALL,
        name="pair_back",
    )
    pair_grad, qkv_cut, key_gain_rows = pair_back(
        query_grad, own_grad, near_back, far_back, qkv_raw, head_gain, cosine, sine, *out_halves
    )
    pieces = [give(pick(qkv_cut, (y + by) % 4, 0), "y", by) for by in (3, 2, 1)]
    qkv_ring, out_sum = rows_call(
        arrive_body,
        [((4 * row_count, qkv_width // 4), low), ((model_width // 2, query_width // 4), low)],
        "arrive",
    )(pick(qkv_cut, y, 0), *pieces)
    input_back = rows_call(
        input_body,
        [((row_count, model_width), low), ((8, model_width), wide)],
        "input_back",
    )
    tokens_grad, input_gain_rows = input_back(
        query_grad, pair_grad, full_qkv, tokens, state_grad, one_input
    )

    def spread_head(vector):
        return jnp.pad(
            vector.reshape(16, head_shard), ((0, 0), (0, gain_shard - head_shard))
        ).reshape(model_width)

    gain_block = jnp.stack(
        [
            input_gain_rows[0],
            state_gain_rows[8],
            state_gain_rows[0],
            output_gain_rows[0],
            spread_head(query_gain_rows[0]),
            spread_head(key_gain_rows[0]),
        ],
        axis=1,
    )
    gain_block = jnp.pad(gain_block, ((0, 0), (0, 122)))
    z = lax.axis_index("z")
    xh = lax.axis_index("xh")
    offsets = jnp.stack(
        [(((z + i) % 4) * 2 + (xh + j) % 2) * rows72 for i in range(4) for j in range(2)]
    ).astype(jnp.int32)
    columns = qkv_width // 4 + 128 + query_width // 4
    parts = pl.pallas_call(
        chip_body,
        in_specs=[pl.BlockSpec(memory_space=pltpu.SMEM)]
        + [pl.BlockSpec(memory_space=pltpu.VMEM)] * 3,
        out_specs=[pl.BlockSpec(memory_space=pltpu.VMEM)] * 4,
        out_shape=[jax.ShapeDtypeStruct((2, rows72, columns), low)] * 4,
        scratch_shapes=[pltpu.VMEM((model_width // 2, columns), wide)],
        compiler_params=pltpu.CompilerParams(vmem_limit_bytes=VMEM),
        cost_estimate=SMALL,
        name="chip",
    )(offsets, *product(core, input_ring, qkv_ring, gain_block), out_sum)
    total = parts[0].astype(wide)
    for by in (1, 3, 2):
        total = total + give(parts[by], "z", by).astype(wide)
    attention_column = total.astype(low)
    attention_half = (
        attention_column[0].astype(wide) + swap_x(attention_column[1]).astype(wide)
    ).astype(low)
    attention_sum = (
        attention_half.astype(wide) + give(attention_half, "xl", 1).astype(wide)
    ).astype(low)
    attention_blocks = in_order(
        [attention_sum] + [take(attention_sum, "y", by) for by in (1, 2, 3)]
    )
    feed_sums = lax.all_gather(ordered(feed_sum, parts[0]), SEQ, axis=0, tiled=False)
    gate_weight_grad, up_weight_grad, down_weight_grad = rows_call(
        spread_out_body, [((rows72, feed_width), wide)] * 3, "spread_out"
    )(feed_sums)
    qkv_cols = qkv_width // 4
    out_cols = query_width // 4
    qkv_weight_grad = jnp.concatenate([b[:, :qkv_cols] for b in attention_blocks], axis=1)
    out_weight_grad = jnp.concatenate([b[:, qkv_cols + 128 :] for b in attention_blocks], axis=1)
    gain_sum = sum(b[:, qkv_cols : qkv_cols + 128].astype(wide) for b in attention_blocks)
    return (
        layer_output,
        tokens_grad,
        qkv_weight_grad[:, :query_width].astype(wide),
        qkv_weight_grad[:, query_width : query_width + head_size].astype(wide),
        qkv_weight_grad[:, query_width + head_size :].astype(wide),
        out_weight_grad.astype(wide),
        gate_weight_grad,
        up_weight_grad,
        down_weight_grad,
        gain_sum[:, 0],
        gain_sum[:head_shard, 4],
        gain_sum[:head_shard, 5],
        gain_sum[:, 1],
        gain_sum[:, 2],
        gain_sum[:, 3],
    )


def solution(mesh):
    fine = Mesh(mesh.devices.reshape(SIZES), AXES)
    rows = P(AXES, None)
    matrix = P(DP, None)
    vector = P(DP)
    return jax.shard_map(
        local,
        mesh=fine,
        in_specs=(rows, rows, vector) + (matrix,) * 7 + (vector,) * 6,
        out_specs=(rows, rows) + (matrix,) * 7 + (vector,) * 6,
        check_vma=False,
    )
```

```python
import functools
import math

import jax
import jax.numpy as jnp
from jax import lax
from jax.experimental import pallas as pl
from jax.experimental.pallas import tpu as pltpu
from jax.sharding import Mesh
from jax.sharding import PartitionSpec as P

EPSILON = 1e-06
GELU_COEFF = 0.044715
AXES = ("z", "xh", "core", "xl", "y")
SIZES = (4, 2, 2, 2, 4)
DP = ("z", "xh", "core")
SEQ = ("xl", "y")
FEED_SLICE = 1792
FEED_TILES = ((0, 1024), (1024, 768))
HEADS = 4
HEAD = 256
SCALE = HEAD**-0.5
ROWS = 256
VMEM = 16 * 1024 * 1024
MOST = 56 * 1024 * 1024
LONG = 12 * 10**9
SMALL = pl.CostEstimate(flops=1000, bytes_accessed=1000, transcendentals=0)


def from_behind(array, by):
    pairs = [(i, i + by) for i in range(8) if 0 <= i + by < 8]
    return lax.ppermute(array, SEQ, pairs)


def take(array, axis, by):
    count = lax.axis_size(axis)
    return lax.ppermute(array, axis, [((i + by) % count, i) for i in range(count)])


def give(array, axis, by):
    count = lax.axis_size(axis)
    return lax.ppermute(array, axis, [(i, (i + by) % count) for i in range(count)])


def swap_x(array):
    return lax.ppermute(array, ("xh", "xl"), [(0, 3), (3, 0), (1, 2), (2, 1)])


def ordered(value, *after):
    return lax.optimization_barrier((value,) + after)[0]


def pick(array, index, axis):
    return lax.dynamic_index_in_dim(array, index, axis, keepdims=False)


def with_other_x(block, beside):
    xh = lax.axis_index("xh")
    return jnp.where(xh == 0, jnp.stack([block, beside]), jnp.stack([beside, block]))


def gather_rows(pair, wait=()):
    _, rows, width = pair.shape
    z = lax.axis_index("z")
    core = lax.axis_index("core")
    ring = [(take(pair, "z", by), by) for by in (1, 3, 2)]
    arrived = [piece for piece, _ in ring]
    own = jnp.zeros((4, 2, rows, width), pair.dtype)
    own = lax.dynamic_update_slice_in_dim(own, pair[None], z, 0)
    own = ordered(own, *wait)
    for piece, by in ring:
        own = lax.dynamic_update_slice_in_dim(own, piece[None], (z + by) % 4, 0)
    other = give(own, "core", 1)
    both = jnp.where(
        core == 0, jnp.stack([own, other], axis=2), jnp.stack([other, own], axis=2)
    )
    return both.reshape(16 * rows, width), arrived


def in_order(blocks):
    y = lax.axis_index("y")
    placed = []
    for place in range(4):
        value = blocks[(place - 3) % 4]
        for at in range(3):
            value = jnp.where(y == at, blocks[(place - at) % 4], value)
        placed.append(value)
    return placed


def inverse_rms(values):
    return lax.rsqrt(jnp.mean(values * values, axis=-1, keepdims=True) + EPSILON)


def rms_backward(values, scaling, upstream):
    inner = jnp.mean(upstream * values, axis=-1, keepdims=True)
    return scaling * (upstream - values * (scaling * scaling) * inner)


def rotary_tables(positions, head_size):
    half_size = head_size // 2
    exponents = lax.iota(jnp.float32, half_size) * (2.0 / head_size)
    frequency = jnp.power(10000.0, -exponents)
    angles = positions.astype(jnp.float32)[:, None] * frequency[None, :]
    return (jnp.cos(angles), jnp.sin(angles))


def gelu_parts(values):
    root_coeff = math.sqrt(2.0 / math.pi)
    square = values * values
    bend = jnp.tanh(values * (root_coeff + (root_coeff * GELU_COEFF) * square))
    part = 0.5 + 0.5 * bend
    gelu_value = values * part
    inner = root_coeff + (3.0 * GELU_COEFF * root_coeff) * square
    gelu_slope = part + gelu_value * (1.0 - bend) * inner
    return (gelu_value, gelu_slope)


def dot(left, right, left_axis=1, right_axis=0):
    return lax.dot_general(
        left,
        right,
        (((left_axis,), (right_axis,)), ((), ())),
        preferred_element_type=jnp.float32,
    )


def turn(first, second, cosine, sine):
    return first * cosine - second * sine, second * cosine + first * sine


def turn_back(first, second, cosine, sine):
    return first * cosine + second * sine, second * cosine - first * sine


def rows_call(body, outs, name, cost=1000):
    def call(*operands):
        specs = [
            pl.BlockSpec(memory_space=pltpu.SMEM)
            if operand.dtype == jnp.int32
            else pl.BlockSpec(memory_space=pltpu.VMEM)
            for operand in operands
        ]
        return pl.pallas_call(
            body,
            out_shape=[jax.ShapeDtypeStruct(shape, dtype) for shape, dtype in outs],
            in_specs=specs,
            out_specs=[pl.BlockSpec(memory_space=pltpu.VMEM) for _ in outs],
            compiler_params=pltpu.CompilerParams(vmem_limit_bytes=VMEM),
            cost_estimate=pl.CostEstimate(flops=cost, bytes_accessed=1000, transcendentals=0),
            name=name,
        )(*operands)

    return call


def blocks_call(body, outs, name, vmem=VMEM, cost=1000):
    steps = 4

    def spec(shape):
        if shape[0] < ROWS:
            return pl.BlockSpec(shape, lambda i: (0, 0))
        return pl.BlockSpec((shape[0] // steps, shape[1]), lambda i: (i, 0))

    def call(*operands):
        return pl.pallas_call(
            body,
            grid=(steps,),
            out_shape=[jax.ShapeDtypeStruct(shape, dtype) for shape, dtype in outs],
            in_specs=[spec(operand.shape) for operand in operands],
            out_specs=[spec(shape) for shape, _ in outs],
            compiler_params=pltpu.CompilerParams(vmem_limit_bytes=vmem),
            cost_estimate=pl.CostEstimate(flops=cost, bytes_accessed=1000, transcendentals=0),
            name=name,
        )(*operands)

    return call


def prepare_body(raw, gain, cosine, sine, query, pair):
    cos, sin = cosine[...], sine[...]
    half = HEAD // 2

    def finish(block, gains):
        hat = block * inverse_rms(block) * gains
        first, second = turn(hat[:, :half], hat[:, half:], cos, sin)
        return jnp.concatenate([first, second], axis=1).astype(jnp.bfloat16)

    for head in range(HEADS):
        at = slice(head * HEAD, (head + 1) * HEAD)
        query[:, at] = finish(raw[:, at], gain[0:1, :])
    keys = HEADS * HEAD
    pair[:, :HEAD] = finish(raw[:, keys : keys + HEAD], gain[1:2, :])
    pair[:, HEAD:] = raw[:, keys + HEAD : keys + 2 * HEAD].astype(jnp.bfloat16)


def attend_body(place, query, far, near, own, context, log_total):
    row = lax.broadcasted_iota(jnp.int32, (ROWS, ROWS), 0)
    column = lax.broadcasted_iota(jnp.int32, (ROWS, ROWS), 1)
    seq = place[0]
    allowed = (
        (row < column) & (seq >= 2),
        jnp.full((ROWS, ROWS), seq >= 1),
        column <= row,
    )
    blocks = (far, near, own)
    lane = lax.broadcasted_iota(jnp.int32, (ROWS, 128), 1)
    logs = jnp.zeros((ROWS, 128), jnp.float32)
    for head in range(HEADS):
        at = slice(head * HEAD, (head + 1) * HEAD)
        scores = [
            jnp.where(ok, dot(query[:, at], block[:, :HEAD], 1, 1) * SCALE, -1e30)
            for ok, block in zip(allowed, blocks)
        ]
        top = jnp.max(jnp.maximum(jnp.maximum(scores[0], scores[1]), scores[2]), 1, keepdims=True)
        terms = [jnp.exp(score - top) for score in scores]
        total = jnp.sum(terms[0] + terms[1] + terms[2], 1, keepdims=True)
        share = 1.0 / total
        out = sum(
            dot((term * share).astype(jnp.bfloat16), block[:, HEAD:])
            for term, block in zip(terms, blocks)
        )
        context[:, at] = out.astype(jnp.bfloat16)
        logs = jnp.where(lane == head, top + jnp.log(total), logs)
    log_total[...] = logs.T[:8]


def attend_back_body(
    place,
    upstream,
    out_weight,
    query,
    far,
    near,
    own,
    log_total,
    raw,
    gain,
    cosine,
    sine,
    far_grad,
    near_grad,
    own_grad,
    query_grad,
    gain_grad,
    key_sums,
    value_sums,
):
    low = jnp.bfloat16
    half = HEAD // 2
    head = pl.program_id(0)

    @pl.when(head == 0)
    def _():
        key_sums[...] = jnp.zeros_like(key_sums)
        value_sums[...] = jnp.zeros_like(value_sums)
        gain_grad[...] = jnp.zeros_like(gain_grad)

    key_at = lax.broadcasted_iota(jnp.int32, (ROWS, ROWS), 0)
    query_at = lax.broadcasted_iota(jnp.int32, (ROWS, ROWS), 1)
    seq = place[0]
    allowed = (
        (query_at < key_at) & (seq >= 2),
        jnp.full((ROWS, ROWS), seq >= 1),
        key_at <= query_at,
    )
    blocks = (far, near, own)
    context_grad = dot(upstream[...], out_weight[...]).astype(low)
    queries = query[...]
    logs = log_total[pl.ds(head, 1), :]
    probs = [
        jnp.where(ok, jnp.exp(dot(block[:, :HEAD], queries, 1, 1) * SCALE - logs), 0.0)
        for ok, block in zip(allowed, blocks)
    ]
    prob_grads = [dot(block[:, HEAD:], context_grad, 1, 1) for block in blocks]
    inner = jnp.sum(
        probs[0] * prob_grads[0] + probs[1] * prob_grads[1] + probs[2] * prob_grads[2],
        0,
        keepdims=True,
    )
    query_rot = 0.0
    for at_block, block in enumerate(blocks):
        score_grad = (probs[at_block] * (prob_grads[at_block] - inner)).astype(low)
        query_rot = query_rot + dot(score_grad, block[:, :HEAD], 0, 0)
        key_sums[at_block] += dot(score_grad, queries)
        value_sums[at_block] += dot(probs[at_block].astype(low), context_grad)
    query_rot = query_rot * SCALE
    first, second = turn_back(query_rot[:, :half], query_rot[:, half:], cosine[...], sine[...])
    upper = jnp.concatenate([first, second], axis=1)
    block = raw[...]
    scaling = inverse_rms(block)
    gain_grad[...] += jnp.broadcast_to(
        jnp.sum(upper * (block * scaling), 0, keepdims=True), (8, HEAD)
    )
    query_grad[...] = rms_backward(block, scaling, upper * gain[0:1, :]).astype(low)

    @pl.when(head == HEADS - 1)
    def _():
        for at_block, grad in enumerate((far_grad, near_grad, own_grad)):
            grad[:, :HEAD] = (key_sums[at_block] * SCALE).astype(grad.dtype)
            grad[:, HEAD:] = value_sums[at_block].astype(grad.dtype)


def pair_back_body(
    query, own, near, far, raw, gain, cosine, sine, out, out_got, pair_grad, cut, gain_grad
):
    half = HEAD // 2
    low = jnp.bfloat16
    total = own[...] + near[...].astype(jnp.float32) + far[...].astype(jnp.float32)
    first, second = turn_back(total[:, :half], total[:, half:HEAD], cosine[...], sine[...])
    upper = jnp.concatenate([first, second], axis=1)
    block = raw[...]
    scaling = inverse_rms(block)
    gain_sum = jnp.sum(upper * (block * scaling), 0, keepdims=True)
    gain_grad[...] = jnp.broadcast_to(gain_sum, (8, HEAD))
    keys = rms_backward(block, scaling, upper * gain[1:2, :]).astype(low)
    values = total[:, HEAD:].astype(low)
    pair_grad[:, :HEAD] = keys
    pair_grad[:, HEAD:] = values
    size = cut.shape[2]
    cut[0, :ROWS] = query[:, :size]
    cut[1, :ROWS] = query[:, size : 2 * size]
    cut[2, :ROWS] = jnp.concatenate([query[:, 2 * size :], keys[:, :half]], axis=1)
    cut[3, :ROWS] = jnp.concatenate([keys[:, half:], values], axis=1)
    for part in range(4):
        at = slice(part * HEAD, (part + 1) * HEAD)
        term = (out[:, at].astype(jnp.float32) + out_got[:, at].astype(jnp.float32)).astype(low)
        cut[part, ROWS:, :HEAD] = term[:384]
        cut[part, ROWS : ROWS + 192, HEAD:] = term[384:, :half]
        cut[part, ROWS + 192 :, HEAD:] = term[384:, half:]


def arrive_body(own, one, two, three, ring, out):
    wide = jnp.float32
    half = HEAD // 2
    for at, block in enumerate((own, one, two, three)):
        ring[at * ROWS : (at + 1) * ROWS] = block[:ROWS]
    total = sum(block[ROWS:].astype(wide) for block in (own, one, two, three)).astype(out.dtype)
    out[:384] = total[:, :HEAD]
    out[384:, :half] = total[:192, HEAD:]
    out[384:, half:] = total[192:, HEAD:]


def chip_body(offsets, here, got, out, *refs):
    *parts, total = refs
    wide = jnp.float32
    columns = here.shape[1]
    rows = parts[0].shape[1]
    total[:, :columns] = here[...].astype(wide) + got[...].astype(wide)
    total[:, columns:] = out[...].astype(wide)
    for at, part in enumerate(parts):
        for block in range(2):
            start = pl.multiple_of(offsets[2 * at + block], 8)
            part[block] = total[pl.ds(start, rows), :].astype(part.dtype)


def residual_body(
    context, out_weight, tokens, attention_gain, feed_gain, raw, state, feed_input
):
    value = dot(context[...], out_weight[...], 1, 1)
    raw[...] = value
    hidden = tokens[...].astype(jnp.float32) + value * inverse_rms(value) * attention_gain[...]
    state[...] = hidden
    feed_input[...] = (hidden * inverse_rms(hidden) * feed_gain[...]).astype(jnp.bfloat16)


def down_body(
    part, near, across, behind, state, cotangent, valid, gain, layer, down_grad, gain_grad
):
    wide = jnp.float32
    raw = (
        part[...].astype(wide)
        + near[...].astype(wide)
        + across[...].astype(wide)
        + behind[...].astype(wide)
    )
    scaling = inverse_rms(raw)
    hat = raw * scaling
    ok = valid[:, :1]
    layer[...] = (ok * (state[...] + hat * gain[...])).astype(jnp.bfloat16)
    upstream = cotangent[...].astype(wide) * ok

    @pl.when(pl.program_id(0) == 0)
    def _():
        gain_grad[...] = jnp.zeros_like(gain_grad)

    gain_grad[...] += jnp.broadcast_to(
        jnp.sum(upstream * hat, 0, keepdims=True), (8, hat.shape[1])
    )
    down_grad[...] = rms_backward(raw, scaling, upstream * gain[...]).astype(jnp.bfloat16)


def state_body(
    part,
    near,
    across,
    behind,
    state,
    raw,
    cotangent,
    valid,
    feed_gain,
    attention_gain,
    attention_grad,
    state_grad,
    gain_grads,
):
    wide = jnp.float32
    feed_grad = (
        part[...].astype(wide)
        + near[...].astype(wide)
        + across[...].astype(wide)
        + behind[...].astype(wide)
    )
    hidden = state[...]
    scaling = inverse_rms(hidden)
    upstream = cotangent[...].astype(wide) * valid[:, :1]
    total = upstream + rms_backward(hidden, scaling, feed_grad * feed_gain[...])
    state_grad[...] = total
    value = raw[...]
    value_scaling = inverse_rms(value)
    width = value.shape[1]

    @pl.when(pl.program_id(0) == 0)
    def _():
        gain_grads[...] = jnp.zeros_like(gain_grads)

    gain_grads[:8] += jnp.broadcast_to(
        jnp.sum(feed_grad * (hidden * scaling), 0, keepdims=True), (8, width)
    )
    gain_grads[8:] += jnp.broadcast_to(
        jnp.sum(total * (value * value_scaling), 0, keepdims=True), (8, width)
    )
    attention_grad[...] = rms_backward(value, value_scaling, total * attention_gain[...]).astype(
        jnp.bfloat16
    )


def input_body(
    query_grad, pair_grad, weight, tokens, state_grad, gain, tokens_grad, gain_grad
):
    queries = query_grad.shape[1]
    pairs = pair_grad.shape[1]
    grad = dot(query_grad[...], weight[:, :queries], 1, 1) + dot(
        pair_grad[...], weight[:, queries : queries + pairs], 1, 1
    )
    value = tokens[...].astype(jnp.float32)
    scaling = inverse_rms(value)
    gain_grad[...] = jnp.broadcast_to(
        jnp.sum(grad * (value * scaling), 0, keepdims=True), (8, value.shape[1])
    )
    tokens_grad[...] = (
        state_grad[...] + rms_backward(value, scaling, grad * gain[...])
    ).astype(jnp.bfloat16)


def feed_body(place, rows, weights, *refs):
    hidden_out, value_out, slope_out, part, total = refs[-5:]
    low = jnp.bfloat16
    for first, size in FEED_TILES:
        gate_at, up_at, down_at = (
            slice(start + first, start + first + size) for start in (0, FEED_SLICE, 2 * FEED_SLICE)
        )
        to = slice(place, place + rows.shape[0])
        gate_raw = dot(rows[...], weights[:, gate_at])
        up_raw = dot(rows[...], weights[:, up_at])
        value, slope = gelu_parts(gate_raw)
        hidden = (value * up_raw).astype(low)
        hidden_out[to, gate_at] = hidden
        value_out[to, gate_at] = value.astype(low)
        slope_out[to, gate_at] = (slope * up_raw).astype(low)
        term = dot(hidden, weights[:, down_at], 1, 1)
        total[...] = term if first == 0 else total[...] + term

    part[...] = total[...].astype(low)


def feed_back_body(place, rows, weights, value, slope, *refs):
    gate_out, up_out, part, total = refs[-4:]
    low = jnp.bfloat16
    for first, size in FEED_TILES:
        gate_at, up_at, down_at = (
            slice(start + first, start + first + size) for start in (0, FEED_SLICE, 2 * FEED_SLICE)
        )
        to = slice(place, place + rows.shape[0])
        hidden_grad = dot(rows[...], weights[:, down_at])
        gate_grad = (hidden_grad * slope[to, gate_at].astype(jnp.float32)).astype(low)
        up_grad = (hidden_grad * value[to, gate_at].astype(jnp.float32)).astype(low)
        gate_out[to, gate_at] = gate_grad
        up_out[to, gate_at] = up_grad
        term = dot(gate_grad, weights[:, gate_at], 1, 1) + dot(up_grad, weights[:, up_at], 1, 1)
        total[...] = term if first == 0 else total[...] + term

    part[...] = total[...].astype(low)


def feed_call(body, rows, weights, read, kept, place, outs, cost, name, unread=()):
    count, width = rows.shape
    operands = [rows, weights, *read, *kept, *unread]
    whole = pl.BlockSpec(memory_space=pltpu.VMEM)
    first_kept = 2 + len(read)
    return pl.pallas_call(
        functools.partial(body, place),
        in_specs=[whole] * first_kept
        + [pl.BlockSpec(memory_space=pl.ANY)] * (len(kept) + len(unread)),
        out_specs=[whole] * (outs + 1),
        out_shape=[jax.ShapeDtypeStruct((4 * ROWS, FEED_SLICE), jnp.bfloat16)] * outs
        + [jax.ShapeDtypeStruct((count, width), jnp.bfloat16)],
        scratch_shapes=[pltpu.VMEM((count, width), jnp.float32)],
        input_output_aliases={first_kept + i: i for i in range(len(kept))},
        compiler_params=pltpu.CompilerParams(vmem_limit_bytes=VMEM),
        cost_estimate=pl.CostEstimate(flops=cost, bytes_accessed=1000, transcendentals=0),
        name=name,
    )(*operands)


def product_body(core, left, right, *refs):
    away, here, total = refs[-3:]
    rows = left.shape[1] // 16
    width = right.shape[1]

    def split(to, first, columns):
        for two in range(4):
            pieces = [
                total[pl.ds(pl.multiple_of((4 * two + 2 * i + first) * rows, 8), rows), :columns]
                for i in (0, 1)
            ]
            yield slice(two * 2 * rows, (two + 1) * 2 * rows), jnp.concatenate(pieces, axis=0)

    for start in range(0, width, total.shape[1]):
        size = min(total.shape[1], width - start)
        at = slice(start, start + size)
        total[:, :size] = dot(left[...], right[:, at], 0, 0)
        for to, first in ((away, 1 - core[0]), (here, core[0])):
            for place, value in split(to, first, size):
                to[place, at] = value.astype(to.dtype)
    if len(refs) > 3:
        extra = refs[0]
        at = slice(width, width + extra.shape[1])
        total[:, : extra.shape[1]] = extra[...]
        for to, first in ((away, 1 - core[0]), (here, core[0])):
            for place, value in split(to, first, extra.shape[1]):
                to[place, at] = value.astype(to.dtype)


def product(core, left, right, *extra, cost=1000):
    width = right.shape[1] + sum(block.shape[1] for block in extra)
    out = jax.ShapeDtypeStruct((left.shape[1] // 2, width), jnp.bfloat16)
    whole = pl.BlockSpec(memory_space=pltpu.VMEM)
    away, here = pl.pallas_call(
        product_body,
        in_specs=[pl.BlockSpec(memory_space=pltpu.SMEM)] + [whole] * (2 + len(extra)),
        out_specs=[whole, whole],
        out_shape=[out, out],
        scratch_shapes=[pltpu.VMEM((left.shape[1], 512), jnp.float32)],
        compiler_params=pltpu.CompilerParams(vmem_limit_bytes=VMEM),
        cost_estimate=pl.CostEstimate(flops=cost, bytes_accessed=1000, transcendentals=0),
        name="product",
    )(core, left, right, *extra)
    return here, give(away, "core", 1)


def spread_in_body(gate, gate_got, up, up_got, down, down_got, spread):
    rows = spread.shape[1]
    half = FEED_SLICE // 2
    gates, ups, downs = (
        here[...].astype(jnp.float32) + got[...].astype(jnp.float32)
        for here, got in ((gate, gate_got), (up, up_got), (down, down_got))
    )
    for block in range(2):
        of = slice(block * rows, (block + 1) * rows)
        to = 2 * block
        spread[to, :, :FEED_SLICE] = gates[of].astype(spread.dtype)
        spread[to, :, FEED_SLICE:] = downs[of, :half].astype(spread.dtype)
        spread[to + 1, :, :FEED_SLICE] = ups[of].astype(spread.dtype)
        spread[to + 1, :, FEED_SLICE:] = downs[of, half:].astype(spread.dtype)


def spread_out_body(sums, gate, up, down):
    width = gate.shape[1]
    half = FEED_SLICE // 2
    for y in range(4):
        start = y * FEED_SLICE
        size = min(FEED_SLICE, width - start)
        gate[:, start : start + size] = sums[y, :, :size].astype(jnp.float32)
        up[:, start : start + size] = sums[4 + y, :, :size].astype(jnp.float32)
        for xl in range(2):
            first = start + xl * half
            size = min(half, width - first)
            down[:, first : first + size] = sums[
                4 * xl + y, :, FEED_SLICE : FEED_SLICE + size
            ].astype(jnp.float32)


def feed_slice(weight):
    y = lax.axis_index("y")
    missing = 4 * FEED_SLICE - weight.shape[1]
    start = jnp.minimum(y * FEED_SLICE, weight.shape[1] - FEED_SLICE)
    block = lax.dynamic_slice_in_dim(weight, start, FEED_SLICE, 1)
    moved = jnp.pad(block[:, missing:], ((0, 0), (0, missing)))
    return jnp.where(y == 3, moved, block)


def local(
    tokens,
    cotangent,
    lengths,
    query_weight,
    key_weight,
    value_weight,
    out_weight,
    gate_weight,
    up_weight,
    down_weight,
    input_gain,
    query_gain,
    key_gain,
    attention_gain,
    feedforward_gain,
    output_gain,
):
    low = jnp.bfloat16
    wide = jnp.float32
    row_count, model_width = tokens.shape
    head_size = key_weight.shape[1]
    head_count = query_weight.shape[1] // head_size
    query_width = head_count * head_size
    qkv_width = query_width + 2 * head_size
    feed_width = gate_weight.shape[1]
    gain_shard = input_gain.shape[0]
    head_shard = query_gain.shape[0]
    y = lax.axis_index("y")
    seq_index = lax.axis_index("xl") * 4 + y
    place = seq_index.reshape(1).astype(jnp.int32)
    core = lax.axis_index("core").reshape(1).astype(jnp.int32)
    positions = seq_index * row_count + lax.iota(jnp.int32, row_count)
    valid = jnp.broadcast_to((positions < lengths[0]).astype(wide)[:, None], (row_count, 128))
    cosine, sine = rotary_tables(positions, head_size)

    def spread(vector):
        return jnp.pad(vector, (0, gain_shard - head_shard))

    gain_columns = jnp.stack(
        [
            input_gain,
            attention_gain,
            feedforward_gain,
            output_gain,
            spread(query_gain),
            spread(key_gain),
        ],
        axis=1,
    )
    gain_columns = jnp.pad(gain_columns, ((0, 0), (0, 122)))
    feed_weights = lax.all_gather(
        jnp.concatenate(
            [feed_slice(gate_weight), feed_slice(up_weight), feed_slice(down_weight)], axis=1
        ),
        DP,
        axis=0,
        tiled=True,
    )
    attention_weights = jnp.concatenate(
        [query_weight, key_weight, value_weight, gain_columns, out_weight], axis=1
    )
    beside = swap_x(attention_weights)
    qkv_columns = qkv_width + gain_columns.shape[1]
    tokens_ring = [take(ordered(tokens, beside), "y", by) for by in (1, 2, 3)]
    full_qkv, arrived = gather_rows(
        with_other_x(attention_weights[:, :qkv_columns], beside[:, :qkv_columns]), tokens_ring
    )
    gains = 1.0 + full_qkv[:, qkv_width : qkv_width + 8].astype(wide).T
    one_input, one_attention, one_feed, one_output = (gains[i : i + 1] for i in range(4))
    head_gain = gains.reshape(8, 16, gain_shard)[4:6, :, :head_shard].reshape(2, head_size)
    head_gain = jnp.pad(head_gain, ((0, 6), (0, 0)))

    def attention_input_of(rows):
        values = rows.astype(wide)
        return (values * inverse_rms(values) * one_input).astype(low)

    attention_input = attention_input_of(tokens)
    qkv_raw = jnp.dot(attention_input, full_qkv[:, :qkv_width], preferred_element_type=wide)
    prepare = rows_call(
        prepare_body,
        [((row_count, query_width), low), ((row_count, 2 * head_size), low)],
        "prepare",
    )
    query_low, local_pair = prepare(qkv_raw, head_gain, cosine, sine)
    near_pair, far_pair = (from_behind(local_pair, distance) for distance in (1, 2))
    input_ring = attention_input_of(
        jnp.concatenate([ordered(tokens, local_pair)] + tokens_ring, axis=0)
    )
    out_pair = with_other_x(out_weight, beside[:, qkv_columns:])
    full_out, _ = gather_rows(ordered(out_pair, *arrived), (input_ring,))
    near_pair, far_pair, input_ring = lax.optimization_barrier((near_pair, far_pair, input_ring))
    attend = rows_call(
        attend_body,
        [((row_count, query_width), low), ((8, row_count), wide)],
        "attend",
        12 * 10**9,
    )
    context_low, log_total = attend(place, query_low, far_pair, near_pair, local_pair)
    residual = rows_call(
        residual_body,
        [
            ((row_count, model_width), wide),
            ((row_count, model_width), wide),
            ((row_count, model_width), low),
        ],
        "residual",
    )
    attention_raw, state, feed_input = residual(
        context_low, full_out, tokens, one_attention, one_feed
    )

    weights, feed_input = lax.optimization_barrier((feed_weights, feed_input))

    def touch(array):
        def body(whole, some):
            some[...] = whole[:16, :128]

        return pl.pallas_call(
            body,
            in_specs=[pl.BlockSpec(memory_space=pltpu.VMEM)],
            out_specs=pl.BlockSpec(memory_space=pltpu.VMEM),
            out_shape=jax.ShapeDtypeStruct((16, 128), array.dtype),
            compiler_params=pltpu.CompilerParams(vmem_limit_bytes=VMEM),
            cost_estimate=pl.CostEstimate(flops=LONG, bytes_accessed=1000, transcendentals=0),
            name="touch",
        )(array)

    def exchange(rows, run):
        two, one, three = (take(rows, "y", by) for by in (2, 1, 3))
        two, touched = lax.optimization_barrier((two, touch(weights)))
        kept, two_part = run(two, [], 3 * row_count, 1000, [touched])
        across = give(two_part, "y", 2)
        both = jnp.concatenate([one, three], axis=0)
        kept, both_part = run(both, kept, 0, LONG)
        from_one = give(both_part[:row_count], "y", 1)
        from_three = give(both_part[row_count:], "y", 3)
        *kept, across, both = lax.optimization_barrier((*kept, across, both))
        kept, own_part = run(rows, kept, 2 * row_count, LONG)
        ring = jnp.concatenate([ordered(both, own_part, from_one, from_three), rows, two], axis=0)
        return kept, [own_part, from_one, across, from_three], ring

    def forward(rows, kept, at, cost, unread=()):
        *kept, part = feed_call(feed_body, rows, weights, [], kept, at, 3, cost, "feed", unread)
        return kept, part

    kept, terms, feed_ring = exchange(feed_input, forward)
    hidden, value, slope = kept
    finish = blocks_call(
        down_body,
        [
            ((row_count, model_width), low),
            ((row_count, model_width), low),
            ((8, model_width), wide),
        ],
        "finish",
    )
    layer_output, down_grad, output_gain_rows = finish(
        *terms, state, cotangent, valid, one_output
    )

    def backward(rows, kept, at, cost):
        *kept, part = feed_call(
            feed_back_body, rows, weights, [value, slope], kept, at, 2, cost, "feed_back"
        )
        return kept, part

    rows72 = gain_shard
    two, one, three = (take(down_grad, "y", by) for by in (2, 1, 3))
    kept, own_part = backward(down_grad, [], 2 * row_count, 1000)
    kept, two_part = backward(two, kept, 3 * row_count, 1000)
    across = give(two_part, "y", 2)
    both = jnp.concatenate([one, three], axis=0)
    (gate_grad, up_grad), both_part = backward(both, kept, 0, LONG)
    from_one = give(both_part[:row_count], "y", 1)
    from_three = give(both_part[row_count:], "y", 3)
    across, both, gate_grad, up_grad = lax.optimization_barrier((across, both, gate_grad, up_grad))
    down_ring = jnp.concatenate([both, down_grad, two], axis=0)
    down_halves = product(core, down_ring, hidden)
    terms = [own_part, from_one, across, from_three]
    gate_halves = product(core, ordered(feed_ring, down_halves[0]), gate_grad)
    up_halves = product(
        core,
        ordered(feed_ring, gate_halves[0], down_halves[1]),
        up_grad,
    )
    halves = [*gate_halves, *up_halves, *down_halves]
    spread_shape = (16, rows72, FEED_SLICE * 3 // 2)
    spread_in = pl.pallas_call(
        spread_in_body,
        grid=(4,),
        in_specs=[pl.BlockSpec((2 * rows72, FEED_SLICE), lambda i: (i, 0))] * 6,
        out_specs=pl.BlockSpec((4, *spread_shape[1:]), lambda i: (i, 0, 0)),
        out_shape=jax.ShapeDtypeStruct(spread_shape, low),
        compiler_params=pltpu.CompilerParams(vmem_limit_bytes=VMEM),
        cost_estimate=SMALL,
        name="spread_in",
    )(*halves)
    feed_sum = lax.psum_scatter(spread_in, ("z", "xh", "xl"), scatter_dimension=0, tiled=False)
    back = blocks_call(
        state_body,
        [
            ((row_count, model_width), low),
            ((row_count, model_width), wide),
            ((16, model_width), wide),
        ],
        "state_back",
        VMEM,
        36000000000,
    )
    attention_grad, state_grad, state_gain_rows = back(
        *terms, state, attention_raw, cotangent, valid, one_feed, one_attention
    )

    def whole(shape):
        return pl.BlockSpec(shape, lambda i: (0,) * len(shape))

    def head_columns(rows):
        return pl.BlockSpec((rows, head_size), lambda i: (0, i))

    smem = pl.BlockSpec(memory_space=pltpu.SMEM)
    pair_block = whole((row_count, 2 * head_size))
    table = whole((row_count, head_size // 2))
    attend_back = pl.pallas_call(
        attend_back_body,
        grid=(head_count,),
        in_specs=[
            smem,
            whole((row_count, model_width)),
            head_columns(model_width),
            head_columns(row_count),
            pair_block,
            pair_block,
            pair_block,
            whole((8, row_count)),
            head_columns(row_count),
            whole((8, head_size)),
            table,
            table,
        ],
        out_specs=[
            pair_block,
            pair_block,
            pair_block,
            head_columns(row_count),
            whole((8, head_size)),
        ],
        out_shape=[
            jax.ShapeDtypeStruct((row_count, 2 * head_size), low),
            jax.ShapeDtypeStruct((row_count, 2 * head_size), low),
            jax.ShapeDtypeStruct((row_count, 2 * head_size), wide),
            jax.ShapeDtypeStruct((row_count, query_width), low),
            jax.ShapeDtypeStruct((8, head_size), wide),
        ],
        scratch_shapes=[pltpu.VMEM((3, row_count, head_size), wide)] * 2,
        compiler_params=pltpu.CompilerParams(vmem_limit_bytes=MOST),
        cost_estimate=pl.CostEstimate(flops=100 * 10**9, bytes_accessed=1000, transcendentals=0),
        name="attend_back",
    )
    far_grad, near_grad, own_grad, query_grad, query_gain_rows = attend_back(
        place,
        attention_grad,
        full_out,
        query_low,
        far_pair,
        near_pair,
        local_pair,
        log_total,
        qkv_raw,
        head_gain,
        cosine,
        sine,
    )
    near_back = from_behind(near_grad, -1)
    far_back = from_behind(far_grad, -2)
    out_halves = product(core, ordered(attention_grad, near_grad), context_low, cost=LONG)
    out_block = whole((model_width // 2, query_width))
    cut_shape = (4, row_count + 384, qkv_width // 4)
    pair_back = pl.pallas_call(
        pair_back_body,
        grid=(1,),
        in_specs=[
            whole((row_count, query_width)),
            pair_block,
            pair_block,
            pair_block,
            pl.BlockSpec((row_count, head_size), lambda i: (0, head_count)),
            whole((8, head_size)),
            table,
            table,
            out_block,
            out_block,
        ],
        out_specs=[pair_block, whole(cut_shape), whole((8, head_size))],
        out_shape=[
            jax.ShapeDtypeStruct((row_count, 2 * head_size), low),
            jax.ShapeDtypeStruct(cut_shape, low),
            jax.ShapeDtypeStruct((8, head_size), wide),
        ],
        compiler_params=pltpu.CompilerParams(vmem_limit_bytes=MOST),
        cost_estimate=SMALL,
        name="pair_back",
    )
    pair_grad, qkv_cut, key_gain_rows = pair_back(
        query_grad, own_grad, near_back, far_back, qkv_raw, head_gain, cosine, sine, *out_halves
    )
    pieces = [give(pick(qkv_cut, (y + by) % 4, 0), "y", by) for by in (3, 2, 1)]
    qkv_ring, out_sum = rows_call(
        arrive_body,
        [((4 * row_count, qkv_width // 4), low), ((model_width // 2, query_width // 4), low)],
        "arrive",
    )(pick(qkv_cut, y, 0), *pieces)
    input_back = rows_call(
        input_body,
        [((row_count, model_width), low), ((8, model_width), wide)],
        "input_back",
    )
    tokens_grad, input_gain_rows = input_back(
        query_grad, pair_grad, full_qkv, tokens, state_grad, one_input
    )

    def spread_head(vector):
        return jnp.pad(
            vector.reshape(16, head_shard), ((0, 0), (0, gain_shard - head_shard))
        ).reshape(model_width)

    gain_block = jnp.stack(
        [
            input_gain_rows[0],
            state_gain_rows[8],
            state_gain_rows[0],
            output_gain_rows[0],
            spread_head(query_gain_rows[0]),
            spread_head(key_gain_rows[0]),
        ],
        axis=1,
    )
    gain_block = jnp.pad(gain_block, ((0, 0), (0, 122)))
    z = lax.axis_index("z")
    xh = lax.axis_index("xh")
    offsets = jnp.stack(
        [(((z + i) % 4) * 2 + (xh + j) % 2) * rows72 for i in range(4) for j in range(2)]
    ).astype(jnp.int32)
    columns = qkv_width // 4 + 128 + query_width // 4
    parts = pl.pallas_call(
        chip_body,
        in_specs=[pl.BlockSpec(memory_space=pltpu.SMEM)]
        + [pl.BlockSpec(memory_space=pltpu.VMEM)] * 3,
        out_specs=[pl.BlockSpec(memory_space=pltpu.VMEM)] * 4,
        out_shape=[jax.ShapeDtypeStruct((2, rows72, columns), low)] * 4,
        scratch_shapes=[pltpu.VMEM((model_width // 2, columns), wide)],
        compiler_params=pltpu.CompilerParams(vmem_limit_bytes=VMEM),
        cost_estimate=SMALL,
        name="chip",
    )(offsets, *product(core, input_ring, qkv_ring, gain_block), out_sum)
    total = parts[0].astype(wide)
    for by in (1, 3, 2):
        total = total + give(parts[by], "z", by).astype(wide)
    attention_column = total.astype(low)
    attention_half = (
        attention_column[0].astype(wide) + swap_x(attention_column[1]).astype(wide)
    ).astype(low)
    attention_sum = (
        attention_half.astype(wide) + give(attention_half, "xl", 1).astype(wide)
    ).astype(low)
    attention_blocks = in_order(
        [attention_sum] + [take(attention_sum, "y", by) for by in (1, 2, 3)]
    )
    feed_sums = lax.all_gather(ordered(feed_sum, parts[0]), SEQ, axis=0, tiled=False)
    gate_weight_grad, up_weight_grad, down_weight_grad = rows_call(
        spread_out_body, [((rows72, feed_width), wide)] * 3, "spread_out"
    )(feed_sums)
    qkv_cols = qkv_width // 4
    out_cols = query_width // 4
    qkv_weight_grad = jnp.concatenate([b[:, :qkv_cols] for b in attention_blocks], axis=1)
    out_weight_grad = jnp.concatenate([b[:, qkv_cols + 128 :] for b in attention_blocks], axis=1)
    gain_sum = sum(b[:, qkv_cols : qkv_cols + 128].astype(wide) for b in attention_blocks)
    return (
        layer_output,
        tokens_grad,
        qkv_weight_grad[:, :query_width].astype(wide),
        qkv_weight_grad[:, query_width : query_width + head_size].astype(wide),
        qkv_weight_grad[:, query_width + head_size :].astype(wide),
        out_weight_grad.astype(wide),
        gate_weight_grad,
        up_weight_grad,
        down_weight_grad,
        gain_sum[:, 0],
        gain_sum[:head_shard, 4],
        gain_sum[:head_shard, 5],
        gain_sum[:, 1],
        gain_sum[:, 2],
        gain_sum[:, 3],
    )


def solution(mesh):
    fine = Mesh(mesh.devices.reshape(SIZES), AXES)
    rows = P(AXES, None)
    matrix = P(DP, None)
    vector = P(DP)
    return jax.shard_map(
        local,
        mesh=fine,
        in_specs=(rows, rows, vector) + (matrix,) * 7 + (vector,) * 6,
        out_specs=(rows, rows) + (matrix,) * 7 + (vector,) * 6,
        check_vma=False,
    )
```
